32 devices in a mesh: dp: 8 (over y, x, core), tensor: 4 (over z).
Axes of the slice: x: 2, y: 2, z: 4, core: 2. Of those that a mesh axis runs over, the one named last changes fastest.
Arguments:
- tokens: bfloat16 [32, 320, 1024], P('dp'), may hold values from -6 to 6
- lengths: int32 [32], P('dp'), may hold values from 65 to 320, as said below
- adapter_ids: int32 [32, 4], P('dp'), may hold values from 0 to 7
- qkv_weight: bfloat16 [1024, 3, 1024], P(None, None, 'tensor'), may hold values from -0.1875 to 0.1875
- qkv_down: bfloat16 [8, 1024, 16], replicated, may hold values from -0.1875 to 0.1875
- qkv_up: bfloat16 [8, 16, 3, 1024], P(None, None, None, 'tensor'), may hold values from -0.75 to 0.75
- out_weight: bfloat16 [1024, 1024], P('tensor'), may hold values from -1 to 1
- out_down: bfloat16 [8, 1024, 16], P(None, 'tensor'), may hold values from -1 to 1
- out_up: bfloat16 [8, 16, 1024], replicated, may hold values from -0.75 to 0.75
- fc1_weight: bfloat16 [1024, 4096], P(None, 'tensor'), may hold values from -0.1875 to 0.1875
- fc1_down: bfloat16 [8, 1024, 16], replicated, may hold values from -0.1875 to 0.1875
- fc1_up: bfloat16 [8, 16, 4096], P(None, None, 'tensor'), may hold values from -0.75 to 0.75
- fc2_weight: bfloat16 [4096, 1024], P('tensor'), may hold values from -0.09375 to 0.09375
- fc2_down: bfloat16 [8, 4096, 16], P(None, 'tensor'), may hold values from -0.09375 to 0.09375
- fc2_up: bfloat16 [8, 16, 1024], replicated, may hold values from -0.75 to 0.75
- cotangent: bfloat16 [32, 320, 1024], P('dp', None, 'tensor'), may hold values from -6 to 6
Outputs:
- output: float32 [32, 320, 1024], P('dp', None, 'tensor')
- input_grad: float32 [32, 320, 1024], P('dp', None, 'tensor')
- grad_qkv_down: float32 [8, 1024, 16], replicated
- grad_qkv_up: float32 [8, 16, 3, 1024], P(None, None, None, 'tensor')
- grad_out_down: float32 [8, 1024, 16], P(None, 'tensor')
- grad_out_up: float32 [8, 16, 1024], replicated
- grad_fc1_down: float32 [8, 1024, 16], replicated
- grad_fc1_up: float32 [8, 16, 4096], P(None, None, 'tensor')
- grad_fc2_down: float32 [8, 4096, 16], P(None, 'tensor')
- grad_fc2_up: float32 [8, 16, 1024], replicated
The draws below stay inside these ranges and needn't reach their ends.
Inputs may be any that keep to these rules, and one draw needn't show every extreme that they name: `lengths`: each image's valid slots are its 64 buffer tokens and a prefix of its other slots; some image fills all 320 slots and some image has only one slot beyond its buffer. `adapter_ids`: columns name the adapter for the qkv, output, fc1 and fc2 projections, in that order.
All inputs are finite; a program needn't handle non-finite values.
Results may differ from the reference program's by a relative error of at most 0.015.
Values may be sent and summed in bfloat16 or wider, within the bound.
A program may use at most 192 MiB of HBM per device.

```python
import jax
import jax.numpy as jnp
from jax import lax

D = 1024
HEADS = 16
HD = 64
FF = 4096
RANK = 16
ADAPT = 8
LEN = 320
BUF = 64
SEQS = 32
N_DP = 8


def draw_lengths(key, part):
    key = jax.random.fold_in(key, 11)
    first_key, second_key, third_key = jax.random.split(key, 3)
    values = jax.random.randint(first_key, (SEQS,), BUF + 1, LEN + 1)
    longest = jax.random.randint(second_key, (), 0, SEQS)
    offset = jax.random.randint(third_key, (), 1, SEQS)
    shortest = (longest + offset) % SEQS
    values = values.at[longest].set(LEN)
    values = values.at[shortest].set(BUF + 1)
    return values.astype(jnp.int32)


def with_ends(drawn, own_key, least, top_value):
    longest = drawn.shape.index(max(drawn.shape))
    spots = []
    for shift in (0, 1):
        where = [jax.random.randint(jax.random.fold_in(own_key, axis), (), 0, length) for axis, length in enumerate(drawn.shape)]
        where[longest] = (where[longest] + shift) % drawn.shape[longest]
        spots.append(tuple(where))
    return drawn.at[spots[0]].set(least).at[spots[1]].set(top_value)


def steps_of(rng, extent, pieces, low, high):
    factor_of, own = 1.0, jax.random.fold_in(rng, 6)
    for position, parts in pieces:
        steps = jnp.exp(jax.random.uniform(jax.random.fold_in(own, position), (parts,), jnp.float32, low / len(pieces), high / len(pieces)))
        factor_of = factor_of * jnp.repeat(steps, extent[position] // parts).reshape([-1 if axis == position else 1 for axis in range(len(extent))])
    return factor_of


def noise(rng, dims, spread, reach, cuts=(), kind=jnp.bfloat16):
    drawn = jax.random.normal(rng, dims, jnp.float32) * spread
    if len(cuts) > 0:
        drawn = steps_of(rng, dims, cuts, -0.22, 0.18) * drawn
    return jnp.clip(drawn, min=-reach, max=reach).astype(kind)


def setup_inputs(seed: int = 0) -> dict:
    key_of = jax.random.split(jax.random.key(seed), 17)
    tokens = noise(key_of[0], (SEQS, LEN, D), 1.0, 6.0, ((0, 8),))
    lengths = draw_lengths(jax.random.fold_in(key_of[16], 71), 0)
    adapter_ids = with_ends(jax.random.randint(key_of[2], (SEQS, 4), 0, ADAPT), jax.random.fold_in(key_of[2], 1), 0, ADAPT - 1).astype(jnp.int32)
    qkv_weight = noise(key_of[3], (D, 3, D), D ** -0.5, 0.1875, ((2, 4),))
    qkv_down = noise(key_of[4], (ADAPT, D, RANK), D ** -0.5, 0.1875)
    qkv_up = noise(key_of[5], (ADAPT, RANK, 3, D), (4 * RANK) ** -0.5, 0.75, ((3, 4),))
    out_weight = noise(key_of[6], (D, D), (D // 32) ** -0.5, 1.0, ((0, 4),))
    out_down = noise(key_of[7], (ADAPT, D, RANK), (D // 32) ** -0.5, 1.0, ((1, 4),))
    out_up = noise(key_of[8], (ADAPT, RANK, D), (4 * RANK) ** -0.5, 0.75)
    fc1_weight = noise(key_of[9], (D, FF), D ** -0.5, 0.1875, ((1, 4),))
    fc1_down = noise(key_of[10], (ADAPT, D, RANK), D ** -0.5, 0.1875)
    fc1_up = noise(key_of[11], (ADAPT, RANK, FF), (4 * RANK) ** -0.5, 0.75, ((2, 4),))
    fc2_weight = noise(key_of[12], (FF, D), FF ** -0.5, 0.09375, ((0, 4),))
    fc2_down = noise(key_of[13], (ADAPT, FF, RANK), FF ** -0.5, 0.09375, ((1, 4),))
    fc2_up = noise(key_of[14], (ADAPT, RANK, D), (4 * RANK) ** -0.5, 0.75)
    cotangent = noise(key_of[15], (SEQS, LEN, D), 1.0, 6.0, ((0, 8), (2, 4)))
    return dict(tokens=tokens, lengths=lengths, adapter_ids=adapter_ids, qkv_weight=qkv_weight, qkv_down=qkv_down, qkv_up=qkv_up, out_weight=out_weight, out_down=out_down, out_up=out_up, fc1_weight=fc1_weight, fc1_down=fc1_down, fc1_up=fc1_up, fc2_weight=fc2_weight, fc2_down=fc2_down, fc2_up=fc2_up, cotangent=cotangent)


EPSILON = 1e-06
NEG_FILL = -1e+30

@jax.custom_vjp
def low(v):
    return lax.optimization_barrier(v.astype(jnp.bfloat16)).astype(jnp.float32)

@jax.custom_vjp
def low_back(v):
    return v

def low_keep(v):
    return (low(v), None)

def low_pass(kept, grad):
    return (grad,)

def back_keep(v):
    return (v, None)

def back_low(kept, grad):
    return (low(grad),)
low.defvjp(low_keep, low_pass)
low_back.defvjp(back_keep, back_low)

def norm_rows(values):
    centred = values - lax.optimization_barrier(jnp.mean(values, axis=-1, keepdims=True))
    return centred * lax.rsqrt(lax.optimization_barrier(jnp.mean(centred * centred, axis=-1, keepdims=True)) + EPSILON)

def dense(left, right):
    return jnp.matmul(left, right, precision=lax.Precision.HIGHEST)

def flat_down(down):
    return jnp.transpose(down, (1, 0, 2)).reshape(down.shape[1], down.shape[0] * down.shape[2])

def adapter_masks(adapter_ids):
    owners = jnp.arange(ADAPT * RANK, dtype=jnp.int32) // RANK
    return [(adapter_ids[:, column][:, None] == owners[None, :]).astype(jnp.float32)[:, None, :] for column in range(4)]

def layer(inputs, adapters, frozen, selectors, keep_mask):
    qkv_down, qkv_up, out_down, out_up, fc1_down, fc1_up, fc2_down, fc2_up = adapters
    qkv_weight, out_weight, fc1_weight, fc2_weight = frozen
    seq_count = inputs.shape[0]
    total_rank = ADAPT * RANK
    first_in = low(norm_rows(inputs))
    lift_qkv = low_back(low(selectors[0] * dense(first_in, flat_down(qkv_down))))
    projected = dense(first_in, qkv_weight.reshape(D, 3 * D)) + dense(lift_qkv, qkv_up.reshape(total_rank, 3 * D))
    projected = low_back(low(projected)).reshape(seq_count, LEN, 3, HEADS, HD)
    scores = jnp.einsum('slhd,smhd->shlm', projected[:, :, 0], projected[:, :, 1], precision=lax.Precision.HIGHEST)
    scores = low_back(scores * HD ** (-0.5))
    masked = jnp.where(keep_mask[:, None, None, :], scores, NEG_FILL)
    shifted = jnp.exp(masked - lax.optimization_barrier(jnp.max(masked, axis=-1, keepdims=True)))
    soft_weights = shifted / lax.optimization_barrier(jnp.sum(shifted, axis=-1, keepdims=True))
    heads_mixed = jnp.einsum('shlm,smhd->slhd', low(soft_weights), projected[:, :, 2], precision=lax.Precision.HIGHEST)
    attended = low_back(low(heads_mixed)).reshape(seq_count, LEN, D)
    lift_out = low_back(low(selectors[1] * dense(attended, flat_down(out_down))))
    branch = low_back(dense(attended, out_weight) + dense(lift_out, out_up.reshape(total_rank, D)))
    mixed_rows = inputs + branch
    second_in = low(norm_rows(mixed_rows))
    lift_fc1 = low_back(low(selectors[2] * dense(second_in, flat_down(fc1_down))))
    before = low_back(dense(second_in, fc1_weight) + dense(lift_fc1, fc1_up.reshape(total_rank, FF)))
    hidden = low(jax.nn.gelu(before, approximate=False))
    lift_fc2 = low_back(low(selectors[3] * dense(hidden, flat_down(fc2_down))))
    result = mixed_rows + dense(hidden, fc2_weight) + dense(lift_fc2, fc2_up.reshape(total_rank, D))
    return keep_mask[:, :, None].astype(jnp.float32) * result

def reference(tokens, lengths, adapter_ids, qkv_weight, qkv_down, qkv_up, out_weight, out_down, out_up, fc1_weight, fc1_down, fc1_up, fc2_weight, fc2_down, fc2_up, cotangent):
    frozen = (qkv_weight.astype(jnp.float32), out_weight.astype(jnp.float32), fc1_weight.astype(jnp.float32), fc2_weight.astype(jnp.float32))
    adapters = (qkv_down.astype(jnp.float32), qkv_up.astype(jnp.float32), out_down.astype(jnp.float32), out_up.astype(jnp.float32), fc1_down.astype(jnp.float32), fc1_up.astype(jnp.float32), fc2_down.astype(jnp.float32), fc2_up.astype(jnp.float32))
    per_group = SEQS // N_DP
    batches = (tokens.astype(jnp.float32).reshape(N_DP, per_group, LEN, D), lengths.reshape(N_DP, per_group), adapter_ids.reshape(N_DP, per_group, 4), cotangent.astype(jnp.float32).reshape(N_DP, per_group, LEN, D))

    def group_step(running, group_batch):
        group_inputs, group_lengths, group_ids, group_cotangent = group_batch
        keep_mask = jnp.arange(LEN, dtype=jnp.int32)[None, :] < group_lengths[:, None]
        selectors = adapter_masks(group_ids)

        def forward(inputs_now, adapters_now):
            return layer(inputs_now, adapters_now, frozen, selectors, keep_mask)
        result, backward = jax.vjp(forward, group_inputs, adapters)
        grad_inputs, grad_adapters = backward(group_cotangent)
        running = tuple((total_now + gradient for total_now, gradient in zip(running, grad_adapters)))
        return (running, (result, grad_inputs))
    starting = tuple((jnp.zeros_like(weight) for weight in adapters))
    running, (results, grad_inputs) = lax.scan(group_step, starting, batches)
    return (results.reshape(SEQS, LEN, D), grad_inputs.reshape(SEQS, LEN, D), running[0], running[1], running[2], running[3], running[4], running[5], running[6], running[7])
```

```python
import jax
import jax.numpy as jnp
from jax import lax
from jax.experimental import pallas as pl
from jax.experimental.pallas import tpu as pltpu
from jax.sharding import PartitionSpec as P


BF = jnp.bfloat16
F32 = jnp.float32
MESH = pl.DeviceIdType.MESH
EPSILON = 1e-6
NEG_FILL = -1e30
HD = 64
GROUP = 8
BLOCK = 32
STEP = 512
ORDER = ((0, 1, 2, 3), (1, 2, 0, 3), (2, 1, 3, 0), (3, 2, 1, 0))


def dot(a, b):
    return lax.dot_general(a, b, (((1,), (0,)), ((), ())), preferred_element_type=F32)


def dot_nt(a, b):
    return lax.dot_general(a, b, (((1,), (1,)), ((), ())), preferred_element_type=F32)


def dot_tn(a, b):
    return lax.dot_general(a, b, (((0,), (0,)), ((), ())), preferred_element_type=F32)


def rows_loop(count, body, block=BLOCK):
    @pl.loop(0, count // block)
    def _(i):
        body(pl.ds(pl.multiple_of(i * block, block), block))


def moments(values):
    centred = values - jnp.mean(values, axis=-1, keepdims=True)
    inverse = lax.rsqrt(jnp.mean(centred * centred, axis=-1, keepdims=True) + EPSILON)
    return centred, inverse


def norm_back(values, grad):
    centred, inverse = moments(values)
    hat = centred * inverse
    return inverse * (
        grad - jnp.mean(grad, axis=-1, keepdims=True) - hat * jnp.mean(grad * hat, axis=-1, keepdims=True)
    )


def pick(position, table):
    out = 0
    for k, v in enumerate(table):
        if v:
            out = out + jnp.where(position == k, v, 0)
    return out


class Bag:
    pass


def prep(r):
    def body(rows):
        centred, inverse = moments(r.x[rows, :].astype(F32))
        r.first[rows, :] = (centred * inverse).astype(BF)

    rows_loop(r.S, body)


def prep_dz(r):
    def body(rows):
        keep = (lax.broadcasted_iota(jnp.int32, (BLOCK, 1), 0) + rows.start) < r.length
        for j in range(4):
            v = r.dzq[j, rows, :]
            r.dz[rows, r.W * j : r.W * (j + 1)] = jnp.where(keep, v, jnp.zeros_like(v))

    rows_loop(r.S, body)
    r.g_fc2[...] = dot_nt(r.dz[...], r.up_fc2[...]).astype(BF)


def attn_fwd(r, q, init):
    S, W = r.S, r.W
    for i in range(3):
        p = dot(r.first[...], r.wq[q, i]) + dot(r.lift_qkv[...], r.sel[q, :, i * W : (i + 1) * W])
        r.proj[q, i] = p.astype(BF)
    valid = lax.broadcasted_iota(jnp.int32, (S, S), 0) < r.length
    lane = lax.broadcasted_iota(jnp.int32, (S, 128), 1)

    @pl.loop(0, W // 128)
    def _(pair):
        cols = pl.ds(pl.multiple_of(pair * 128, 128), 128)
        qp = r.proj[q, 0, :, cols]
        kp = r.proj[q, 1, :, cols]
        vp = r.proj[q, 2, :, cols]
        res = []
        for h in range(2):
            qm = jnp.where((lane // HD) == h, qp, jnp.zeros_like(qp))
            st = jnp.where(valid, dot_nt(kp, qm) * (HD**-0.5), NEG_FILL)
            e = jnp.exp(st - jnp.max(st, axis=0, keepdims=True))
            soft = e * (1.0 / jnp.sum(e, axis=0, keepdims=True))
            r.soft[q * (W // HD) + pair * 2 + h] = soft
            res.append(dot_tn(soft.astype(BF), vp))
        r.att[q, :, cols] = jnp.where((lane // HD) == 0, res[0], res[1]).astype(BF)

    a = r.att[q]
    t = dot(a, r.wo[q])
    l = dot_nt(a, r.sel[q, :, 3 * W : 4 * W])
    if init:
        r.branch[...] = t
        r.lift_out_acc[...] = l
    else:
        r.branch[...] += t
        r.lift_out_acc[...] += l


def after_attn(r):
    r.lift_out[...] = r.lift_out_acc[...].astype(BF)
    r.branch[...] += dot(r.lift_out[...], r.up_out[...])

    def body(rows):
        mixed = r.x[rows, :].astype(F32) + r.branch[rows, :]
        r.mixed[rows, :] = mixed
        centred, inverse = moments(mixed)
        r.second[rows, :] = (centred * inverse).astype(BF)

    rows_loop(r.S, body)
    r.lift_fc1[...] = dot_nt(r.second[...], r.dn_fc1[...]).astype(BF)
    r.outacc[...] = jnp.zeros_like(r.outacc)
    r.gsec[...] = jnp.zeros_like(r.gsec)
    r.lift_fc2_acc[...] = jnp.zeros_like(r.lift_fc2_acc)
    r.glf1_acc[...] = jnp.zeros_like(r.glf1_acc)


def ffn_unit(r, q, u):
    W, FQ = r.W, r.FQ
    cols = pl.ds(u * STEP, STEP)
    up1 = r.sel[q, :, 4 * W + u * STEP : 4 * W + (u + 1) * STEP]
    dn2 = r.sel[q, :, 4 * W + FQ + u * STEP : 4 * W + FQ + (u + 1) * STEP]
    r.before[...] = dot(r.second[...], r.w1[q, :, cols]) + dot(r.lift_fc1[...], up1)
    r.gh[...] = dot_nt(r.dz[...], r.w2[q, cols, :]) + dot(r.g_fc2[...], dn2)

    def body(rows):
        b = r.before[rows, :]
        cdf = 0.5 * (1.0 + lax.erf(b * (0.5**0.5)))
        r.hidden[rows, :] = (b * cdf).astype(BF)
        slope = cdf + b * jnp.exp(-0.5 * b * b) * 0.3989422804014327
        r.gb[rows, :] = (slope * r.gh[rows, :]).astype(BF)

    rows_loop(r.S, body)
    h = r.hidden[...]
    g = r.gb[...]
    r.outacc[...] += dot(h, r.w2[q, cols, :])
    r.gsec[...] += dot_nt(g, r.w1[q, :, cols])
    r.lift_fc2_acc[...] += dot_nt(h, dn2)
    r.glf1_acc[...] += dot_nt(g, up1)
    r.gall[q, :, u * STEP : (u + 1) * STEP] = dot_tn(r.lift_fc1[...], g).astype(BF)
    r.gall[q, :, FQ + u * STEP : FQ + (u + 1) * STEP] = dot_tn(r.g_fc2[...], h).astype(BF)


def after_ffn_out(r):
    r.lift_fc2[...] = r.lift_fc2_acc[...].astype(BF)
    r.outacc[...] += dot(r.lift_fc2[...], r.up_fc2[...])

    def body(rows):
        keep = (lax.broadcasted_iota(jnp.int32, (BLOCK, 1), 0) + rows.start) < r.length
        r.out[rows, :] = jnp.where(keep, r.mixed[rows, :] + r.outacc[rows, :], 0.0).astype(BF)

    rows_loop(r.S, body)


def put_rep(r, value, base):
    v = value.astype(BF)
    for j in range(4):
        r.gall[j, :, base : base + r.W] = v[:, r.W * j : r.W * (j + 1)]


def after_ffn_back(r):
    g1 = r.glf1_acc[...].astype(BF)
    put_rep(r, dot_tn(r.lift_fc2[...], r.dz[...]), 2 * r.FQ + r.W)
    put_rep(r, dot_tn(g1, r.second[...]), 2 * r.FQ)
    r.gsec[...] += dot(g1, r.dn_fc1[...])

    def body(rows):
        g = r.dz[rows, :].astype(F32) + norm_back(r.mixed[rows, :], r.gsec[rows, :])
        r.mixed[rows, :] = g
        r.gbr[rows, :] = g.astype(BF)

    rows_loop(r.S, body)
    gbr = r.gbr[...]
    put_rep(r, dot_tn(r.lift_out[...], gbr), 2 * r.FQ + 2 * r.W)
    r.g_out[...] = dot_nt(gbr, r.up_out[...]).astype(BF)
    r.glq_acc[...] = jnp.zeros_like(r.glq_acc)
    r.gsec[...] = jnp.zeros_like(r.gsec)


def attn_back(r, q):
    S, W = r.S, r.W
    od = r.sel[q, :, 3 * W : 4 * W]
    late = r.early
    r.gall[q, :, late + 3 * W : late + 4 * W] = dot_tn(r.g_out[...], r.att[q]).astype(BF)
    r.ga[...] = (dot_nt(r.gbr[...], r.wo[q]) + dot(r.g_out[...], od)).astype(BF)
    lane = lax.broadcasted_iota(jnp.int32, (S, 128), 1)

    @pl.loop(0, W // 128)
    def _(pair):
        cols = pl.ds(pl.multiple_of(pair * 128, 128), 128)
        qp = r.proj[q, 0, :, cols]
        kp = r.proj[q, 1, :, cols]
        vp = r.proj[q, 2, :, cols]
        gp = r.ga[:, cols]
        gv, gq, gk = [], [], []
        for h in range(2):
            mine = (lane // HD) == h
            gm = jnp.where(mine, gp, jnp.zeros_like(gp))
            qm = jnp.where(mine, qp, jnp.zeros_like(qp))
            soft = r.soft[q * (W // HD) + pair * 2 + h]
            gv.append(dot(soft.astype(BF), gm))
            gs = dot_nt(vp, gm)
            ds = (soft * (gs - jnp.sum(soft * gs, axis=0, keepdims=True))).astype(BF)
            gk.append(dot(ds, qm))
            gq.append(dot_tn(ds, kp))
        sc = HD**-0.5
        r.gp[0, :, cols] = (jnp.where((lane // HD) == 0, gq[0], gq[1]) * sc).astype(BF)
        r.gp[1, :, cols] = ((gk[0] + gk[1]) * sc).astype(BF)
        r.gp[2, :, cols] = (gv[0] + gv[1]).astype(BF)

    for i in range(3):
        g = r.gp[i]
        r.gall[q, :, late + i * W : late + (i + 1) * W] = dot_tn(r.lift_qkv[...], g).astype(BF)
        r.glq_acc[...] += dot_nt(g, r.sel[q, :, i * W : (i + 1) * W])
        r.gsec[...] += dot_nt(g, r.wq[q, i])


def finish_grads(r):
    gq = r.glq_acc[...].astype(BF)
    put_rep(r, dot_tn(gq, r.first[...]), r.early + 4 * r.W)
    r.gsec[...] += dot(gq, r.dn_qkv[...])


def finish_rows(r):
    def body(rows):
        r.gin[rows, :] = (r.mixed[rows, :] + norm_back(r.x[rows, :].astype(F32), r.gsec[rows, :])).astype(BF)

    rows_loop(r.S, body)


class Stream:
    def __init__(self, r):
        self.r = r
        d = self.d = lax.axis_index("dp")
        self.z = lax.axis_index("tensor")
        m = self.m = d % GROUP
        self.base = d - m
        self.dx = d + 2 - 4 * ((m // 2) % 2)
        self.dy = d + 4 - 8 * (m // 4)
        self.ds = d + 1 - 2 * (m % 2)
        self.dd = self.dx + self.dy - d
        self.q = [pick(self.z, [ORDER[k][i] for k in range(4)]) for i in range(4)]
        self.units = [("A", p, i) for i in (1, 2, 3) for p in range(2)]
        self.units += [("B", p, i) for i in (1, 2, 3) for p in range(4)]

    def greet(self):
        bar = pltpu.get_barrier_semaphore()
        for k in range(1, GROUP):
            peer = self.base + (self.m + k) % GROUP
            pl.semaphore_signal(bar, inc=1, device_id=(peer, self.z), device_id_type=MESH)
        for k in range(1, 4):
            pl.semaphore_signal(bar, inc=1, device_id=(self.d, (self.z + k) % 4), device_id_type=MESH)

    def met(self):
        pl.semaphore_wait(pltpu.get_barrier_semaphore(), GROUP + 2)

    def parts(self, kind, p, q, d, half=None):
        r, m = self.r, d - self.base
        if half is None:
            a, c = pl.ds(pl.multiple_of(m * 128, 128), 128), pl.ds(0, r.D)
        else:
            a, c = pl.ds(pl.multiple_of(m * 128 + 64 * half, 64), 64), pl.ds(r.D // 2 * half, r.D // 2)
        if kind == "A":
            b = pl.ds(pl.multiple_of(p * 128 + m * 16, 16), 16)
            return (r.wq.at[q, :, a, pl.ds(128 * p, 128)], r.wo.at[q, b, c])
        b = pl.ds(pl.multiple_of(p * 256 + m * 32, 32), 32)
        return (r.w1.at[q, a, pl.ds(256 * p, 256)], r.w2.at[q, b, c])

    def own(self, kind, p):
        r, m = self.r, self.m
        a = pl.ds(pl.multiple_of(m * 128, 128), 128)
        if kind == "A":
            return (r.hq.at[:, a, pl.ds(128 * p, 128)], r.ho.at[pl.ds(pl.multiple_of(p * 128 + m * 16, 16), 16), :])
        return (r.h1.at[a, pl.ds(256 * p, 256)], r.h2.at[pl.ds(pl.multiple_of(p * 256 + m * 32, 32), 32), :])

    def send(self, srcs, dsts, sem, dev):
        for s, t in zip(srcs, dsts):
            pltpu.make_async_remote_copy(
                src_ref=s, dst_ref=t, send_sem=self.r.sends, recv_sem=sem, device_id=dev, device_id_type=MESH
            ).start()

    def wait(self, rows, sem):
        v = self.r.w2.at[0, pl.ds(0, rows), :]
        pltpu.make_async_copy(v, v, sem).wait()

    def index(self, kind, p, i):
        return (i - 1) * 2 + p if kind == "A" else 6 + (i - 1) * 4 + p

    def own_sends(self, kind, p):
        z, d = self.z, self.d
        src = self.own(kind, p)
        dst = self.parts(kind, p, z, d)
        for step, last in ((1, 3), (-1, 0)):
            i = pick(z, [ORDER[k + step].index(k) if 0 <= k + step <= 3 else 0 for k in range(4)])

            @pl.when(z != last)
            def _():
                self.send(src, dst, self.r.rz.at[self.index(kind, p, i)], (d, z + step))

    def z_stage(self, t):
        kind, p, i = self.units[t]
        z, d, r = self.z, self.d, self.r
        self.wait(64, r.rz.at[t])
        piece = self.parts(kind, p, self.q[i], d)
        for step in (1, -1):
            go, slot = [], []
            for k in range(4):
                quarter = ORDER[k][i]
                on = 0 <= k + step <= 3 and (quarter < k if step == 1 else quarter > k)
                go.append(int(on))
                slot.append(ORDER[k + step].index(quarter) if on else 0)
            if any(go):

                @pl.when(pick(z, go) == 1)
                def _():
                    self.send(piece, piece, r.rz.at[self.index(kind, p, pick(z, slot))], (d, z + step))

        self.send(piece, piece, r.rx.at[t], (self.dx, z))
        self.send(piece, piece, r.ry.at[t], (self.dy, z))
        self.send(piece, piece, r.rs.at[t], (self.ds, z))

    def xy_stage(self, t):
        kind, p, i = self.units[t]
        z, q, r = self.z, self.q[i], self.r
        for sem, frm, to, half in ((r.rx, self.dx, self.dy, 0), (r.ry, self.dy, self.dx, 1)):
            self.wait(64, sem.at[t])
            h = self.parts(kind, p, q, frm, half)
            self.send(h, h, r.rd.at[t], (to, z))
            w = self.parts(kind, p, q, frm)
            self.send(w, w, r.rs.at[t], (self.ds, z))

    def d_stage(self, t):
        kind, p, i = self.units[t]
        self.wait(64, self.r.rd.at[t])
        w = self.parts(kind, p, self.q[i], self.dd)
        self.send(w, w, self.r.rs.at[t], (self.ds, self.z))

    def s_stage(self, t):
        self.wait(256, self.r.rs.at[t])

    def finish_sends(self):
        counts = []
        for k in range(4):
            c = 6 * ((k < 3) + (k > 0))
            for kind, p, i in self.units:
                quarter = ORDER[k][i]
                c += int(quarter < k and k < 3) + int(quarter > k and k > 0)
            counts.append(c + 7 * len(self.units))

        @pl.loop(0, pick(self.z, counts))
        def _(i):
            self.wait(64, self.r.sends)


    def to_planes(self, view, target, send_sem, recv_sem):
        for k in range(1, 4):
            j = (self.z + k) % 4
            pltpu.make_async_remote_copy(
                src_ref=view(j), dst_ref=target, send_sem=send_sem, recv_sem=recv_sem, device_id=(self.d, j), device_id_type=MESH
            ).start()

    def to_group(self, view, target, send_sem, recv_sem):
        for k in range(1, GROUP):
            m = (self.m + k) % GROUP
            pltpu.make_async_remote_copy(
                src_ref=view(m), dst_ref=target, send_sem=send_sem, recv_sem=recv_sem, device_id=(self.base + m, self.z), device_id_type=MESH
            ).start()

    def done(self, ref, *sems):
        for s in sems:
            pltpu.make_async_copy(ref, ref, s).wait()


def one_hot(r, p, transposed):
    R, T, n = r.R, r.T, r.n_img
    shape = (T, n * R) if transposed else (n * R, T)
    a = lax.broadcasted_iota(jnp.int32, shape, 1 if transposed else 0)
    b = lax.broadcasted_iota(jnp.int32, shape, 0 if transposed else 1)
    owner = jnp.zeros(shape, jnp.int32)
    for i in range(n):
        owner = jnp.where(a // R == i, r.ids[i, p], owner)
    hit = (b // R == owner) & (a % R == b % R)
    return jnp.where(hit, 1.0, 0.0).astype(BF)


def choose(r, p, flat):
    shape = (r.R, r.T)
    a = lax.broadcasted_iota(jnp.int32, shape, 0)
    b = lax.broadcasted_iota(jnp.int32, shape, 1)
    hit = (b // r.R == r.my_ids[p]) & (a == b % r.R)
    return dot(jnp.where(hit, 1.0, 0.0).astype(BF), flat).astype(BF)


def kernel(names, sizes, *refs):
    r = Bag()
    for n, f in zip(names, refs):
        setattr(r, n, f)
    for n, v in sizes.items():
        setattr(r, n, v)
    c = Stream(r)
    z, d = c.z, c.d
    W, FQ, R, n = r.W, r.FQ, r.R, r.n_img
    E = r.early
    r.length = r.len[z]
    r.my_ids = [r.ids[z, p] for p in range(4)]
    c.greet()
    load = []

    def fetch(src, dst):
        cp = pltpu.make_async_copy(src, dst, r.loc.at[len(load)])
        cp.start()
        load.append(cp)
        return cp

    l_x = fetch(r.tokens.at[z], r.x)
    l_ad = [fetch(getattr(r, "h_" + k), getattr(r, k)) for k in ("aqd", "aqu", "aod", "a1u", "a2d", "aou", "a1d", "a2u")]
    l_q = fetch(r.hq, r.wq.at[z])
    l_o = fetch(r.ho, r.wo.at[z])
    l_1 = fetch(r.h1, r.w1.at[z])
    l_2 = fetch(r.h2, r.w2.at[z])
    l_c = fetch(r.cot.at[z], r.dzq.at[z])
    c.met()
    kinds = [("A", 0), ("A", 1)] + [("B", p) for p in range(4)]
    for k in kinds[:2]:
        c.own_sends(*k)
    for cp in l_ad:
        cp.wait()
    hot = one_hot(r, 0, False)
    for i in range(3):
        flat = r.aqu[:, i].reshape(r.T, W)
        r.selout[:, :, i * W : (i + 1) * W] = dot(hot, flat).astype(BF).reshape(n, R, W)
    r.selout[:, :, 3 * W : 4 * W] = dot(one_hot(r, 1, False), r.aod[...]).astype(BF).reshape(n, R, W)
    r.selout[:, :, 4 * W : 4 * W + FQ] = dot(one_hot(r, 2, False), r.a1u[...]).astype(BF).reshape(n, R, FQ)
    r.selout[:, :, 4 * W + FQ :] = dot(one_hot(r, 3, False), r.a2d[...]).astype(BF).reshape(n, R, FQ)
    c.to_planes(lambda j: r.selout.at[j], r.sel.at[z], r.misc.at[0], r.misc.at[1])
    r.sel[z] = r.selout[z]
    for k in kinds[2:4]:
        c.own_sends(*k)
    r.dn_qkv[...] = choose(r, 0, r.aqd[...])
    r.up_out[...] = choose(r, 1, r.aou[...])
    r.dn_fc1[...] = choose(r, 2, r.a1d[...])
    r.up_fc2[...] = choose(r, 3, r.a2u[...])
    l_x.wait()
    prep(r)
    r.lift_qkv[...] = dot_nt(r.first[...], r.dn_qkv[...]).astype(BF)
    l_q.wait()
    l_o.wait()

    N = len(c.units)
    LZ, LX, LD = 2, 1, 1
    lag = LZ + LX + LD
    work = {}

    def at(tick, f):
        work.setdefault(tick, []).append(f)

    at(0, lambda: attn_fwd(r, c.q[0], True))
    at(1 + lag, lambda: c.done(r.sel.at[pl.ds(0, 3)], r.misc.at[0], r.misc.at[1]))
    at(1 + lag, lambda: attn_fwd(r, c.q[1], False))
    at(3 + lag, lambda: attn_fwd(r, c.q[2], False))
    at(2 + lag, lambda: [c.done(r.dzq.at[pl.ds(0, 3)], r.misc.at[2], r.misc.at[3]), l_c.wait(), prep_dz(r)])
    at(5 + lag, lambda: attn_fwd(r, c.q[3], False))
    at(5 + lag, lambda: [after_attn(r), l_1.wait(), l_2.wait()])
    at(6 + lag, lambda: ffn_unit(r, c.q[0], 0))
    at(7 + lag, lambda: ffn_unit(r, c.q[0], 1))
    for i in (1, 2, 3):
        for u in range(2):
            last = 6 + (i - 1) * 4 + 2 * u + 1
            at(last + lag, lambda i=i, u=u: ffn_unit(r, c.q[i], u))
    at(0, lambda: [c.own_sends(*kinds[4]), c.own_sends(*kinds[5])])
    at(0, lambda: c.to_planes(lambda j: r.cot.at[j], r.dzq.at[z], r.misc.at[2], r.misc.at[3]))
    for t in range(N + lag):
        if t < N:
            c.z_stage(t)
        if 0 <= t - LZ < N:
            c.xy_stage(t - LZ)
        if 0 <= t - LZ - LX < N:
            c.d_stage(t - LZ - LX)
        if 0 <= t - lag < N:
            c.s_stage(t - lag)
        for f in work.get(t, ()):
            f()

    after_ffn_out(r)
    mine = pl.ds(pl.multiple_of(z * W, W), W)

    def cut(ref):
        return lambda j: ref.at[:, pl.ds(pl.multiple_of(j * W, W), W)]

    c.to_planes(cut(r.out), r.outr.at[z], r.misc.at[4], r.misc.at[5])
    k_out = fetch(r.out.at[:, mine], r.outr.at[z])
    after_ffn_back(r)

    stages = []

    def make_stages(lo, rep, hi, s, fs, fr):
        cols, reps, own = pl.ds(lo, hi - lo), pl.ds(rep, hi - rep), pl.ds(lo, rep - lo)
        sem = [r.misc.at[s + k] for k in range(10)]

        def one():
            c.to_planes(lambda j: r.gall.at[j, :, cols], r.sp.at[z, :, cols], sem[0], sem[1])
            r.sp[z, :, cols] = r.gall[z, :, cols]

        def two():
            c.done(r.sp.at[pl.ds(0, 3), :, cols], sem[0], sem[1])
            for a, b, p in r.blocks:
                if lo <= a < hi:
                    v = r.sp[:, :, a:b].reshape(n * R, b - a)
                    r.dense[:, a:b] = dot(one_hot(r, p, True), v).astype(BF)
            c.to_group(lambda m: r.dense.at[pl.ds(pl.multiple_of(m * R, R), R), cols], r.rsb.at[c.m, :, cols], sem[2], sem[3])
            r.rsb[c.m, :, cols] = r.dense[pl.ds(pl.multiple_of(c.m * R, R), R), cols]

        def three():
            c.done(r.rsb.at[pl.ds(0, GROUP - 1), :, cols], sem[2], sem[3])
            total = r.rsb[0, :, cols].astype(F32)
            for k in range(1, GROUP):
                total = total + r.rsb[k, :, cols].astype(F32)
            r.red[:, cols] = total.astype(BF)
            zc = pl.ds(fr, hi - rep)
            c.to_planes(lambda j: r.red.at[:, reps], r.zb.at[z, :, zc], sem[4], sem[5])
            r.zb[z, :, zc] = r.red[:, reps]
            c.to_group(lambda m: r.red.at[:, own], r.fin_s.at[c.m, :, pl.ds(fs, rep - lo)], sem[6], sem[7])
            fetch(r.red.at[:, own], r.fin_s.at[c.m, :, pl.ds(fs, rep - lo)])

        def four():
            zc = pl.ds(fr, hi - rep)
            c.done(r.zb.at[pl.ds(0, 3), :, zc], sem[4], sem[5])
            c.to_group(lambda m: r.zb.at[:, :, zc], r.fin_r.at[c.m, :, :, zc], sem[8], sem[9])
            fetch(r.zb.at[:, :, zc], r.fin_r.at[c.m, :, :, zc])

        def five():
            zc = pl.ds(fr, hi - rep)
            c.done(r.fin_s.at[pl.ds(0, GROUP - 1), :, pl.ds(fs, rep - lo)], sem[6], sem[7])
            c.done(r.fin_r.at[pl.ds(0, GROUP - 1), :, :, zc], sem[8], sem[9])

        return one, two, three, four, five

    early = make_stages(0, 2 * FQ, E, 8, 0, 0)
    late = make_stages(E, E + 4 * W, E + 5 * W, 18, 2 * FQ, 3 * W)
    early[0]()
    attn_back(r, 0)
    early[1]()
    attn_back(r, 1)
    early[2]()
    attn_back(r, 2)
    early[3]()
    attn_back(r, 3)
    finish_grads(r)
    late[0]()
    finish_rows(r)
    c.to_planes(cut(r.gin), r.ginr.at[z], r.misc.at[6], r.misc.at[7])
    k_in = fetch(r.gin.at[:, mine], r.ginr.at[z])
    late[1]()
    late[2]()
    late[3]()
    early[4]()
    c.done(r.outr.at[pl.ds(0, 3)], r.misc.at[4], r.misc.at[5])
    c.finish_sends()
    late[4]()
    c.done(r.ginr.at[pl.ds(0, 3)], r.misc.at[6], r.misc.at[7])
    for cp in load[len(l_ad) + 6 :]:
        cp.wait()


def spread(out_ref, gin_ref, fs_ref, fr_ref, output, input_grad, qd, qu, od, ou, f1d, f1u, f2d, f2u):
    W = out_ref.shape[2]
    FQ = f1u.shape[2]
    output[...] = out_ref[...].astype(F32)
    input_grad[...] = gin_ref[...].astype(F32)
    f1u[...] = fs_ref[:, :, :FQ].astype(F32)
    f2d[...] = fs_ref[:, :, FQ : 2 * FQ].astype(F32)
    for i in range(3):
        qu[:, i] = fs_ref[:, :, 2 * FQ + i * W : 2 * FQ + (i + 1) * W].astype(F32)
    od[...] = fs_ref[:, :, 2 * FQ + 3 * W :].astype(F32)
    for k, ref in enumerate((f1d, f2u, ou, qd)):
        for j in range(4):
            ref[:, :, W * j : W * (j + 1)] = fr_ref[:, j, :, W * k : W * (k + 1)].astype(F32)


def make_shards(groups):
    def shards(
        tokens, lengths, adapter_ids, qkv_weight, qkv_down, qkv_up, out_weight, out_down, out_up,
        fc1_weight, fc1_down, fc1_up, fc2_weight, fc2_down, fc2_up, cotangent,
    ):
        n, S, D = tokens.shape
        A, _, R = qkv_down.shape
        T = A * R
        W = out_weight.shape[0]
        FQ = fc1_weight.shape[1]
        early = 2 * FQ + 3 * W
        total = early + 5 * W
        blocks = (
            (0, FQ, 2), (FQ, 2 * FQ, 3), (2 * FQ, 2 * FQ + W, 2), (2 * FQ + W, 2 * FQ + 2 * W, 3), (2 * FQ + 2 * W, early, 1),
            (early, early + 3 * W, 0), (early + 3 * W, early + 4 * W, 1), (early + 4 * W, total, 0),
        )
        sizes = dict(n_img=n, S=S, D=D, R=R, T=T, W=W, FQ=FQ, early=early, blocks=blocks)

        def turned(a):
            return jnp.transpose(a, (0, 2, 1)).reshape(T, a.shape[1])

        args = dict(
            len=lengths, ids=adapter_ids, tokens=tokens, cot=cotangent,
            hq=jnp.transpose(qkv_weight, (1, 0, 2)), ho=out_weight, h1=fc1_weight, h2=fc2_weight,
            h_aqd=turned(qkv_down), h_aqu=jnp.transpose(qkv_up, (0, 2, 1, 3)), h_aod=turned(out_down),
            h_a1u=fc1_up.reshape(T, FQ), h_a2d=turned(fc2_down), h_aou=out_up.reshape(T, D),
            h_a1d=turned(fc1_down), h_a2u=fc2_up.reshape(T, D),
        )
        outs = dict(outr=(n, S, W), ginr=(n, S, W), fin_s=(GROUP, R, 2 * FQ + 4 * W), fin_r=(GROUP, 4, R, 4 * W))
        vm = dict(
            wq=((4, 3, D, W), BF), wo=((4, W, D), BF), w1=((4, D, FQ), BF), w2=((4, FQ, D), BF),
            aqd=((T, D), BF), aqu=((A, 3, R, W), BF), aod=((T, W), BF), a1u=((T, FQ), BF), a2d=((T, FQ), BF),
            aou=((T, D), BF), a1d=((T, D), BF), a2u=((T, D), BF),
            selout=((n, R, 4 * W + 2 * FQ), BF), sel=((4, R, 4 * W + 2 * FQ), BF),
            dn_qkv=((R, D), BF), up_out=((R, D), BF), dn_fc1=((R, D), BF), up_fc2=((R, D), BF),
            x=((S, D), BF), dzq=((4, S, W), BF), dz=((S, D), BF),
            first=((S, D), BF), lift_qkv=((S, R), BF), g_fc2=((S, R), BF), proj=((4, 3, S, W), BF),
            soft=((4 * W // HD, S, S), F32), att=((4, S, W), BF), branch=((S, D), F32), lift_out_acc=((S, R), F32),
            lift_out=((S, R), BF), mixed=((S, D), F32), second=((S, D), BF), lift_fc1=((S, R), BF), outacc=((S, D), F32),
            gsec=((S, D), F32), lift_fc2_acc=((S, R), F32), glf1_acc=((S, R), F32), before=((S, STEP), F32), gh=((S, STEP), F32),
            hidden=((S, STEP), BF), gb=((S, STEP), BF), lift_fc2=((S, R), BF), gbr=((S, D), BF), g_out=((S, R), BF),
            glq_acc=((S, R), F32), ga=((S, W), BF), gp=((3, S, W), BF), out=((S, D), BF), gin=((S, D), BF),
            gall=((4, R, total), BF), sp=((n, R, total), BF), dense=((T, total), BF), rsb=((GROUP, R, total), BF),
            red=((R, total), BF), zb=((4, R, 4 * W), BF),
        )
        units = 18
        sems = dict(rz=units, rx=units, ry=units, rd=units, rs=units, sends=None, loc=24, misc=28)
        names = list(args) + list(outs) + list(vm) + list(sems)
        anywhere = pl.BlockSpec(memory_space=pl.ANY)
        got = pl.pallas_call(
            lambda *refs: kernel(names, sizes, *refs),
            out_shape=tuple(jax.ShapeDtypeStruct(s, BF) for s in outs.values()),
            in_specs=[pl.BlockSpec(memory_space=pltpu.SMEM)] * 2 + [anywhere] * (len(args) - 2),
            out_specs=tuple([anywhere] * len(outs)),
            scratch_shapes=[pltpu.VMEM(s, t) for s, t in vm.values()]
            + [pltpu.SemaphoreType.DMA if k is None else pltpu.SemaphoreType.DMA((k,)) for k in sems.values()],
            compiler_params=pltpu.CompilerParams(collective_id=0, has_side_effects=True, vmem_limit_bytes=60 * 2**20),
        )(*args.values())
        outr, ginr, fin_s, fin_r = got
        if groups > 1:
            across = [[m + GROUP * g for g in range(groups)] for m in range(GROUP)]
            fin_s, fin_r = lax.psum((fin_s.astype(F32), fin_r.astype(F32)), "dp", axis_index_groups=across)
        full = (A, R, D)
        vmem = pl.BlockSpec(memory_space=pltpu.VMEM)
        shapes = ((n, S, W), (n, S, W), full, (A, 3, R, W), (A, R, W), full, full, (A, R, FQ), (A, R, FQ), full)
        output, input_grad, qd, qu, od, ou, f1d, f1u, f2d, f2u = pl.pallas_call(
            spread,
            out_shape=tuple(jax.ShapeDtypeStruct(s, F32) for s in shapes),
            in_specs=[vmem] * 4,
            out_specs=tuple([vmem] * len(shapes)),
            compiler_params=pltpu.CompilerParams(vmem_limit_bytes=40 * 2**20),
        )(outr, ginr, fin_s, fin_r)
        back = lambda a: jnp.transpose(a, (0, 2, 1))
        return (output, input_grad, back(qd), jnp.transpose(qu, (0, 2, 1, 3)), back(od), ou, back(f1d), f1u, back(f2d), f2u)

    return shards


def solution(mesh):
    in_specs = (
        P("dp", None, None), P("dp"), P("dp", None), P(None, None, "tensor"), P(), P(None, None, None, "tensor"),
        P("tensor", None), P(None, "tensor", None), P(), P(None, "tensor"), P(), P(None, None, "tensor"),
        P("tensor", None), P(None, "tensor", None), P(), P("dp", None, "tensor"),
    )
    out_specs = (
        P("dp", None, "tensor"), P("dp", None, "tensor"), P(), P(None, None, None, "tensor"), P(None, "tensor", None),
        P(), P(), P(None, None, "tensor"), P(None, "tensor", None), P(),
    )
    shards = make_shards(mesh.shape["dp"] // GROUP)
    return jax.shard_map(shards, mesh=mesh, in_specs=in_specs, out_specs=out_specs, check_vma=False)
```

```python
import jax
import jax.numpy as jnp
from jax import lax
from jax.experimental import pallas as pl
from jax.experimental.pallas import tpu as pltpu
from jax.sharding import PartitionSpec as P


BF = jnp.bfloat16
F32 = jnp.float32
MESH = pl.DeviceIdType.MESH
EPSILON = 1e-6
NEG_FILL = -1e30
HD = 64
GROUP = 8
BLOCK = 160
SMALL = 32
STEP = 512


def dot(a, b):
    return lax.dot_general(a, b, (((1,), (0,)), ((), ())), preferred_element_type=F32)


def dot_nt(a, b):
    return lax.dot_general(a, b, (((1,), (1,)), ((), ())), preferred_element_type=F32)


def dot_tn(a, b):
    return lax.dot_general(a, b, (((0,), (0,)), ((), ())), preferred_element_type=F32)


def rows_loop(count, body, block=BLOCK):
    @pl.loop(0, count // block)
    def _(i):
        body(pl.ds(pl.multiple_of(i * block, block), block))


def moments(values):
    centred = values - jnp.mean(values, axis=-1, keepdims=True)
    inverse = lax.rsqrt(jnp.mean(centred * centred, axis=-1, keepdims=True) + EPSILON)
    return centred, inverse


def norm_back(values, grad):
    centred, inverse = moments(values)
    hat = centred * inverse
    return inverse * (
        grad - jnp.mean(grad, axis=-1, keepdims=True) - hat * jnp.mean(grad * hat, axis=-1, keepdims=True)
    )


class Bag:
    pass


def prep(r):
    def body(rows):
        centred, inverse = moments(r.x[rows, :].astype(F32))
        r.first[rows, :] = (centred * inverse).astype(BF)

    rows_loop(r.S, body)


def prep_dz(r):
    def body(rows):
        keep = (lax.broadcasted_iota(jnp.int32, (BLOCK, 1), 0) + rows.start) < r.length
        for j in range(4):
            v = r.dzq[j, rows, :]
            r.dz[rows, r.W * j : r.W * (j + 1)] = jnp.where(keep, v, jnp.zeros_like(v))

    rows_loop(r.S, body)
    r.g_fc2[...] = dot_nt(r.dz[...], r.up_fc2[...]).astype(BF)


def by_head(r, v, ref):
    head = lax.broadcasted_iota(jnp.int32, (r.S, r.W), 1) // HD
    for h in range(r.W // HD):
        ref[h * r.S : (h + 1) * r.S, :] = jnp.where(head == h, v, jnp.zeros_like(v))


def own_lanes(r, t):
    head = lax.broadcasted_iota(jnp.int32, (r.S, r.W), 1) // HD
    out = t[: r.S]
    for h in range(1, r.W // HD):
        out = jnp.where(head == h, t[h * r.S : (h + 1) * r.S], out)
    return out


def block_of(q, width):
    return pl.ds(pl.multiple_of(q * width, width), width)


def attn_fwd(r, q):
    S, W = r.S, r.W
    p = dot(r.first[...], r.wq[q]) + dot(r.lift_qkv[...], r.sel_qu[:, block_of(q, 3 * W)])
    r.proj[q] = p.astype(BF)
    by_head(r, r.proj[q, :, 0:W], r.qm.at[q])
    r.st[...] = dot_nt(r.proj[q, :, W : 2 * W], r.qm[q])
    valid = lax.broadcasted_iota(jnp.int32, (S, 128), 0) < r.length

    for k in range(r.st.shape[1] // 128):
        c = slice(k * 128, (k + 1) * 128)
        v = jnp.where(valid, r.st[:, c] * (HD**-0.5), NEG_FILL)
        e = jnp.exp(v - jnp.max(v, axis=0, keepdims=True))
        soft = e * (1.0 / jnp.sum(e, axis=0, keepdims=True))
        r.soft[q, :, c] = soft
        r.ds[:, c] = soft.astype(BF)

    att = own_lanes(r, dot_tn(r.ds[...], r.proj[q, :, 2 * W : 3 * W])).astype(BF)
    r.att[:, block_of(q, W)] = att
    r.branch[...] += dot(att, r.wo[q])


def after_attn(r):
    r.lift_out[...] = dot_nt(r.att[...], r.sel_od[...]).astype(BF)
    r.branch[...] += dot(r.lift_out[...], r.up_out[...])

    def body(rows):
        mixed = r.x[rows, :].astype(F32) + r.branch[rows, :]
        r.mixed[rows, :] = mixed
        centred, inverse = moments(mixed)
        r.second[rows, :] = (centred * inverse).astype(BF)

    rows_loop(r.S, body)
    r.lift_fc1[...] = dot_nt(r.second[...], r.dn_fc1[...]).astype(BF)
    r.outacc[...] = jnp.zeros_like(r.outacc)
    r.gsec[...] = jnp.zeros_like(r.gsec)
    r.lift_fc2_acc[...] = jnp.zeros_like(r.lift_fc2_acc)
    r.glf1_acc[...] = jnp.zeros_like(r.glf1_acc)


def ffn_unit(r, q, u):
    FQ = r.FQ
    cols = block_of(u, STEP)
    wide = pl.ds(pl.multiple_of(q * FQ + u * STEP, STEP), STEP)
    up1 = r.sel_f1[:, wide]
    dn2 = r.sel_f2[:, wide]
    r.before[...] = dot(r.second[...], r.w1[q, :, cols]) + dot(r.lift_fc1[...], up1)
    r.gh[...] = dot_nt(r.dz[...], r.w2[q, cols, :]) + dot(r.g_fc2[...], dn2)

    def body(rows):
        b = r.before[rows, :]
        cdf = 0.5 * (1.0 + lax.erf(b * (0.5**0.5)))
        r.hidden[rows, :] = (b * cdf).astype(BF)
        slope = cdf + b * jnp.exp(-0.5 * b * b) * 0.3989422804014327
        r.gb[rows, :] = (slope * r.gh[rows, :]).astype(BF)

    for k in range(r.S // SMALL):
        body(pl.ds(k * SMALL, SMALL))
    h = r.hidden[...]
    g = r.gb[...]
    r.outacc[...] += dot(h, r.w2[q, cols, :])
    r.gsec[...] += dot_nt(g, r.w1[q, :, cols])
    r.lift_fc2_acc[...] += dot_nt(h, dn2)
    r.glf1_acc[...] += dot_nt(g, up1)
    r.g_f1[:, wide] = dot_tn(r.lift_fc1[...], g).astype(BF)
    r.g_f2[:, wide] = dot_tn(r.g_fc2[...], h).astype(BF)


def after_ffn_out(r):
    r.outacc[...] += dot(r.lift_fc2[...], r.up_fc2[...])

    def body(rows):
        keep = (lax.broadcasted_iota(jnp.int32, (BLOCK, 1), 0) + rows.start) < r.length
        r.out[rows, :] = jnp.where(keep, r.mixed[rows, :] + r.outacc[rows, :], 0.0).astype(BF)

    rows_loop(r.S, body)


def after_ffn_back(r):
    r.lift_fc2[...] = r.lift_fc2_acc[...].astype(BF)
    g1 = r.glf1_acc[...].astype(BF)
    r.g_f2u[...] = dot_tn(r.lift_fc2[...], r.dz[...]).astype(BF)
    r.g_f1d[...] = dot_tn(g1, r.second[...]).astype(BF)
    r.gsec[...] += dot(g1, r.dn_fc1[...])

    def body(rows):
        g = r.dz[rows, :].astype(F32) + norm_back(r.mixed[rows, :], r.gsec[rows, :])
        r.gsec[rows, :] = g
        r.gbr[rows, :] = g.astype(BF)

    rows_loop(r.S, body)
    gbr = r.gbr[...]
    r.g_ou[...] = dot_tn(r.lift_out[...], gbr).astype(BF)
    r.g_out[...] = dot_nt(gbr, r.up_out[...]).astype(BF)


def back_attended(r):
    W = r.W
    r.ga[...] = dot(r.g_out[...], r.sel_od[...])
    for q in range(4):
        c = slice(q * W, (q + 1) * W)
        r.ga[:, c] += dot_nt(r.gbr[...], r.wo[q])
    r.g_od[...] = dot_tn(r.g_out[...], r.att[...]).astype(BF)


def attn_back(r, q):
    W = r.W
    sc = HD**-0.5
    by_head(r, r.ga[:, block_of(q, W)].astype(BF), r.gm)
    k = r.proj[q, :, W : 2 * W]
    r.st[...] = dot_nt(r.proj[q, :, 2 * W : 3 * W], r.gm[...])
    gv = dot(r.soft[q].astype(BF), r.gm[...])

    for i in range(r.st.shape[1] // 128):
        c = slice(i * 128, (i + 1) * 128)
        soft, gs = r.soft[q, :, c], r.st[:, c]
        r.ds[:, c] = (soft * (gs - jnp.sum(soft * gs, axis=0, keepdims=True))).astype(BF)

    ds = r.ds[...]
    base = pl.multiple_of(3 * W * q, 128)
    r.gp[:, pl.ds(base, W)] = (own_lanes(r, dot_tn(ds, k)) * sc).astype(BF)
    r.gp[:, pl.ds(base + W, W)] = (dot(ds, r.qm[q]) * sc).astype(BF)
    r.gp[:, pl.ds(base + 2 * W, W)] = gv.astype(BF)
    wide = block_of(q, 3 * W)
    r.g_qu[:, wide] = dot_tn(r.lift_qkv[...], r.gp[:, wide]).astype(BF)


def finish_grads(r):
    gq = dot_nt(r.gp[...], r.sel_qu[...]).astype(BF)
    r.g_qd[...] = dot_tn(gq, r.first[...]).astype(BF)
    r.g_qkv[...] = gq


def back_first(r):
    W = r.W
    r.mixed[...] = dot(r.g_qkv[...], r.dn_qkv[...])
    for q in range(4):
        r.mixed[...] += dot_nt(r.gp[:, 3 * W * q : 3 * W * (q + 1)], r.wq[q])


def finish_rows(r, k):
    rows = slice(k * (r.S // 2), (k + 1) * (r.S // 2))
    r.gin[rows, :] = (r.gsec[rows, :] + norm_back(r.x[rows, :].astype(F32), r.mixed[rows, :])).astype(BF)


class Stream:
    def __init__(self, r):
        self.r = r
        d = self.d = lax.axis_index("dp")
        self.z = lax.axis_index("tensor")
        m = self.m = d % GROUP
        self.base = d - m
        self.dx = d + 2 - 4 * ((m // 2) % 2)
        self.dy = d + 4 - 8 * (m // 4)
        self.ds = d + 1 - 2 * (m % 2)
        self.dd = self.dx + self.dy - d
        self.inner = (self.z + 1) // 2 == 1
        self.n_a, self.n = 6, 18

    def quarter(self, i):
        return (self.z + jnp.where(self.z < 2, i, 4 - i)) % 4

    def unit(self, t, f):
        pl.when(t < self.n_a)(lambda: f("A", t % 2, t // 2 + 1))
        pl.when(t >= self.n_a)(lambda: f("B", (t - self.n_a) % 4, (t - self.n_a) // 4 + 1))

    def greet(self):
        bar = pltpu.get_barrier_semaphore()
        for k in range(1, GROUP):
            peer = self.base + (self.m + k) % GROUP
            pl.semaphore_signal(bar, inc=1, device_id=(peer, self.z), device_id_type=MESH)
        for k in range(1, 4):
            pl.semaphore_signal(bar, inc=1, device_id=(self.d, (self.z + k) % 4), device_id_type=MESH)

    def met(self):
        pl.semaphore_wait(pltpu.get_barrier_semaphore(), GROUP + 2)

    def parts(self, kind, p, q, d, half=None):
        r, m = self.r, d - self.base
        first, c = (0, pl.ds(0, r.D)) if half is None else (half, pl.ds(r.D // 2 * half, r.D // 2))
        if kind == "A":
            n = r.D // GROUP // 2
            k = r.W // GROUP // 2
            part = n if half is None else n // 2
            a = pl.ds(pl.multiple_of((2 * m + p) * n + first * part, part), part)
            b = pl.ds(pl.multiple_of((2 * m + p) * k, k), k)
            return ((r.wq.at[q, a, :]), (r.wo.at[q, b, c]))
        n = r.D // GROUP
        width = r.FQ // 4
        k = width // GROUP
        part = n if half is None else n // 2
        a = pl.ds(pl.multiple_of(m * n + first * part, part), part)
        b = pl.ds(pl.multiple_of(p * width + m * k, k), k)
        return (r.w1.at[q, a, block_of(p, width)], r.w2.at[q, b, c])

    def own(self, kind, p):
        r, m, z = self.r, self.m, self.z
        first, second = self.parts(kind, p, z, self.d)
        if kind == "A":
            n = r.D // GROUP // 2
            k = r.W // GROUP // 2
            a = pl.ds(pl.multiple_of((2 * m + p) * n, n), n)
            pairs = [(r.hq.at[i, a, :], r.wq.at[z, a, pl.ds(i * r.W, r.W)]) for i in range(3)]
            return pairs + [(r.ho.at[pl.ds(pl.multiple_of((2 * m + p) * k, k), k), :], second)]
        n = r.D // GROUP
        k = r.FQ // 4 // GROUP
        a = pl.ds(pl.multiple_of(m * n, n), n)
        b = pl.ds(pl.multiple_of(p * (r.FQ // 4) + m * k, k), k)
        return [(r.h1.at[a, block_of(p, r.FQ // 4)], first), (r.h2.at[b, :], second)]

    def send(self, srcs, dsts, sem, dev):
        for s, t in zip(srcs, dsts):
            pltpu.make_async_remote_copy(
                src_ref=s, dst_ref=t, send_sem=self.r.sends, recv_sem=sem, device_id=dev, device_id_type=MESH
            ).start()

    def wait(self, rows, sem):
        v = self.r.w2.at[0, pl.ds(0, rows), :]
        pltpu.make_async_copy(v, v, sem).wait()

    def index(self, kind, p, i):
        return (i - 1) * 2 + p if kind == "A" else 6 + (i - 1) * 4 + p

    def inner_sends(self, kind, p):
        z, d = self.z, self.d

        @pl.when(self.inner)
        def _():
            src, dst = zip(*self.own(kind, p))
            for to in (3 * (z - 1), 3 - z):
                self.send(src, dst, self.r.rz.at[self.index(kind, p, 1)], (d, to))

    def outer_sends(self, kind, p, i):
        z, d = self.z, self.d

        @pl.when(z % 3 == 0)
        def _():
            src, dst = zip(*self.own(kind, p))
            to = 2 - z // 3 if i == 2 else 1 + z // 3
            self.send(src, dst, self.r.rz.at[self.index(kind, p, i)], (d, to))

    def z_stage(self, t):
        self.wait(64, self.r.rz.at[t])

        def forward(kind, p, i):
            @pl.when(self.inner & (i < 3))
            def _():
                piece = self.parts(kind, p, self.quarter(i), self.d)
                self.send(piece, piece, self.r.rz.at[self.index(kind, p, i + 1)], (self.d, 3 * (self.z - 1)))

        self.unit(t, forward)

    def xy_sends(self, t):
        def go(kind, p, i):
            z, r = self.z, self.r
            piece = self.parts(kind, p, self.quarter(i), self.d)
            self.send(piece, piece, r.rx.at[t], (self.dx, z))
            self.send(piece, piece, r.ry.at[t], (self.dy, z))
            self.send(piece, piece, r.rs.at[t], (self.ds, z))

        self.unit(t, go)

    def xy_stage(self, t):
        def go(kind, p, i):
            z, q, r = self.z, self.quarter(i), self.r
            for sem, frm, to, half in ((r.rx, self.dx, self.dy, 0), (r.ry, self.dy, self.dx, 1)):
                self.wait(64, sem.at[t])
                h = self.parts(kind, p, q, frm, half)
                self.send(h, h, r.rd.at[t], (to, z))
                w = self.parts(kind, p, q, frm)
                self.send(w, w, r.rs.at[t], (self.ds, z))

        self.unit(t, go)

    def d_stage(self, t):
        def go(kind, p, i):
            self.wait(64, self.r.rd.at[t])
            w = self.parts(kind, p, self.quarter(i), self.dd)
            self.send(w, w, self.r.rs.at[t], (self.ds, self.z))

        self.unit(t, go)

    def s_stage(self, t):
        self.wait(256, self.r.rs.at[t])

    def finish_sends(self):
        kinds = 6
        always = 7 * self.n + 2 * kinds

        @pl.loop(0, jnp.where(self.inner, always + 2 * kinds, always))
        def _(i):
            self.wait(64, self.r.sends)


    def to_planes(self, view, target, send_sem, recv_sem):
        for k in range(1, 4):
            j = (self.z + k) % 4
            pltpu.make_async_remote_copy(
                src_ref=view(j), dst_ref=target, send_sem=send_sem, recv_sem=recv_sem, device_id=(self.d, j), device_id_type=MESH
            ).start()

    def to_group(self, view, target, send_sem, recv_sem):
        for k in range(1, GROUP):
            m = (self.m + k) % GROUP
            pltpu.make_async_remote_copy(
                src_ref=view(m), dst_ref=target, send_sem=send_sem, recv_sem=recv_sem, device_id=(self.base + m, self.z), device_id_type=MESH
            ).start()

    def share(self, src, dst, sems):
        place = dst(self.m)
        for to in (self.dx, self.dy, self.dd):
            pltpu.make_async_remote_copy(
                src_ref=src, dst_ref=place, send_sem=sems[0], recv_sem=sems[1], device_id=(to, self.z), device_id_type=MESH
            ).start()
        pltpu.make_async_remote_copy(
            src_ref=src, dst_ref=place, send_sem=sems[2], recv_sem=sems[3], device_id=(self.ds, self.z), device_id_type=MESH
        ).start()

    def pass_on(self, three, dst, sems):
        self.done(three, sems[1])
        for frm in (self.dx, self.dy, self.dd):
            place = dst(frm - self.base)
            pltpu.make_async_remote_copy(
                src_ref=place, dst_ref=place, send_sem=sems[2], recv_sem=sems[3], device_id=(self.ds, self.z), device_id_type=MESH
            ).start()

    def done(self, ref, *sems):
        for s in sems:
            pltpu.make_async_copy(ref, ref, s).wait()


class Sems:
    def __init__(self, ref, first):
        self.ref, self.first = ref, first

    def __getitem__(self, k):
        if isinstance(k, slice):
            return [self[i] for i in range(k.start, k.stop)]
        return self.ref.at[self.first + k]


def one_hot(r, p, transposed):
    R, T, n = r.R, r.T, r.n_img
    shape = (T, n * R) if transposed else (n * R, T)
    a = lax.broadcasted_iota(jnp.int32, shape, 1 if transposed else 0)
    b = lax.broadcasted_iota(jnp.int32, shape, 0 if transposed else 1)
    owner = jnp.zeros(shape, jnp.int32)
    for i in range(n):
        owner = jnp.where(a // R == i, r.ids[i, p], owner)
    hit = (b // R == owner) & (a % R == b % R)
    return jnp.where(hit, 1.0, 0.0).astype(BF)


def choose(r, p, flat):
    shape = (r.R, r.T)
    a = lax.broadcasted_iota(jnp.int32, shape, 0)
    b = lax.broadcasted_iota(jnp.int32, shape, 1)
    hit = (b // r.R == r.my_ids[p]) & (a == b % r.R)
    return dot(jnp.where(hit, 1.0, 0.0).astype(BF), flat).astype(BF)


def kernel(names, sizes, *refs):
    r = Bag()
    for n, f in zip(names, refs):
        setattr(r, n, f)
    for n, v in sizes.items():
        setattr(r, n, v)
    c = Stream(r)
    z, d = c.z, c.d
    S, W, FQ, R, n = r.S, r.W, r.FQ, r.R, r.n_img
    r.before, r.gh = r.st.at[:, pl.ds(0, STEP)], r.st.at[:, pl.ds(STEP, STEP)]
    r.hidden, r.gb = r.ds.at[:, pl.ds(0, STEP)], r.ds.at[:, pl.ds(STEP, STEP)]
    r.ga = r.branch
    r.out, r.gin = r.second, r.first
    r.length = r.len[z]
    r.my_ids = [r.ids[z, p] for p in range(4)]
    c.greet()
    load = []

    def fetch(ends):
        slot = len(load)
        copy = lambda: pltpu.make_async_copy(*ends(), r.loc.at[slot])
        copy().start()
        load.append(copy)
        return copy

    l_x = fetch(lambda: (r.tokens.at[z], r.x))
    l_ad = {k: fetch(lambda k=k: (getattr(r, "h_" + k), getattr(r, k))) for k in ("aqd", "aqu", "aod", "a1u", "a2d", "aou", "a1d", "a2u")}
    l_q = [fetch(lambda i=i: (r.hq.at[i], r.wq.at[z, :, pl.ds(i * W, W)])) for i in range(3)]
    l_q.append(fetch(lambda: (r.ho, r.wo.at[z])))
    l_f = [fetch(lambda: (r.h1, r.w1.at[z])), fetch(lambda: (r.h2, r.w2.at[z]))]
    l_c = fetch(lambda: (r.cot.at[z], r.dzq.at[z]))
    c.met()

    def wait_all(copies):
        for copy in copies:
            copy().wait()

    def pick_attn():
        wait_all([l_ad["aqu"], l_ad["aod"]])
        hot = one_hot(r, 0, False)
        for i in range(3):
            r.out_qu[:, :, i * W : (i + 1) * W] = dot(hot, r.aqu[:, i].reshape(r.T, W)).astype(BF).reshape(n, R, W)
        r.out_od[...] = dot(one_hot(r, 1, False), r.aod[...]).astype(BF).reshape(n, R, W)
        c.to_planes(lambda j: r.out_qu.at[j], r.sel_qu.at[:, block_of(z, 3 * W)], r.misc.at[0], r.misc.at[1])
        c.to_planes(lambda j: r.out_od.at[j], r.sel_od.at[:, block_of(z, W)], r.misc.at[70], r.misc.at[71])
        r.sel_qu[:, block_of(z, 3 * W)] = r.out_qu[z]
        r.sel_od[:, block_of(z, W)] = r.out_od[z]

    def have_attn():
        c.done(r.sel_qu.at[:, pl.ds(0, 9 * W)], r.misc.at[0], r.misc.at[1])
        c.done(r.sel_od.at[:, pl.ds(0, 3 * W)], r.misc.at[70], r.misc.at[71])

    def pick_ffn():
        wait_all([l_ad["a1u"], l_ad["a2d"]])
        r.out_f1[...] = dot(one_hot(r, 2, False), r.a1u[...]).astype(BF).reshape(n, R, FQ)
        r.out_f2[...] = dot(one_hot(r, 3, False), r.a2d[...]).astype(BF).reshape(n, R, FQ)
        r.sel_f1[:, block_of(z, FQ)] = r.out_f1[z]
        r.sel_f2[:, block_of(z, FQ)] = r.out_f2[z]

    def send_f1():
        c.to_planes(lambda j: r.out_f1.at[j], r.sel_f1.at[:, block_of(z, FQ)], r.misc.at[72], r.misc.at[73])

    def send_f2():
        c.to_planes(lambda j: r.out_f2.at[j], r.sel_f2.at[:, block_of(z, FQ)], r.misc.at[74], r.misc.at[75])

    def have_ffn():
        c.done(r.sel_f1.at[:, pl.ds(0, 3 * FQ)], r.misc.at[72], r.misc.at[73])
        c.done(r.sel_f2.at[:, pl.ds(0, 3 * FQ)], r.misc.at[74], r.misc.at[75])

    def pick_first():
        l_ad["aqd"]().wait()
        r.dn_qkv[...] = choose(r, 0, r.aqd[...])
        r.lift_qkv[...] = dot_nt(r.first[...], r.dn_qkv[...]).astype(BF)

    def pick_rest():
        wait_all([l_ad["aou"], l_ad["a1d"], l_ad["a2u"]])
        r.up_out[...] = choose(r, 1, r.aou[...])
        r.dn_fc1[...] = choose(r, 2, r.a1d[...])
        r.up_fc2[...] = choose(r, 3, r.a2u[...])

    CUTS = 5

    def send_cot(k):
        rows = pl.ds(k * (S // CUTS), S // CUTS)
        c.to_planes(lambda j: r.cot.at[j, rows, :], r.dzq.at[z, rows, :], r.misc.at[2], r.misc.at[3])

    def have_cot():
        c.done(r.dzq.at[pl.ds(0, 3)], r.misc.at[2], r.misc.at[3])
        l_c().wait()
        prep_dz(r)

    def ffn(n):
        i, u = n // 2, n % 2
        q = c.quarter(i)
        ffn_unit(r, q, u)

        @pl.when(i > 0)
        def _():
            wide = pl.ds(pl.multiple_of(q * FQ + u * STEP, STEP), STEP)
            for ref, base in ((r.g_f1, 0), (r.g_f2, FQ)):
                pltpu.make_async_remote_copy(
                    src_ref=ref.at[:, wide], dst_ref=r.sp.at[z, :, pl.ds(pl.multiple_of(base + u * STEP, STEP), STEP)],
                    send_sem=r.misc.at[8], recv_sem=r.misc.at[9], device_id=(d, q), device_id_type=MESH,
                ).start()

    N = c.n
    LZ, LX, LD = 2, 1, 1
    lag = LZ + LX + LD
    c.inner_sends("A", 0)
    c.inner_sends("A", 1)
    l_x().wait()
    prep(r)
    r.branch[...] = jnp.zeros_like(r.branch)
    c.z_stage(0)

    @pl.loop(0, N + lag)
    def _(t):
        pl.when(t < N)(lambda: c.xy_sends(t))
        pl.when((t >= LZ) & (t < LZ + N))(lambda: c.xy_stage(t - LZ))
        pl.when((t >= LZ + LX) & (t < LZ + LX + N))(lambda: c.d_stage(t - LZ - LX))
        pl.when(t >= lag)(lambda: c.s_stage(t - lag))
        pl.when(t + 1 < N)(lambda: c.z_stage(t + 1))
        pl.when(t < 4)(lambda: c.inner_sends("B", t))

        @pl.when((t == 0) | (t == 2))
        def _():
            for p in range(2):
                pl.when(t == 0)(lambda: c.outer_sends("A", p, 2))
                pl.when(t == 2)(lambda: c.outer_sends("A", p, 3))

        pl.when((t >= 2) & (t < 6))(lambda: c.outer_sends("B", t - 2, 2))
        pl.when((t >= 6) & (t < 10))(lambda: c.outer_sends("B", t - 6, 3))
        pl.when((t >= 3) & (t < 3 + 2 * CUTS) & (t % 2 == 1))(lambda: send_cot((t - 3) // 2))
        pl.when(t == 0)(pick_first)
        pl.when(t == 1)(pick_attn)
        pl.when(t == 2)(lambda: wait_all(l_q))
        pl.when(t == 3)(pick_rest)
        pl.when(t == 4)(pick_ffn)
        pl.when(t == 9)(send_f1)
        pl.when(t == 11)(send_f2)
        pl.when(t == 1 + lag)(have_attn)
        pl.when((t == 2) | (t == 1 + lag) | (t == 3 + lag) | (t == 5 + lag))(lambda: attn_fwd(r, c.quarter((t - 2) // 2)))

        @pl.when(t == 5 + lag)
        def _():
            after_attn(r)
            wait_all(l_f)

        pl.when(t == 13)(have_cot)
        pl.when(t == 15)(have_ffn)
        pl.when((t >= 13) & (t != 20))(lambda: ffn(jnp.minimum(t - 13, 7)))

    mine = block_of(z, W)

    def cut(ref):
        return lambda j: ref.at[:, block_of(j, W)]

    def group(lo, own_end, hi, s, fs, fr, out=None):
        cols, own, reps, zc = pl.ds(lo, hi - lo), pl.ds(lo, own_end - lo), pl.ds(own_end, hi - own_end), pl.ds(fr, hi - own_end)
        sem = Sems(r.misc, s)
        fin = pl.ds(fs, own_end - lo)
        fin_s = r.fin_s if out is None else out

        def send_whole(ref, col):
            c.to_planes(lambda j: ref, r.sp.at[z, :, cols], sem[0], sem[1])
            r.sp[z, :, cols] = ref[...]

        def send(sources):
            for ref, width, col in sources:
                c.to_planes(lambda j: ref.at[:, block_of(j, width)], r.sp.at[z, :, pl.ds(col, width)], sem[0], sem[1])
                r.sp[z, :, col : col + width] = ref[:, block_of(z, width)]

        def expand():
            c.done(r.sp.at[pl.ds(0, 3), :, cols], sem[0], sem[1])
            for a, b, p in r.blocks:
                if lo <= a < hi:
                    r.dense[:, a:b] = dot(one_hot(r, p, True), r.sp[:, :, a:b].reshape(n * R, b - a)).astype(BF)
            c.to_group(lambda m: r.dense.at[block_of(m, R), cols], r.rsb.at[c.m, :, cols], sem[2], sem[3])
            r.rsb[c.m, :, cols] = r.dense[block_of(c.m, R), cols]

        def reduce():
            c.done(r.rsb.at[pl.ds(0, GROUP - 1), :, cols], sem[2], sem[3])
            sums = r.rsb[0, :, cols].astype(F32)
            for k in range(1, GROUP):
                sums = sums + r.rsb[k, :, cols].astype(F32)
            r.red[:, cols] = sums.astype(BF)
            if hi > own_end:
                c.to_planes(lambda j: r.red.at[:, reps], r.zb.at[z, :, zc], sem[4], sem[5])
                r.zb[z, :, zc] = r.red[:, reps]
            if own_end > lo:
                c.share(r.red.at[:, own], lambda m: fin_s.at[m, :, fin], sem[6:10])
                fetch(lambda: (r.red.at[:, own], fin_s.at[c.m, :, fin]))

        def share():
            c.done(r.zb.at[pl.ds(0, 3), :, zc], sem[4], sem[5])
            c.share(r.zb.at[:, :, zc], lambda m: r.fin_r.at[m, :, :, zc], sem[10:14])
            fetch(lambda: (r.zb.at[:, :, zc], r.fin_r.at[c.m, :, :, zc]))

        def relay():
            if own_end > lo:
                c.pass_on(fin_s.at[pl.ds(0, 3), :, fin], lambda m: fin_s.at[m, :, fin], sem[6:10])

        def relay_rep():
            c.pass_on(r.fin_r.at[pl.ds(0, 3), :, :, zc], lambda m: r.fin_r.at[m, :, :, zc], sem[10:14])

        def close():
            if own_end > lo:
                c.done(fin_s.at[pl.ds(0, 3), :, fin], sem[6])
                c.done(fin_s.at[pl.ds(0, 4), :, fin], sem[8], sem[9])
            if hi > own_end:
                c.done(r.fin_r.at[pl.ds(0, 3), :, :, zc], sem[10])
                c.done(r.fin_r.at[pl.ds(0, 4), :, :, zc], sem[12], sem[13])

        return send if out is None else send_whole, expand, reduce, share, relay, relay_rep, close

    m0, l0, end = r.starts
    _, e_expand, e_reduce, _, e_relay, _, e_close = group(0, m0, m0, 8, 0, 0)
    m_send, m_expand, m_reduce, m_share, _, m_relay, m_close = group(m0, m0, l0, 22, 0, 0)
    p0 = l0 + 4 * W
    l_send, l_expand, l_reduce, _, l_relay, _, l_close = group(l0, p0, p0, 36, 2 * FQ, 0)
    p_send, p_expand, p_reduce, _, p_relay, _, p_close = group(p0, end, end, 56, 0, 0, r.fin_p)

    def back(q):
        attn_back(r, q)
        for ref, width, col in ((r.g_qu, 3 * W, l0), (r.g_od, W, l0 + 3 * W)):
            src, dst = ref.at[:, block_of(q, width)], r.sp.at[z, :, pl.ds(col, width)]

            @pl.when(z != q)
            def _():
                pltpu.make_async_remote_copy(
                    src_ref=src, dst_ref=dst, send_sem=r.misc.at[36], recv_sem=r.misc.at[37], device_id=(d, q), device_id_type=MESH
                ).start()

    after_ffn_back(r)
    m_send([(r.g_f1d, W, m0), (r.g_f2u, W, m0 + W), (r.g_ou, W, m0 + 2 * W)])
    after_ffn_out(r)
    c.to_planes(cut(r.out), r.outr.at[z], r.misc.at[4], r.misc.at[5])
    fetch(lambda: (r.out.at[:, mine], r.outr.at[z]))
    for ref, base in ((r.g_f1, 0), (r.g_f2, FQ)):
        r.sp[z, :, base : base + FQ] = ref[:, block_of(z, FQ)]
    back_attended(r)
    e_expand()

    @pl.loop(0, 4)
    def _(q):
        back(q)

    e_reduce()
    m_expand()
    finish_grads(r)
    p_send(r.g_qd, p0)
    for ref, width, col in ((r.g_qu, 3 * W, l0), (r.g_od, W, l0 + 3 * W)):
        r.sp[z, :, col : col + width] = ref[:, block_of(z, width)]
    m_reduce()
    back_first(r)
    half = S // 2

    def send_gin(k):
        rows = pl.ds(k * half, half)
        c.to_planes(lambda j: r.gin.at[rows, block_of(j, W)], r.ginr.at[z, rows, :], r.misc.at[6], r.misc.at[7])
        fetch(lambda: (r.gin.at[rows, mine], r.ginr.at[z, rows, :]))

    p_expand()
    l_expand()
    finish_rows(r, 0)
    send_gin(0)
    finish_rows(r, 1)
    send_gin(1)
    e_relay()
    m_share()
    p_reduce()
    l_reduce()
    m_relay()
    l_relay()
    p_relay()
    e_close()
    m_close()
    c.done(r.outr.at[pl.ds(0, 3)], r.misc.at[4], r.misc.at[5])
    c.finish_sends()
    l_close()
    p_close()
    c.done(r.ginr.at[pl.ds(0, 3)], r.misc.at[6], r.misc.at[7])
    wait_all(load[1 + len(l_ad) + 7 :])


def spread(names, *refs):
    r = Bag()
    for n, f in zip(names, refs):
        setattr(r, n, f)
    W = r.b_out.shape[2]
    FQ = r.v_f1u.shape[2]
    loads = []
    for k, (src, dst) in enumerate(((r.outr, r.b_out), (r.ginr, r.b_gin), (r.fin_s, r.b_s), (r.fin_r, r.b_r), (r.fin_p, r.b_p))):
        loads.append(pltpu.make_async_copy(src, dst, r.sem_in.at[k]))
        loads[-1].start()
    stores = []

    def store(key):
        stores.append(pltpu.make_async_copy(getattr(r, "v_" + key), getattr(r, "o_" + key), r.sem_out.at[len(stores)]))
        stores[-1].start()

    def widen(ref, value):
        ref[...] = value.astype(F32)

    loads[0].wait()
    widen(r.v_out, r.b_out[...])
    store("out")
    loads[1].wait()
    widen(r.v_gin, r.b_gin[...])
    store("gin")
    loads[2].wait()
    widen(r.v_f1u, r.b_s[:, :, :FQ])
    store("f1u")
    widen(r.v_f2d, r.b_s[:, :, FQ : 2 * FQ])
    store("f2d")
    for i in range(3):
        r.v_qu[:, i] = r.b_s[:, :, 2 * FQ + i * W : 2 * FQ + (i + 1) * W].astype(F32)
    store("qu")
    widen(r.v_od, r.b_s[:, :, 2 * FQ + 3 * W :])
    store("od")
    loads[3].wait()
    for k, key in enumerate(("f1d", "f2u", "ou")):
        for j in range(4):
            getattr(r, "v_" + key)[:, :, W * j : W * (j + 1)] = r.b_r[:, j, :, W * k : W * (k + 1)].astype(F32)
        store(key)
    loads[4].wait()
    widen(r.v_qd, r.b_p[...])
    store("qd")
    for cp in stores:
        cp.wait()


def make_shards(groups):
    def shards(
        tokens, lengths, adapter_ids, qkv_weight, qkv_down, qkv_up, out_weight, out_down, out_up,
        fc1_weight, fc1_down, fc1_up, fc2_weight, fc2_down, fc2_up, cotangent,
    ):
        n, S, D = tokens.shape
        A, _, R = qkv_down.shape
        T = A * R
        W = out_weight.shape[0]
        FQ = fc1_weight.shape[1]
        m0 = 2 * FQ
        l0 = m0 + 3 * W
        total = l0 + 4 * W + D
        blocks = (
            (0, FQ, 2), (FQ, m0, 3), (m0, m0 + W, 2), (m0 + W, m0 + 2 * W, 3), (m0 + 2 * W, l0, 1),
            (l0, l0 + 3 * W, 0), (l0 + 3 * W, l0 + 4 * W, 1), (l0 + 4 * W, total, 0),
        )
        sizes = dict(n_img=n, S=S, D=D, R=R, T=T, W=W, FQ=FQ, starts=(m0, l0, total), blocks=blocks)

        def turned(a):
            return jnp.transpose(a, (0, 2, 1)).reshape(T, a.shape[1])

        args = dict(
            len=lengths, ids=adapter_ids, tokens=tokens, cot=cotangent,
            hq=jnp.transpose(qkv_weight, (1, 0, 2)), ho=out_weight, h1=fc1_weight, h2=fc2_weight,
            h_aqd=turned(qkv_down), h_aqu=jnp.transpose(qkv_up, (0, 2, 1, 3)), h_aod=turned(out_down),
            h_a1u=fc1_up.reshape(T, FQ), h_a2d=turned(fc2_down), h_aou=out_up.reshape(T, D),
            h_a1d=turned(fc1_down), h_a2u=fc2_up.reshape(T, D),
        )
        outs = dict(outr=(n, S, W), ginr=(n, S, W), fin_s=(GROUP, R, 2 * FQ + 4 * W), fin_r=(GROUP, 4, R, 3 * W), fin_p=(GROUP, R, D))
        heads = W // HD
        vm = dict(
            wq=((4, D, 3 * W), BF), wo=((4, W, D), BF), w1=((4, D, FQ), BF), w2=((4, FQ, D), BF),
            aqd=((T, D), BF), aqu=((A, 3, R, W), BF), aod=((T, W), BF), a1u=((T, FQ), BF), a2d=((T, FQ), BF),
            aou=((T, D), BF), a1d=((T, D), BF), a2u=((T, D), BF),
            out_qu=((n, R, 3 * W), BF), out_od=((n, R, W), BF), out_f1=((n, R, FQ), BF), out_f2=((n, R, FQ), BF),
            sel_qu=((R, 12 * W), BF), sel_od=((R, 4 * W), BF), sel_f1=((R, 4 * FQ), BF), sel_f2=((R, 4 * FQ), BF),
            dn_qkv=((R, D), BF), up_out=((R, D), BF), dn_fc1=((R, D), BF), up_fc2=((R, D), BF),
            x=((S, D), BF), dzq=((4, S, W), BF), dz=((S, D), BF),
            first=((S, D), BF), lift_qkv=((S, R), BF), g_fc2=((S, R), BF), proj=((4, S, 3 * W), BF), qm=((4, heads * S, W), BF),
            st=((S, heads * S), F32), ds=((S, heads * S), BF), soft=((4, S, heads * S), F32), att=((S, 4 * W), BF),
            branch=((S, D), F32), lift_out=((S, R), BF), mixed=((S, D), F32), second=((S, D), BF), lift_fc1=((S, R), BF),
            outacc=((S, D), F32), gsec=((S, D), F32), lift_fc2_acc=((S, R), F32), glf1_acc=((S, R), F32),
            lift_fc2=((S, R), BF), gbr=((S, D), BF), g_out=((S, R), BF), gm=((heads * S, W), BF), gp=((S, 12 * W), BF),
            g_qkv=((S, R), BF),
            g_f1=((R, 4 * FQ), BF), g_f2=((R, 4 * FQ), BF), g_f1d=((R, D), BF), g_f2u=((R, D), BF), g_ou=((R, D), BF),
            g_qu=((R, 12 * W), BF), g_od=((R, 4 * W), BF), g_qd=((R, D), BF),
            sp=((n, R, total), BF), dense=((T, total), BF), rsb=((GROUP, R, total), BF), red=((R, total), BF),
            zb=((4, R, 3 * W), BF),
        )
        units = 18
        sems = dict(rz=units, rx=units, ry=units, rd=units, rs=units, sends=None, loc=28, misc=76)
        names = list(args) + list(outs) + list(vm) + list(sems)
        anywhere = pl.BlockSpec(memory_space=pl.ANY)
        got = pl.pallas_call(
            lambda *refs: kernel(names, sizes, *refs),
            out_shape=tuple(jax.ShapeDtypeStruct(s, BF) for s in outs.values()),
            in_specs=[pl.BlockSpec(memory_space=pltpu.SMEM)] * 2 + [anywhere] * (len(args) - 2),
            out_specs=tuple([anywhere] * len(outs)),
            scratch_shapes=[pltpu.VMEM(s, t) for s, t in vm.values()]
            + [pltpu.SemaphoreType.DMA if k is None else pltpu.SemaphoreType.DMA((k,)) for k in sems.values()],
            compiler_params=pltpu.CompilerParams(collective_id=0, has_side_effects=True, vmem_limit_bytes=60 * 2**20),
        )(*args.values())
        outr, ginr, fin_s, fin_r, fin_p = got
        if groups > 1:
            across = [[m + GROUP * g for g in range(groups)] for m in range(GROUP)]
            fin_s, fin_r, fin_p = lax.psum(tuple(v.astype(F32) for v in (fin_s, fin_r, fin_p)), "dp", axis_index_groups=across)
        full = (A, R, D)
        wide = dict(
            out=(n, S, W), gin=(n, S, W), qd=full, qu=(A, 3, R, W), od=(A, R, W), ou=full, f1d=full, f1u=(A, R, FQ), f2d=(A, R, FQ), f2u=full
        )
        held = dict(b_out=outr, b_gin=ginr, b_s=fin_s, b_r=fin_r, b_p=fin_p)
        names = ["outr", "ginr", "fin_s", "fin_r", "fin_p"] + ["o_" + k for k in wide] + list(held) + ["v_" + k for k in wide] + ["sem_in", "sem_out"]
        output, input_grad, qd, qu, od, ou, f1d, f1u, f2d, f2u = pl.pallas_call(
            lambda *refs: spread(names, *refs),
            out_shape=tuple(jax.ShapeDtypeStruct(v, F32) for v in wide.values()),
            in_specs=[anywhere] * 5,
            out_specs=tuple([anywhere] * len(wide)),
            scratch_shapes=[pltpu.VMEM(v.shape, v.dtype) for v in held.values()]
            + [pltpu.VMEM(v, F32) for v in wide.values()]
            + [pltpu.SemaphoreType.DMA((5,)), pltpu.SemaphoreType.DMA((len(wide),))],
            compiler_params=pltpu.CompilerParams(vmem_limit_bytes=60 * 2**20),
        )(outr, ginr, fin_s, fin_r, fin_p)
        back = lambda a: jnp.transpose(a, (0, 2, 1))
        return (output, input_grad, back(qd), jnp.transpose(qu, (0, 2, 1, 3)), back(od), ou, back(f1d), f1u, back(f2d), f2u)

    return shards


def solution(mesh):
    in_specs = (
        P("dp", None, None), P("dp"), P("dp", None), P(None, None, "tensor"), P(), P(None, None, None, "tensor"),
        P("tensor", None), P(None, "tensor", None), P(), P(None, "tensor"), P(), P(None, None, "tensor"),
        P("tensor", None), P(None, "tensor", None), P(), P("dp", None, "tensor"),
    )
    out_specs = (
        P("dp", None, "tensor"), P("dp", None, "tensor"), P(), P(None, None, None, "tensor"), P(None, "tensor", None),
        P(), P(), P(None, None, "tensor"), P(None, "tensor", None), P(),
    )
    shards = make_shards(mesh.shape["dp"] // GROUP)
    return jax.shard_map(shards, mesh=mesh, in_specs=in_specs, out_specs=out_specs, check_vma=False)
```

```python
import jax
import jax.numpy as jnp
from jax import lax
from jax.experimental import pallas as pl
from jax.experimental.pallas import tpu as pltpu
from jax.sharding import PartitionSpec as P


BF = jnp.bfloat16
F32 = jnp.float32
MESH = pl.DeviceIdType.MESH
EPSILON = 1e-6
NEG_FILL = -1e30
HD = 64
GROUP = 8
BLOCK = 160
SMALL = 32
STEP = 512


def dot(a, b):
    return lax.dot_general(a, b, (((1,), (0,)), ((), ())), preferred_element_type=F32)


def dot_nt(a, b):
    return lax.dot_general(a, b, (((1,), (1,)), ((), ())), preferred_element_type=F32)


def dot_tn(a, b):
    return lax.dot_general(a, b, (((0,), (0,)), ((), ())), preferred_element_type=F32)


def rows_loop(count, body, block=BLOCK):
    @pl.loop(0, count // block)
    def _(i):
        body(pl.ds(pl.multiple_of(i * block, block), block))


def moments(values):
    centred = values - jnp.mean(values, axis=-1, keepdims=True)
    inverse = lax.rsqrt(jnp.mean(centred * centred, axis=-1, keepdims=True) + EPSILON)
    return centred, inverse


def norm_back(values, grad):
    centred, inverse = moments(values)
    hat = centred * inverse
    return inverse * (
        grad - jnp.mean(grad, axis=-1, keepdims=True) - hat * jnp.mean(grad * hat, axis=-1, keepdims=True)
    )


class Bag:
    pass


def prep(r):
    def body(rows):
        centred, inverse = moments(r.x[rows, :].astype(F32))
        r.first[rows, :] = (centred * inverse).astype(BF)

    rows_loop(r.S, body)


def prep_dz(r):
    def body(rows):
        keep = (lax.broadcasted_iota(jnp.int32, (BLOCK, 1), 0) + rows.start) < r.length
        for j in range(4):
            v = r.dzq[j, rows, :]
            r.dz[rows, r.W * j : r.W * (j + 1)] = jnp.where(keep, v, jnp.zeros_like(v))

    rows_loop(r.S, body)
    r.g_fc2[...] = dot_nt(r.dz[...], r.up_fc2[...]).astype(BF)


def by_head(r, v, ref):
    head = lax.broadcasted_iota(jnp.int32, (r.S, r.W), 1) // HD
    for h in range(r.W // HD):
        ref[h * r.S : (h + 1) * r.S, :] = jnp.where(head == h, v, jnp.zeros_like(v))


def own_lanes(r, t):
    head = lax.broadcasted_iota(jnp.int32, (r.S, r.W), 1) // HD
    out = t[: r.S]
    for h in range(1, r.W // HD):
        out = jnp.where(head == h, t[h * r.S : (h + 1) * r.S], out)
    return out


def block_of(q, width):
    return pl.ds(pl.multiple_of(q * width, width), width)


def attn_fwd(r, q):
    S, W = r.S, r.W
    p = dot(r.first[...], r.wq[q]) + dot(r.lift_qkv[...], r.sel_qu[:, block_of(q, 3 * W)])
    r.proj[q] = p.astype(BF)
    by_head(r, r.proj[q, :, 0:W], r.qm.at[q])
    r.st[...] = dot_nt(r.proj[q, :, W : 2 * W], r.qm[q])
    valid = lax.broadcasted_iota(jnp.int32, (S, 128), 0) < r.length

    for k in range(r.st.shape[1] // 128):
        c = slice(k * 128, (k + 1) * 128)
        v = jnp.where(valid, r.st[:, c] * (HD**-0.5), NEG_FILL)
        e = jnp.exp(v - jnp.max(v, axis=0, keepdims=True))
        soft = e * (1.0 / jnp.sum(e, axis=0, keepdims=True))
        r.soft[q, :, c] = soft
        r.ds[:, c] = soft.astype(BF)

    att = own_lanes(r, dot_tn(r.ds[...], r.proj[q, :, 2 * W : 3 * W])).astype(BF)
    r.att[:, block_of(q, W)] = att
    r.branch[...] += dot(att, r.wo[q])


def after_attn(r):
    r.lift_out[...] = dot_nt(r.att[...], r.sel_od[...]).astype(BF)
    r.branch[...] += dot(r.lift_out[...], r.up_out[...])

    def body(rows):
        mixed = r.x[rows, :].astype(F32) + r.branch[rows, :]
        r.mixed[rows, :] = mixed
        centred, inverse = moments(mixed)
        r.second[rows, :] = (centred * inverse).astype(BF)

    rows_loop(r.S, body)
    r.lift_fc1[...] = dot_nt(r.second[...], r.dn_fc1[...]).astype(BF)
    r.outacc[...] = jnp.zeros_like(r.outacc)
    r.gsec[...] = jnp.zeros_like(r.gsec)
    r.lift_fc2_acc[...] = jnp.zeros_like(r.lift_fc2_acc)
    r.glf1_acc[...] = jnp.zeros_like(r.glf1_acc)


def ffn_unit(r, q, u):
    FQ = r.FQ
    cols = block_of(u, STEP)
    wide = pl.ds(pl.multiple_of(q * FQ + u * STEP, STEP), STEP)
    up1 = r.sel_f1[:, wide]
    dn2 = r.sel_f2[:, wide]
    r.before[...] = dot(r.second[...], r.w1[q, :, cols]) + dot(r.lift_fc1[...], up1)
    r.gh[...] = dot_nt(r.dz[...], r.w2[q, cols, :]) + dot(r.g_fc2[...], dn2)

    def body(rows):
        b = r.before[rows, :]
        cdf = 0.5 * (1.0 + lax.erf(b * (0.5**0.5)))
        r.hidden[rows, :] = (b * cdf).astype(BF)
        slope = cdf + b * jnp.exp(-0.5 * b * b) * 0.3989422804014327
        r.gb[rows, :] = (slope * r.gh[rows, :]).astype(BF)

    for k in range(r.S // SMALL):
        body(pl.ds(k * SMALL, SMALL))
    h = r.hidden[...]
    g = r.gb[...]
    r.outacc[...] += dot(h, r.w2[q, cols, :])
    r.gsec[...] += dot_nt(g, r.w1[q, :, cols])
    r.lift_fc2_acc[...] += dot_nt(h, dn2)
    r.glf1_acc[...] += dot_nt(g, up1)
    r.g_f1[:, wide] = dot_tn(r.lift_fc1[...], g).astype(BF)
    r.g_f2[:, wide] = dot_tn(r.g_fc2[...], h).astype(BF)


def after_ffn_out(r):
    r.outacc[...] += dot(r.lift_fc2[...], r.up_fc2[...])

    def body(rows):
        keep = (lax.broadcasted_iota(jnp.int32, (BLOCK, 1), 0) + rows.start) < r.length
        v = jnp.where(keep, r.mixed[rows, :] + r.outacc[rows, :], 0.0).astype(BF)
        for j in range(4):
            r.outq[j, rows, :] = v[:, r.W * j : r.W * (j + 1)]

    rows_loop(r.S, body)


def after_ffn_back(r):
    g1 = r.glf1_acc[...].astype(BF)
    r.g_f2u[...] = dot_tn(r.lift_fc2[...], r.dz[...]).astype(BF)
    r.g_f1d[...] = dot_tn(g1, r.second[...]).astype(BF)
    r.gsec[...] += dot(g1, r.dn_fc1[...])

    def body(rows):
        g = r.dz[rows, :].astype(F32) + norm_back(r.mixed[rows, :], r.gsec[rows, :])
        r.gsec[rows, :] = g
        r.gbr[rows, :] = g.astype(BF)

    rows_loop(r.S, body)
    gbr = r.gbr[...]
    r.g_ou[...] = dot_tn(r.lift_out[...], gbr).astype(BF)
    r.g_out[...] = dot_nt(gbr, r.up_out[...]).astype(BF)


def back_attended(r):
    W = r.W
    r.ga[...] = dot(r.g_out[...], r.sel_od[...])
    for q in range(4):
        c = slice(q * W, (q + 1) * W)
        r.ga[:, c] += dot_nt(r.gbr[...], r.wo[q])
    r.g_od[...] = dot_tn(r.g_out[...], r.att[...]).astype(BF)


def attn_back(r, q):
    W = r.W
    sc = HD**-0.5
    by_head(r, r.ga[:, block_of(q, W)].astype(BF), r.gm)
    k = r.proj[q, :, W : 2 * W]
    r.st[...] = dot_nt(r.proj[q, :, 2 * W : 3 * W], r.gm[...])
    gv = dot(r.soft[q].astype(BF), r.gm[...])

    for i in range(r.st.shape[1] // 128):
        c = slice(i * 128, (i + 1) * 128)
        soft, gs = r.soft[q, :, c], r.st[:, c]
        r.ds[:, c] = (soft * (gs - jnp.sum(soft * gs, axis=0, keepdims=True))).astype(BF)

    ds = r.ds[...]
    base = pl.multiple_of(3 * W * q, 128)
    r.gp[:, pl.ds(base, W)] = (own_lanes(r, dot_tn(ds, k)) * sc).astype(BF)
    r.gp[:, pl.ds(base + W, W)] = (dot(ds, r.qm[q]) * sc).astype(BF)
    r.gp[:, pl.ds(base + 2 * W, W)] = gv.astype(BF)
    wide = block_of(q, 3 * W)
    r.g_qu[:, wide] = dot_tn(r.lift_qkv[...], r.gp[:, wide]).astype(BF)


def finish_grads(r):
    gq = dot_nt(r.gp[...], r.sel_qu[...]).astype(BF)
    r.g_qd[...] = dot_tn(gq, r.first[...]).astype(BF)
    r.g_qkv[...] = gq


def back_first(r):
    W = r.W
    r.mixed[...] = dot(r.g_qkv[...], r.dn_qkv[...])
    for q in range(4):
        r.mixed[...] += dot_nt(r.gp[:, 3 * W * q : 3 * W * (q + 1)], r.wq[q])


def finish_rows(r, k):
    rows = slice(k * (r.S // 2), (k + 1) * (r.S // 2))
    r.gin[rows, :] = (r.gsec[rows, :] + norm_back(r.x[rows, :].astype(F32), r.mixed[rows, :])).astype(BF)


class Stream:
    def __init__(self, r):
        self.r = r
        d = self.d = lax.axis_index("dp")
        self.z = lax.axis_index("tensor")
        m = self.m = d % GROUP
        self.base = d - m
        self.dx = d + 2 - 4 * ((m // 2) % 2)
        self.dy = d + 4 - 8 * (m // 4)
        self.ds = d + 1 - 2 * (m % 2)
        self.dd = self.dx + self.dy - d
        self.inner = (self.z + 1) // 2 == 1
        self.n_a, self.n = 6, 18

    def quarter(self, i):
        return (self.z + jnp.where(self.z < 2, i, 4 - i)) % 4

    def unit(self, t, f):
        pl.when(t < self.n_a)(lambda: f("A", t % 2, t // 2 + 1))
        pl.when((t >= self.n_a) & (t < self.n - 4))(lambda: f("B", (t - self.n_a) % 4, (t - self.n_a) // 4 + 1))
        last = t - (self.n - 4)
        pl.when((last >= 0) & (last % 2 == 0))(lambda: f("X", last, 3))
        pl.when((last >= 0) & (last % 2 == 1))(lambda: f("Y", last, 3))

    def pair(self, kind):
        return (self.dy, self.dx) if kind == "X" else (self.dx, self.dy)

    def greet(self):
        bar = pltpu.get_barrier_semaphore()
        for k in range(1, GROUP):
            peer = self.base + (self.m + k) % GROUP
            pl.semaphore_signal(bar, inc=1, device_id=(peer, self.z), device_id_type=MESH)
        for k in range(1, 4):
            pl.semaphore_signal(bar, inc=1, device_id=(self.d, (self.z + k) % 4), device_id_type=MESH)

    def met(self):
        pl.semaphore_wait(pltpu.get_barrier_semaphore(), GROUP + 2)

    def parts(self, kind, p, q, d, half=None):
        r, m = self.r, d - self.base
        first, c = (0, pl.ds(0, r.D)) if half is None else (half, pl.ds(r.D // 2 * half, r.D // 2))
        if kind == "A":
            n = r.D // GROUP // 2
            k = r.W // GROUP // 2
            part = n if half is None else n // 2
            a = pl.ds(pl.multiple_of((2 * m + p) * n + first * part, part), part)
            b = pl.ds(pl.multiple_of((2 * m + p) * k, k), k)
            return ((r.wq.at[q, a, :]), (r.wo.at[q, b, c]))
        n = r.D // GROUP
        width = r.FQ // 4
        k = width // GROUP
        part = n if half is None else n // 2
        a = pl.ds(pl.multiple_of(m * n + first * part, part), part)
        b = pl.ds(pl.multiple_of(p * width + m * k, k), k)
        return (r.w1.at[q, a, block_of(p, width)], r.w2.at[q, b, c])

    def own(self, kind, p, d=None):
        r, z = self.r, self.z
        d = self.d if d is None else d
        m = d - self.base
        first, second = self.parts(kind, p, z, d)
        if kind == "A":
            n = r.D // GROUP // 2
            k = r.W // GROUP // 2
            a = pl.ds(pl.multiple_of((2 * m + p) * n, n), n)
            pairs = [(r.hq.at[i, a, :], r.wq.at[z, a, pl.ds(i * r.W, r.W)]) for i in range(3)]
            return pairs + [(r.ho.at[pl.ds(pl.multiple_of((2 * m + p) * k, k), k), :], second)]
        n = r.D // GROUP
        k = r.FQ // 4 // GROUP
        a = pl.ds(pl.multiple_of(m * n, n), n)
        b = pl.ds(pl.multiple_of(p * (r.FQ // 4) + m * k, k), k)
        return [(r.h1.at[a, block_of(p, r.FQ // 4)], first), (r.h2.at[b, :], second)]

    def send(self, srcs, dsts, sem, dev):
        for s, t in zip(srcs, dsts):
            pltpu.make_async_remote_copy(
                src_ref=s, dst_ref=t, send_sem=self.r.sends, recv_sem=sem, device_id=dev, device_id_type=MESH
            ).start()

    def wait(self, rows, sem):
        v = self.r.w2.at[0, pl.ds(0, rows), :]
        pltpu.make_async_copy(v, v, sem).wait()

    def index(self, kind, p, i):
        return (i - 1) * 2 + p if kind == "A" else 6 + (i - 1) * 4 + p

    def inner_sends(self, kind, p):
        z, d = self.z, self.d

        @pl.when(self.inner)
        def _():
            src, dst = zip(*self.own(kind, p))
            for to in (3 * (z - 1), 3 - z):
                self.send(src, dst, self.r.rz.at[self.index(kind, p, 1)], (d, to))

    def outer_sends(self, kind, p, i):
        z, d = self.z, self.d

        @pl.when(z % 3 == 0)
        def _():
            src, dst = zip(*self.own(kind, p))
            to = 2 - z // 3 if i == 2 else 1 + z // 3
            sem = self.r.rz.at[self.index(kind, p, i)]
            self.send(src, dst, sem, (d, to))
            if kind == "B" and i == 3:
                for n, wide in ((0, "X"), (1, "Y")):

                    @pl.when(p % 2 == n)
                    def _():
                        src, dst = zip(*self.own("B", p, self.pair(wide)[0]))
                        self.send(src, dst, sem, (d, to))

    def z_stage(self, t):
        def forward(kind, p, i):
            self.wait(128 if kind in "XY" else 64, self.r.rz.at[t])
            if kind in "AB":

                @pl.when(self.inner & (i < 3))
                def _():
                    piece = self.parts(kind, p, self.quarter(i), self.d)
                    self.send(piece, piece, self.r.rz.at[self.index(kind, p, i + 1)], (self.d, 3 * (self.z - 1)))

        self.unit(t, forward)

    def xy_sends(self, t):
        def go(kind, p, i):
            z, r, q = self.z, self.r, self.quarter(i)
            if kind in "AB":
                carried, targets = (self.d,), ((r.rx, self.dx), (r.ry, self.dy))
            else:
                beside, across = self.pair(kind)
                carried, targets = (self.d, beside), (((r.rx if kind == "X" else r.ry), across),)
            for frm in carried:
                piece = self.parts(kind, p, q, frm)
                for sem, to in targets + ((r.rs, self.ds),):
                    self.send(piece, piece, sem.at[t], (to, z))

        self.unit(t, go)

    def xy_stage(self, t):
        def go(kind, p, i):
            z, q, r = self.z, self.quarter(i), self.r
            if kind in "XY":
                self.wait(128, (r.rx if kind == "X" else r.ry).at[t])
                for frm in (self.pair(kind)[1], self.dd):
                    w = self.parts(kind, p, q, frm)
                    self.send(w, w, r.rs.at[t], (self.ds, z))
                return
            for sem, frm, to, half in ((r.rx, self.dx, self.dy, 0), (r.ry, self.dy, self.dx, 1)):
                self.wait(64, sem.at[t])
                h = self.parts(kind, p, q, frm, half)
                self.send(h, h, r.rd.at[t], (to, z))
                w = self.parts(kind, p, q, frm)
                self.send(w, w, r.rs.at[t], (self.ds, z))
                if kind == "B":
                    n = 0 if to is self.dx else 1

                    @pl.when(self.inner & (i == 2) & (p % 2 == n))
                    def _():
                        self.send(w, w, r.rz.at[self.index("B", p, 3)], (self.d, 3 * (z - 1)))

        self.unit(t, go)

    def d_stage(self, t):
        def go(kind, p, i):
            if kind in "AB":
                self.wait(64, self.r.rd.at[t])
                w = self.parts(kind, p, self.quarter(i), self.dd)
                self.send(w, w, self.r.rs.at[t], (self.ds, self.z))

        self.unit(t, go)

    def s_stage(self, t):
        self.wait(256, self.r.rs.at[t])

    def finish_sends(self):
        kinds = 6
        always = 7 * self.n - 4 + 2 * kinds + 4

        @pl.loop(0, jnp.where(self.inner, always + 2 * kinds, always))
        def _(i):
            self.wait(64, self.r.sends)


    def to_planes(self, view, target, send_sem, recv_sem):
        for k in range(1, 4):
            j = (self.z + k) % 4
            pltpu.make_async_remote_copy(
                src_ref=view(j), dst_ref=target, send_sem=send_sem, recv_sem=recv_sem, device_id=(self.d, j), device_id_type=MESH
            ).start()

    def to_group(self, view, target, send_sem, recv_sem):
        for k in range(1, GROUP):
            m = (self.m + k) % GROUP
            pltpu.make_async_remote_copy(
                src_ref=view(m), dst_ref=target, send_sem=send_sem, recv_sem=recv_sem, device_id=(self.base + m, self.z), device_id_type=MESH
            ).start()

    def share(self, src, dst, sems):
        place = dst(self.m)
        for to in (self.dx, self.dy, self.dd):
            pltpu.make_async_remote_copy(
                src_ref=src, dst_ref=place, send_sem=sems[0], recv_sem=sems[1], device_id=(to, self.z), device_id_type=MESH
            ).start()
        pltpu.make_async_remote_copy(
            src_ref=src, dst_ref=place, send_sem=sems[2], recv_sem=sems[3], device_id=(self.ds, self.z), device_id_type=MESH
        ).start()

    def pass_on(self, three, dst, sems):
        self.done(three, sems[1])
        for frm in (self.dx, self.dy, self.dd):
            place = dst(frm - self.base)
            pltpu.make_async_remote_copy(
                src_ref=place, dst_ref=place, send_sem=sems[2], recv_sem=sems[3], device_id=(self.ds, self.z), device_id_type=MESH
            ).start()

    def done(self, ref, *sems):
        for s in sems:
            pltpu.make_async_copy(ref, ref, s).wait()


class Sems:
    def __init__(self, ref, first):
        self.ref, self.first = ref, first

    def __getitem__(self, k):
        if isinstance(k, slice):
            return [self[i] for i in range(k.start, k.stop)]
        return self.ref.at[self.first + k]


def one_hot(r, p, transposed):
    R, T, n = r.R, r.T, r.n_img
    shape = (T, n * R) if transposed else (n * R, T)
    a = lax.broadcasted_iota(jnp.int32, shape, 1 if transposed else 0)
    b = lax.broadcasted_iota(jnp.int32, shape, 0 if transposed else 1)
    owner = jnp.zeros(shape, jnp.int32)
    for i in range(n):
        owner = jnp.where(a // R == i, r.ids[i, p], owner)
    hit = (b // R == owner) & (a % R == b % R)
    return jnp.where(hit, 1.0, 0.0).astype(BF)


def choose(r, p, flat):
    shape = (r.R, r.T)
    a = lax.broadcasted_iota(jnp.int32, shape, 0)
    b = lax.broadcasted_iota(jnp.int32, shape, 1)
    hit = (b // r.R == r.my_ids[p]) & (a == b % r.R)
    return dot(jnp.where(hit, 1.0, 0.0).astype(BF), flat).astype(BF)


def kernel(names, sizes, *refs):
    r = Bag()
    for n, f in zip(names, refs):
        setattr(r, n, f)
    for n, v in sizes.items():
        setattr(r, n, v)
    c = Stream(r)
    z, d = c.z, c.d
    S, W, FQ, R, n = r.S, r.W, r.FQ, r.R, r.n_img
    r.before, r.gh = r.st.at[:, pl.ds(0, STEP)], r.st.at[:, pl.ds(STEP, STEP)]
    r.hidden, r.gb = r.ds.at[:, pl.ds(0, STEP)], r.ds.at[:, pl.ds(STEP, STEP)]
    r.ga = r.branch
    r.outq, r.gin = r.dzq, r.first
    for k, name in enumerate(("aqd", "aou", "a1d", "a2u")):
        setattr(r, name, r.dense.at[:, pl.ds(k * r.D, r.D)])
    r.length = r.len[z]
    r.my_ids = [r.ids[z, p] for p in range(4)]
    c.greet()
    load = []

    def fetch(ends):
        slot = len(load)
        copy = lambda: pltpu.make_async_copy(*ends(), r.loc.at[slot])
        copy().start()
        load.append(copy)
        return copy

    l_x = fetch(lambda: (r.tokens.at[z], r.x))
    l_ad = {k: fetch(lambda k=k: (getattr(r, "h_" + k), getattr(r, k))) for k in ("aqd", "aqu", "aod", "a1u", "a2d", "aou", "a1d", "a2u")}
    l_q = [fetch(lambda i=i: (r.hq.at[i], r.wq.at[z, :, pl.ds(i * W, W)])) for i in range(3)]
    l_q.append(fetch(lambda: (r.ho, r.wo.at[z])))
    l_f = [fetch(lambda: (r.h1, r.w1.at[z])), fetch(lambda: (r.h2, r.w2.at[z]))]
    l_c = fetch(lambda: (r.cot.at[z], r.dzq.at[z]))
    c.met()

    def wait_all(copies):
        for copy in copies:
            copy().wait()

    def pick_attn():
        wait_all([l_ad["aqu"], l_ad["aod"]])
        hot = one_hot(r, 0, False)
        for i in range(3):
            r.out_qu[:, :, i * W : (i + 1) * W] = dot(hot, r.aqu[:, i].reshape(r.T, W)).astype(BF).reshape(n, R, W)
        r.out_od[...] = dot(one_hot(r, 1, False), r.aod[...]).astype(BF).reshape(n, R, W)
        c.to_planes(lambda j: r.out_qu.at[j], r.sel_qu.at[:, block_of(z, 3 * W)], r.misc.at[0], r.misc.at[1])
        c.to_planes(lambda j: r.out_od.at[j], r.sel_od.at[:, block_of(z, W)], r.misc.at[70], r.misc.at[71])
        r.sel_qu[:, block_of(z, 3 * W)] = r.out_qu[z]
        r.sel_od[:, block_of(z, W)] = r.out_od[z]

    def have_attn():
        c.done(r.sel_qu.at[:, pl.ds(0, 9 * W)], r.misc.at[0], r.misc.at[1])
        c.done(r.sel_od.at[:, pl.ds(0, 3 * W)], r.misc.at[70], r.misc.at[71])

    def pick_ffn():
        wait_all([l_ad["a1u"], l_ad["a2d"]])
        r.out_f1[...] = dot(one_hot(r, 2, False), r.a1u[...]).astype(BF).reshape(n, R, FQ)
        r.out_f2[...] = dot(one_hot(r, 3, False), r.a2d[...]).astype(BF).reshape(n, R, FQ)
        r.sel_f1[:, block_of(z, FQ)] = r.out_f1[z]
        r.sel_f2[:, block_of(z, FQ)] = r.out_f2[z]

    def send_f1():
        c.to_planes(lambda j: r.out_f1.at[j], r.sel_f1.at[:, block_of(z, FQ)], r.misc.at[72], r.misc.at[73])

    def send_f2():
        c.to_planes(lambda j: r.out_f2.at[j], r.sel_f2.at[:, block_of(z, FQ)], r.misc.at[74], r.misc.at[75])

    def have_ffn():
        c.done(r.sel_f1.at[:, pl.ds(0, 3 * FQ)], r.misc.at[72], r.misc.at[73])
        c.done(r.sel_f2.at[:, pl.ds(0, 3 * FQ)], r.misc.at[74], r.misc.at[75])

    def pick_first():
        l_ad["aqd"]().wait()
        r.dn_qkv[...] = choose(r, 0, r.aqd[...])
        r.lift_qkv[...] = dot_nt(r.first[...], r.dn_qkv[...]).astype(BF)

    def pick_rest():
        wait_all([l_ad["aou"], l_ad["a1d"], l_ad["a2u"]])
        r.up_out[...] = choose(r, 1, r.aou[...])
        r.dn_fc1[...] = choose(r, 2, r.a1d[...])
        r.up_fc2[...] = choose(r, 3, r.a2u[...])

    CUTS = 5

    def send_cot(k):
        rows = pl.ds(k * (S // CUTS), S // CUTS)
        c.to_planes(lambda j: r.cot.at[j, rows, :], r.dzq.at[z, rows, :], r.misc.at[2], r.misc.at[3])

    def have_cot():
        c.done(r.dzq.at[pl.ds(0, 3)], r.misc.at[2], r.misc.at[3])
        l_c().wait()
        prep_dz(r)

    def ffn(n):
        i, u = n // 2, n % 2
        q = c.quarter(i)
        ffn_unit(r, q, u)

        @pl.when(i > 0)
        def _():
            wide = pl.ds(pl.multiple_of(q * FQ + u * STEP, STEP), STEP)
            for ref, base in ((r.g_f1, 0), (r.g_f2, FQ)):
                pltpu.make_async_remote_copy(
                    src_ref=ref.at[:, wide], dst_ref=r.sp.at[z, :, pl.ds(pl.multiple_of(base + u * STEP, STEP), STEP)],
                    send_sem=r.misc.at[8], recv_sem=r.misc.at[9], device_id=(d, q), device_id_type=MESH,
                ).start()

    N = c.n
    LZ, LX, LD = 1, 1, 1
    lag = LZ + LX + LD
    c.inner_sends("A", 0)
    c.inner_sends("A", 1)
    l_x().wait()
    prep(r)
    r.branch[...] = jnp.zeros_like(r.branch)
    c.z_stage(0)

    @pl.loop(0, N + lag)
    def _(t):
        pl.when(t < N)(lambda: c.xy_sends(t))
        pl.when((t >= LZ) & (t < LZ + N))(lambda: c.xy_stage(t - LZ))
        pl.when((t >= LZ + LX) & (t < LZ + LX + N))(lambda: c.d_stage(t - LZ - LX))
        pl.when(t >= lag)(lambda: c.s_stage(t - lag))
        pl.when(t + 1 < N)(lambda: c.z_stage(t + 1))
        pl.when((t >= 1) & (t < 5))(lambda: c.inner_sends("B", t - 1))

        @pl.when((t == 0) | (t == 2))
        def _():
            for p in range(2):
                pl.when(t == 0)(lambda: c.outer_sends("A", p, 2))
                pl.when(t == 2)(lambda: c.outer_sends("A", p, 3))

        pl.when((t >= 4) & (t < 8))(lambda: c.outer_sends("B", t - 4, 2))
        pl.when((t >= 9) & (t < 13))(lambda: c.outer_sends("B", t - 9, 3))
        pl.when((t >= 2) & (t < 2 + 2 * CUTS) & (t % 2 == 0))(lambda: send_cot((t - 2) // 2))
        pl.when(t == 0)(pick_first)
        pl.when(t == 1)(pick_attn)
        pl.when(t == 2)(lambda: wait_all(l_q))
        pl.when(t == 3)(pick_rest)
        pl.when(t == 4)(pick_ffn)
        pl.when(t == 9)(send_f1)
        pl.when(t == 11)(send_f2)
        pl.when(t == 1 + lag)(have_attn)
        pl.when((t == 2) | (t == 1 + lag) | (t == 3 + lag) | (t == 5 + lag))(lambda: attn_fwd(r, c.quarter((t - 1) // 2)))

        @pl.when(t == 5 + lag)
        def _():
            after_attn(r)
            wait_all(l_f)

        pl.when(t == 12)(have_cot)
        pl.when(t == 14)(have_ffn)
        pl.when((t >= 12) & (t != 19))(lambda: ffn(jnp.minimum(t - 12, 7)))

    mine = block_of(z, W)

    def group(lo, own_end, hi, s, fs, fr, out=None):
        cols, own, reps, zc = pl.ds(lo, hi - lo), pl.ds(lo, own_end - lo), pl.ds(own_end, hi - own_end), pl.ds(fr, hi - own_end)
        sem = Sems(r.misc, s)
        fin = pl.ds(fs, own_end - lo)
        fin_s = r.fin_s if out is None else out

        def send_whole(ref, col):
            c.to_planes(lambda j: ref, r.sp.at[z, :, cols], sem[0], sem[1])
            r.sp[z, :, cols] = ref[...]

        def send(sources):
            for ref, width, col in sources:
                c.to_planes(lambda j: ref.at[:, block_of(j, width)], r.sp.at[z, :, pl.ds(col, width)], sem[0], sem[1])
                r.sp[z, :, col : col + width] = ref[:, block_of(z, width)]

        def expand():
            c.done(r.sp.at[pl.ds(0, 3), :, cols], sem[0], sem[1])
            for a, b, p in r.blocks:
                if lo <= a < hi:
                    r.dense[:, a:b] = dot(one_hot(r, p, True), r.sp[:, :, a:b].reshape(n * R, b - a)).astype(BF)
            c.to_group(lambda m: r.dense.at[block_of(m, R), cols], r.rsb.at[c.m, :, cols], sem[2], sem[3])
            r.rsb[c.m, :, cols] = r.dense[block_of(c.m, R), cols]

        def reduce():
            c.done(r.rsb.at[pl.ds(0, GROUP - 1), :, cols], sem[2], sem[3])
            sums = r.rsb[0, :, cols].astype(F32)
            for k in range(1, GROUP):
                sums = sums + r.rsb[k, :, cols].astype(F32)
            r.red[:, cols] = sums.astype(BF)
            if hi > own_end:
                c.to_planes(lambda j: r.red.at[:, reps], r.zb.at[z, :, zc], sem[4], sem[5])
                r.zb[z, :, zc] = r.red[:, reps]
            if own_end > lo:
                c.share(r.red.at[:, own], lambda m: fin_s.at[m, :, fin], sem[6:10])
                fetch(lambda: (r.red.at[:, own], fin_s.at[c.m, :, fin]))

        def share():
            c.done(r.zb.at[pl.ds(0, 3), :, zc], sem[4], sem[5])
            c.share(r.zb.at[:, :, zc], lambda m: r.fin_r.at[m, :, :, zc], sem[10:14])
            fetch(lambda: (r.zb.at[:, :, zc], r.fin_r.at[c.m, :, :, zc]))

        def relay():
            if own_end > lo:
                c.pass_on(fin_s.at[pl.ds(0, 3), :, fin], lambda m: fin_s.at[m, :, fin], sem[6:10])

        def relay_rep():
            c.pass_on(r.fin_r.at[pl.ds(0, 3), :, :, zc], lambda m: r.fin_r.at[m, :, :, zc], sem[10:14])

        def close():
            if own_end > lo:
                c.done(fin_s.at[pl.ds(0, 3), :, fin], sem[6])
                c.done(fin_s.at[pl.ds(0, 4), :, fin], sem[8], sem[9])
            if hi > own_end:
                c.done(r.fin_r.at[pl.ds(0, 3), :, :, zc], sem[10])
                c.done(r.fin_r.at[pl.ds(0, 4), :, :, zc], sem[12], sem[13])

        return send if out is None else send_whole, expand, reduce, share, relay, relay_rep, close

    m0, l0, end = r.starts
    _, e_expand, e_reduce, _, e_relay, _, e_close = group(0, m0, m0, 8, 0, 0)
    m_send, m_expand, m_reduce, m_share, _, m_relay, m_close = group(m0, m0, l0, 22, 0, 0)
    p0 = l0 + 4 * W
    l_send, l_expand, l_reduce, _, l_relay, _, l_close = group(l0, p0, p0, 36, 2 * FQ, 0)
    p_send, p_expand, p_reduce, _, p_relay, _, p_close = group(p0, end, end, 56, 0, 0, r.fin_p)

    def back(q):
        attn_back(r, q)
        for ref, width, col in ((r.g_qu, 3 * W, l0), (r.g_od, W, l0 + 3 * W)):
            src, dst = ref.at[:, block_of(q, width)], r.sp.at[z, :, pl.ds(col, width)]

            @pl.when(z != q)
            def _():
                pltpu.make_async_remote_copy(
                    src_ref=src, dst_ref=dst, send_sem=r.misc.at[36], recv_sem=r.misc.at[37], device_id=(d, q), device_id_type=MESH
                ).start()

    def send_out(k):
        rows = pl.ds(k * (S // 2), S // 2)
        c.to_planes(lambda j: r.outq.at[j, rows, :], r.outr.at[z, rows, :], r.misc.at[4], r.misc.at[5])
        fetch(lambda: (r.outq.at[z, rows, :], r.outr.at[z, rows, :]))

    r.lift_fc2[...] = r.lift_fc2_acc[...].astype(BF)
    after_ffn_out(r)
    send_out(0)
    after_ffn_back(r)
    m_send([(r.g_f1d, W, m0), (r.g_f2u, W, m0 + W), (r.g_ou, W, m0 + 2 * W)])
    send_out(1)
    for ref, base in ((r.g_f1, 0), (r.g_f2, FQ)):
        r.sp[z, :, base : base + FQ] = ref[:, block_of(z, FQ)]
    back_attended(r)
    e_expand()

    @pl.loop(0, 4)
    def _(q):
        back(q)

    e_reduce()
    m_expand()
    finish_grads(r)
    p_send(r.g_qd, p0)
    for ref, width, col in ((r.g_qu, 3 * W, l0), (r.g_od, W, l0 + 3 * W)):
        r.sp[z, :, col : col + width] = ref[:, block_of(z, width)]
    m_reduce()
    back_first(r)
    half = S // 2

    def send_gin(k):
        rows = pl.ds(k * half, half)
        c.to_planes(lambda j: r.gin.at[rows, block_of(j, W)], r.ginr.at[z, rows, :], r.misc.at[6], r.misc.at[7])
        fetch(lambda: (r.gin.at[rows, mine], r.ginr.at[z, rows, :]))

    p_expand()
    l_expand()
    finish_rows(r, 0)
    send_gin(0)
    finish_rows(r, 1)
    send_gin(1)
    e_relay()
    m_share()
    p_reduce()
    l_reduce()
    m_relay()
    l_relay()
    p_relay()
    e_close()
    m_close()
    c.done(r.outr.at[pl.ds(0, 3)], r.misc.at[4], r.misc.at[5])
    c.finish_sends()
    l_close()
    p_close()
    c.done(r.ginr.at[pl.ds(0, 3)], r.misc.at[6], r.misc.at[7])
    wait_all(load[1 + len(l_ad) + 7 :])


def spread(names, *refs):
    r = Bag()
    for n, f in zip(names, refs):
        setattr(r, n, f)
    W = r.b_out.shape[2]
    FQ = r.v_f1u.shape[2]
    loads = []
    for k, (src, dst) in enumerate(((r.outr, r.b_out), (r.ginr, r.b_gin), (r.fin_s, r.b_s), (r.fin_r, r.b_r), (r.fin_p, r.b_p))):
        loads.append(pltpu.make_async_copy(src, dst, r.sem_in.at[k]))
        loads[-1].start()
    stores = []

    def store(key):
        stores.append(pltpu.make_async_copy(getattr(r, "v_" + key), getattr(r, "o_" + key), r.sem_out.at[len(stores)]))
        stores[-1].start()

    def widen(ref, value):
        ref[...] = value.astype(F32)

    loads[0].wait()
    widen(r.v_out, r.b_out[...])
    store("out")
    loads[1].wait()
    widen(r.v_gin, r.b_gin[...])
    store("gin")
    loads[2].wait()
    widen(r.v_f1u, r.b_s[:, :, :FQ])
    store("f1u")
    widen(r.v_f2d, r.b_s[:, :, FQ : 2 * FQ])
    store("f2d")
    for i in range(3):
        r.v_qu[:, i] = r.b_s[:, :, 2 * FQ + i * W : 2 * FQ + (i + 1) * W].astype(F32)
    store("qu")
    widen(r.v_od, r.b_s[:, :, 2 * FQ + 3 * W :])
    store("od")
    loads[3].wait()
    for k, key in enumerate(("f1d", "f2u", "ou")):
        for j in range(4):
            getattr(r, "v_" + key)[:, :, W * j : W * (j + 1)] = r.b_r[:, j, :, W * k : W * (k + 1)].astype(F32)
        store(key)
    loads[4].wait()
    widen(r.v_qd, r.b_p[...])
    store("qd")
    for cp in stores:
        cp.wait()


def make_shards(groups):
    def shards(
        tokens, lengths, adapter_ids, qkv_weight, qkv_down, qkv_up, out_weight, out_down, out_up,
        fc1_weight, fc1_down, fc1_up, fc2_weight, fc2_down, fc2_up, cotangent,
    ):
        n, S, D = tokens.shape
        A, _, R = qkv_down.shape
        T = A * R
        W = out_weight.shape[0]
        FQ = fc1_weight.shape[1]
        m0 = 2 * FQ
        l0 = m0 + 3 * W
        total = l0 + 4 * W + D
        blocks = (
            (0, FQ, 2), (FQ, m0, 3), (m0, m0 + W, 2), (m0 + W, m0 + 2 * W, 3), (m0 + 2 * W, l0, 1),
            (l0, l0 + 3 * W, 0), (l0 + 3 * W, l0 + 4 * W, 1), (l0 + 4 * W, total, 0),
        )
        sizes = dict(n_img=n, S=S, D=D, R=R, T=T, W=W, FQ=FQ, starts=(m0, l0, total), blocks=blocks)

        def turned(a):
            return jnp.transpose(a, (0, 2, 1)).reshape(T, a.shape[1])

        args = dict(
            len=lengths, ids=adapter_ids, tokens=tokens, cot=cotangent,
            hq=jnp.transpose(qkv_weight, (1, 0, 2)), ho=out_weight, h1=fc1_weight, h2=fc2_weight,
            h_aqd=turned(qkv_down), h_aqu=jnp.transpose(qkv_up, (0, 2, 1, 3)), h_aod=turned(out_down),
            h_a1u=fc1_up.reshape(T, FQ), h_a2d=turned(fc2_down), h_aou=out_up.reshape(T, D),
            h_a1d=turned(fc1_down), h_a2u=fc2_up.reshape(T, D),
        )
        outs = dict(outr=(n, S, W), ginr=(n, S, W), fin_s=(GROUP, R, 2 * FQ + 4 * W), fin_r=(GROUP, 4, R, 3 * W), fin_p=(GROUP, R, D))
        heads = W // HD
        vm = dict(
            wq=((4, D, 3 * W), BF), wo=((4, W, D), BF), w1=((4, D, FQ), BF), w2=((4, FQ, D), BF),
            aqu=((A, 3, R, W), BF), aod=((T, W), BF), a1u=((T, FQ), BF), a2d=((T, FQ), BF),
            out_qu=((n, R, 3 * W), BF), out_od=((n, R, W), BF), out_f1=((n, R, FQ), BF), out_f2=((n, R, FQ), BF),
            sel_qu=((R, 12 * W), BF), sel_od=((R, 4 * W), BF), sel_f1=((R, 4 * FQ), BF), sel_f2=((R, 4 * FQ), BF),
            dn_qkv=((R, D), BF), up_out=((R, D), BF), dn_fc1=((R, D), BF), up_fc2=((R, D), BF),
            x=((S, D), BF), dzq=((4, S, W), BF), dz=((S, D), BF),
            first=((S, D), BF), lift_qkv=((S, R), BF), g_fc2=((S, R), BF), proj=((4, S, 3 * W), BF), qm=((4, heads * S, W), BF),
            st=((S, heads * S), F32), ds=((S, heads * S), BF), soft=((4, S, heads * S), F32), att=((S, 4 * W), BF),
            branch=((S, D), F32), lift_out=((S, R), BF), mixed=((S, D), F32), second=((S, D), BF), lift_fc1=((S, R), BF),
            outacc=((S, D), F32), gsec=((S, D), F32), lift_fc2_acc=((S, R), F32), glf1_acc=((S, R), F32),
            lift_fc2=((S, R), BF), gbr=((S, D), BF), g_out=((S, R), BF), gm=((heads * S, W), BF), gp=((S, 12 * W), BF),
            g_qkv=((S, R), BF),
            g_f1=((R, 4 * FQ), BF), g_f2=((R, 4 * FQ), BF), g_f1d=((R, D), BF), g_f2u=((R, D), BF), g_ou=((R, D), BF),
            g_qu=((R, 12 * W), BF), g_od=((R, 4 * W), BF), g_qd=((R, D), BF),
            sp=((n, R, total), BF), dense=((T, total), BF), rsb=((GROUP, R, total), BF), red=((R, total), BF),
            zb=((4, R, 3 * W), BF),
        )
        units = 18
        sems = dict(rz=units, rx=units, ry=units, rd=units, rs=units, sends=None, loc=28, misc=76)
        names = list(args) + list(outs) + list(vm) + list(sems)
        anywhere = pl.BlockSpec(memory_space=pl.ANY)
        got = pl.pallas_call(
            lambda *refs: kernel(names, sizes, *refs),
            out_shape=tuple(jax.ShapeDtypeStruct(s, BF) for s in outs.values()),
            in_specs=[pl.BlockSpec(memory_space=pltpu.SMEM)] * 2 + [anywhere] * (len(args) - 2),
            out_specs=tuple([anywhere] * len(outs)),
            scratch_shapes=[pltpu.VMEM(s, t) for s, t in vm.values()]
            + [pltpu.SemaphoreType.DMA if k is None else pltpu.SemaphoreType.DMA((k,)) for k in sems.values()],
            compiler_params=pltpu.CompilerParams(collective_id=0, has_side_effects=True, vmem_limit_bytes=60 * 2**20),
        )(*args.values())
        outr, ginr, fin_s, fin_r, fin_p = got
        if groups > 1:
            across = [[m + GROUP * g for g in range(groups)] for m in range(GROUP)]
            fin_s, fin_r, fin_p = lax.psum(tuple(v.astype(F32) for v in (fin_s, fin_r, fin_p)), "dp", axis_index_groups=across)
        full = (A, R, D)
        wide = dict(
            out=(n, S, W), gin=(n, S, W), qd=full, qu=(A, 3, R, W), od=(A, R, W), ou=full, f1d=full, f1u=(A, R, FQ), f2d=(A, R, FQ), f2u=full
        )
        held = dict(b_out=outr, b_gin=ginr, b_s=fin_s, b_r=fin_r, b_p=fin_p)
        names = ["outr", "ginr", "fin_s", "fin_r", "fin_p"] + ["o_" + k for k in wide] + list(held) + ["v_" + k for k in wide] + ["sem_in", "sem_out"]
        output, input_grad, qd, qu, od, ou, f1d, f1u, f2d, f2u = pl.pallas_call(
            lambda *refs: spread(names, *refs),
            out_shape=tuple(jax.ShapeDtypeStruct(v, F32) for v in wide.values()),
            in_specs=[anywhere] * 5,
            out_specs=tuple([anywhere] * len(wide)),
            scratch_shapes=[pltpu.VMEM(v.shape, v.dtype) for v in held.values()]
            + [pltpu.VMEM(v, F32) for v in wide.values()]
            + [pltpu.SemaphoreType.DMA((5,)), pltpu.SemaphoreType.DMA((len(wide),))],
            compiler_params=pltpu.CompilerParams(vmem_limit_bytes=60 * 2**20),
        )(outr, ginr, fin_s, fin_r, fin_p)
        back = lambda a: jnp.transpose(a, (0, 2, 1))
        return (output, input_grad, back(qd), jnp.transpose(qu, (0, 2, 1, 3)), back(od), ou, back(f1d), f1u, back(f2d), f2u)

    return shards


def solution(mesh):
    in_specs = (
        P("dp", None, None), P("dp"), P("dp", None), P(None, None, "tensor"), P(), P(None, None, None, "tensor"),
        P("tensor", None), P(None, "tensor", None), P(), P(None, "tensor"), P(), P(None, None, "tensor"),
        P("tensor", None), P(None, "tensor", None), P(), P("dp", None, "tensor"),
    )
    out_specs = (
        P("dp", None, "tensor"), P("dp", None, "tensor"), P(), P(None, None, None, "tensor"), P(None, "tensor", None),
        P(), P(), P(None, None, "tensor"), P(None, "tensor", None), P(),
    )
    shards = make_shards(mesh.shape["dp"] // GROUP)
    return jax.shard_map(shards, mesh=mesh, in_specs=in_specs, out_specs=out_specs, check_vma=False)
```

```python
import jax
import jax.numpy as jnp
from jax import lax
from jax.experimental import pallas as pl
from jax.experimental.pallas import tpu as pltpu
from jax.sharding import PartitionSpec as P


BF = jnp.bfloat16
F32 = jnp.float32
MESH = pl.DeviceIdType.MESH
EPSILON = 1e-6
NEG_FILL = -1e30
HD = 64
GROUP = 8
BLOCK = 160
SMALL = 32
STEP = 512


def dot(a, b):
    return lax.dot_general(a, b, (((1,), (0,)), ((), ())), preferred_element_type=F32)


def dot_nt(a, b):
    return lax.dot_general(a, b, (((1,), (1,)), ((), ())), preferred_element_type=F32)


def dot_tn(a, b):
    return lax.dot_general(a, b, (((0,), (0,)), ((), ())), preferred_element_type=F32)


def rows_loop(count, body, block=BLOCK):
    @pl.loop(0, count // block)
    def _(i):
        body(pl.ds(pl.multiple_of(i * block, block), block))


def moments(values):
    centred = values - jnp.mean(values, axis=-1, keepdims=True)
    inverse = lax.rsqrt(jnp.mean(centred * centred, axis=-1, keepdims=True) + EPSILON)
    return centred, inverse


def norm_back(values, grad):
    centred, inverse = moments(values)
    hat = centred * inverse
    return inverse * (
        grad - jnp.mean(grad, axis=-1, keepdims=True) - hat * jnp.mean(grad * hat, axis=-1, keepdims=True)
    )


class Bag:
    pass


def prep(r):
    def body(rows):
        centred, inverse = moments(r.x[rows, :].astype(F32))
        r.first[rows, :] = (centred * inverse).astype(BF)

    rows_loop(r.S, body)


def prep_dz(r):
    def body(rows):
        keep = (lax.broadcasted_iota(jnp.int32, (BLOCK, 1), 0) + rows.start) < r.length
        for j in range(4):
            v = r.dzq[j, rows, :]
            r.dz[rows, r.W * j : r.W * (j + 1)] = jnp.where(keep, v, jnp.zeros_like(v))

    rows_loop(r.S, body)
    r.g_fc2[...] = dot_nt(r.dz[...], r.up_fc2[...]).astype(BF)


def by_head(r, v, ref):
    head = lax.broadcasted_iota(jnp.int32, (r.S, r.W), 1) // HD
    for h in range(r.W // HD):
        ref[h * r.S : (h + 1) * r.S, :] = jnp.where(head == h, v, jnp.zeros_like(v))


def own_lanes(r, t):
    head = lax.broadcasted_iota(jnp.int32, (r.S, r.W), 1) // HD
    out = t[: r.S]
    for h in range(1, r.W // HD):
        out = jnp.where(head == h, t[h * r.S : (h + 1) * r.S], out)
    return out


def block_of(q, width):
    return pl.ds(pl.multiple_of(q * width, width), width)


def attn_fwd(r, q):
    S, W = r.S, r.W
    p = dot(r.first[...], r.wq[q]) + dot(r.lift_qkv[...], r.sel_qu[:, block_of(q, 3 * W)])
    r.proj[q] = p.astype(BF)
    by_head(r, r.proj[q, :, 0:W], r.qm.at[q])
    r.st[...] = dot_nt(r.proj[q, :, W : 2 * W], r.qm[q])
    valid = lax.broadcasted_iota(jnp.int32, (S, 128), 0) < r.length

    for k in range(r.st.shape[1] // 128):
        c = slice(k * 128, (k + 1) * 128)
        v = jnp.where(valid, r.st[:, c] * (HD**-0.5), NEG_FILL)
        e = jnp.exp(v - jnp.max(v, axis=0, keepdims=True))
        soft = e * (1.0 / jnp.sum(e, axis=0, keepdims=True))
        r.soft[q, :, c] = soft
        r.ds[:, c] = soft.astype(BF)

    att = own_lanes(r, dot_tn(r.ds[...], r.proj[q, :, 2 * W : 3 * W])).astype(BF)
    r.att[:, block_of(q, W)] = att
    r.branch[...] += dot(att, r.wo[q])


def after_attn(r):
    r.lift_out[...] = dot_nt(r.att[...], r.sel_od[...]).astype(BF)
    r.branch[...] += dot(r.lift_out[...], r.up_out[...])

    def body(rows):
        mixed = r.x[rows, :].astype(F32) + r.branch[rows, :]
        r.mixed[rows, :] = mixed
        centred, inverse = moments(mixed)
        r.second[rows, :] = (centred * inverse).astype(BF)

    rows_loop(r.S, body)
    r.lift_fc1[...] = dot_nt(r.second[...], r.dn_fc1[...]).astype(BF)
    r.outacc[...] = jnp.zeros_like(r.outacc)
    r.gsec[...] = jnp.zeros_like(r.gsec)
    r.lift_fc2_acc[...] = jnp.zeros_like(r.lift_fc2_acc)
    r.glf1_acc[...] = jnp.zeros_like(r.glf1_acc)


def ffn_unit(r, q, u):
    FQ = r.FQ
    cols = block_of(u, STEP)
    wide = pl.ds(pl.multiple_of(q * FQ + u * STEP, STEP), STEP)
    up1 = r.sel_f1[:, wide]
    dn2 = r.sel_f2[:, wide]
    r.before[...] = dot(r.second[...], r.w1[q, :, cols]) + dot(r.lift_fc1[...], up1)
    r.gh[...] = dot_nt(r.dz[...], r.w2[q, cols, :]) + dot(r.g_fc2[...], dn2)

    def body(rows):
        b = r.before[rows, :]
        cdf = 0.5 * (1.0 + lax.erf(b * (0.5**0.5)))
        r.hidden[rows, :] = (b * cdf).astype(BF)
        slope = cdf + b * jnp.exp(-0.5 * b * b) * 0.3989422804014327
        r.gb[rows, :] = (slope * r.gh[rows, :]).astype(BF)

    for k in range(r.S // SMALL):
        body(pl.ds(k * SMALL, SMALL))
    h = r.hidden[...]
    g = r.gb[...]
    r.outacc[...] += dot(h, r.w2[q, cols, :])
    r.gsec[...] += dot_nt(g, r.w1[q, :, cols])
    r.lift_fc2_acc[...] += dot_nt(h, dn2)
    r.glf1_acc[...] += dot_nt(g, up1)
    r.g_f1[:, wide] = dot_tn(r.lift_fc1[...], g).astype(BF)
    r.g_f2[:, wide] = dot_tn(r.g_fc2[...], h).astype(BF)


def after_ffn_out(r):
    r.outacc[...] += dot(r.lift_fc2[...], r.up_fc2[...])

    def body(rows):
        keep = (lax.broadcasted_iota(jnp.int32, (BLOCK, 1), 0) + rows.start) < r.length
        v = jnp.where(keep, r.mixed[rows, :] + r.outacc[rows, :], 0.0).astype(BF)
        for j in range(4):
            r.outq[j, rows, :] = v[:, r.W * j : r.W * (j + 1)]

    rows_loop(r.S, body)


def after_ffn_back(r):
    g1 = r.glf1_acc[...].astype(BF)
    r.g_f2u[...] = dot_tn(r.lift_fc2[...], r.dz[...]).astype(BF)
    r.g_f1d[...] = dot_tn(g1, r.second[...]).astype(BF)
    r.gsec[...] += dot(g1, r.dn_fc1[...])

    def body(rows):
        g = r.dz[rows, :].astype(F32) + norm_back(r.mixed[rows, :], r.gsec[rows, :])
        r.gsec[rows, :] = g
        r.gbr[rows, :] = g.astype(BF)

    rows_loop(r.S, body)
    gbr = r.gbr[...]
    r.g_ou[...] = dot_tn(r.lift_out[...], gbr).astype(BF)
    r.g_out[...] = dot_nt(gbr, r.up_out[...]).astype(BF)


def back_attended(r):
    W = r.W
    r.ga[...] = dot(r.g_out[...], r.sel_od[...])
    for q in range(4):
        c = slice(q * W, (q + 1) * W)
        r.ga[:, c] += dot_nt(r.gbr[...], r.wo[q])
    r.g_od[...] = dot_tn(r.g_out[...], r.att[...]).astype(BF)


def attn_back(r, q):
    W = r.W
    sc = HD**-0.5
    by_head(r, r.ga[:, block_of(q, W)].astype(BF), r.gm)
    k = r.proj[q, :, W : 2 * W]
    r.st[...] = dot_nt(r.proj[q, :, 2 * W : 3 * W], r.gm[...])
    gv = dot(r.soft[q].astype(BF), r.gm[...])

    for i in range(r.st.shape[1] // 128):
        c = slice(i * 128, (i + 1) * 128)
        soft, gs = r.soft[q, :, c], r.st[:, c]
        r.ds[:, c] = (soft * (gs - jnp.sum(soft * gs, axis=0, keepdims=True))).astype(BF)

    ds = r.ds[...]
    base = pl.multiple_of(3 * W * q, 128)
    r.gp[:, pl.ds(base, W)] = (own_lanes(r, dot_tn(ds, k)) * sc).astype(BF)
    r.gp[:, pl.ds(base + W, W)] = (dot(ds, r.qm[q]) * sc).astype(BF)
    r.gp[:, pl.ds(base + 2 * W, W)] = gv.astype(BF)
    wide = block_of(q, 3 * W)
    r.g_qu[:, wide] = dot_tn(r.lift_qkv[...], r.gp[:, wide]).astype(BF)


def finish_grads(r):
    gq = dot_nt(r.gp[...], r.sel_qu[...]).astype(BF)
    r.g_qd[...] = dot_tn(gq, r.first[...]).astype(BF)
    r.g_qkv[...] = gq


def back_first(r):
    W = r.W
    r.mixed[...] = dot(r.g_qkv[...], r.dn_qkv[...])
    for q in range(4):
        r.mixed[...] += dot_nt(r.gp[:, 3 * W * q : 3 * W * (q + 1)], r.wq[q])


def finish_rows(r, k):
    rows = slice(k * (r.S // 2), (k + 1) * (r.S // 2))
    r.gin[rows, :] = (r.gsec[rows, :] + norm_back(r.x[rows, :].astype(F32), r.mixed[rows, :])).astype(BF)


class Stream:
    def __init__(self, r):
        self.r = r
        d = self.d = lax.axis_index("dp")
        self.z = lax.axis_index("tensor")
        m = self.m = d % GROUP
        self.base = d - m
        self.dx = d + 2 - 4 * ((m // 2) % 2)
        self.dy = d + 4 - 8 * (m // 4)
        self.ds = d + 1 - 2 * (m % 2)
        self.dd = self.dx + self.dy - d
        self.inner = (self.z + 1) // 2 == 1
        self.n_a, self.n = 6, 18

    def quarter(self, i):
        return (self.z + jnp.where(self.z < 2, i, 4 - i)) % 4

    def unit(self, t, f):
        pl.when(t < self.n_a)(lambda: f("A", t % 2, t // 2 + 1))
        pl.when((t >= self.n_a) & (t < self.n - 4))(lambda: f("B", (t - self.n_a) % 4, (t - self.n_a) // 4 + 1))
        last = t - (self.n - 4)
        pl.when((last >= 0) & (last % 2 == 0))(lambda: f("X", last, 3))
        pl.when((last >= 0) & (last % 2 == 1))(lambda: f("Y", last, 3))

    def pair(self, kind):
        return (self.dy, self.dx) if kind == "X" else (self.dx, self.dy)

    def greet(self):
        bar = pltpu.get_barrier_semaphore()
        for k in range(1, GROUP):
            peer = self.base + (self.m + k) % GROUP
            pl.semaphore_signal(bar, inc=1, device_id=(peer, self.z), device_id_type=MESH)
        for k in range(1, 4):
            pl.semaphore_signal(bar, inc=1, device_id=(self.d, (self.z + k) % 4), device_id_type=MESH)

    def met(self):
        pl.semaphore_wait(pltpu.get_barrier_semaphore(), GROUP + 2)

    def parts(self, kind, p, q, d, half=None):
        r, m = self.r, d - self.base
        first, c = (0, pl.ds(0, r.D)) if half is None else (half, pl.ds(r.D // 2 * half, r.D // 2))
        if kind == "A":
            n = r.D // GROUP // 2
            k = r.W // GROUP // 2
            part = n if half is None else n // 2
            a = pl.ds(pl.multiple_of((2 * m + p) * n + first * part, part), part)
            b = pl.ds(pl.multiple_of((2 * m + p) * k, k), k)
            return ((r.wq.at[q, a, :]), (r.wo.at[q, b, c]))
        n = r.D // GROUP
        width = r.FQ // 4
        k = width // GROUP
        part = n if half is None else n // 2
        a = pl.ds(pl.multiple_of(m * n + first * part, part), part)
        b = pl.ds(pl.multiple_of(p * width + m * k, k), k)
        return (r.w1.at[q, a, block_of(p, width)], r.w2.at[q, b, c])

    def own(self, kind, p, d=None):
        r, z = self.r, self.z
        d = self.d if d is None else d
        m = d - self.base
        first, second = self.parts(kind, p, z, d)
        if kind == "A":
            n = r.D // GROUP // 2
            k = r.W // GROUP // 2
            a = pl.ds(pl.multiple_of((2 * m + p) * n, n), n)
            pairs = [(r.hq.at[i, a, :], r.wq.at[z, a, pl.ds(i * r.W, r.W)]) for i in range(3)]
            return pairs + [(r.ho.at[pl.ds(pl.multiple_of((2 * m + p) * k, k), k), :], second)]
        n = r.D // GROUP
        k = r.FQ // 4 // GROUP
        a = pl.ds(pl.multiple_of(m * n, n), n)
        b = pl.ds(pl.multiple_of(p * (r.FQ // 4) + m * k, k), k)
        return [(r.h1.at[a, block_of(p, r.FQ // 4)], first), (r.h2.at[b, :], second)]

    def send(self, srcs, dsts, sem, dev):
        for s, t in zip(srcs, dsts):
            pltpu.make_async_remote_copy(
                src_ref=s, dst_ref=t, send_sem=self.r.sends, recv_sem=sem, device_id=dev, device_id_type=MESH
            ).start()

    def wait(self, rows, sem):
        v = self.r.w2.at[0, pl.ds(0, rows), :]
        pltpu.make_async_copy(v, v, sem).wait()

    def index(self, kind, p, i):
        return (i - 1) * 2 + p if kind == "A" else 6 + (i - 1) * 4 + p

    def inner_sends(self, kind, p):
        z, d = self.z, self.d

        @pl.when(self.inner)
        def _():
            src, dst = zip(*self.own(kind, p))
            for to in (3 * (z - 1), 3 - z):
                self.send(src, dst, self.r.rz.at[self.index(kind, p, 1)], (d, to))

    def outer_sends(self, kind, p, i):
        z, d = self.z, self.d

        @pl.when(z % 3 == 0)
        def _():
            src, dst = zip(*self.own(kind, p))
            to = 2 - z // 3 if i == 2 else 1 + z // 3
            sem = self.r.rz.at[self.index(kind, p, i)]
            self.send(src, dst, sem, (d, to))
            if kind == "B" and i == 3:
                for n, wide in ((0, "X"), (1, "Y")):

                    @pl.when(p % 2 == n)
                    def _():
                        src, dst = zip(*self.own("B", p, self.pair(wide)[0]))
                        self.send(src, dst, sem, (d, to))

    def z_stage(self, t):
        def forward(kind, p, i):
            self.wait(128 if kind in "XY" else 64, self.r.rz.at[t])
            if kind in "AB":

                @pl.when(self.inner & (i < 3))
                def _():
                    piece = self.parts(kind, p, self.quarter(i), self.d)
                    self.send(piece, piece, self.r.rz.at[self.index(kind, p, i + 1)], (self.d, 3 * (self.z - 1)))

        self.unit(t, forward)

    def xy_sends(self, t):
        def go(kind, p, i):
            z, r, q = self.z, self.r, self.quarter(i)
            if kind in "AB":
                carried, targets = (self.d,), ((r.rx, self.dx), (r.ry, self.dy))
            else:
                beside, across = self.pair(kind)
                carried, targets = (self.d, beside), (((r.rx if kind == "X" else r.ry), across),)
            for frm in carried:
                piece = self.parts(kind, p, q, frm)
                for sem, to in targets + ((r.rs, self.ds),):
                    self.send(piece, piece, sem.at[t], (to, z))

        self.unit(t, go)

    def xy_stage(self, t):
        def go(kind, p, i):
            z, q, r = self.z, self.quarter(i), self.r
            if kind in "XY":
                self.wait(128, (r.rx if kind == "X" else r.ry).at[t])
                for frm in (self.pair(kind)[1], self.dd):
                    w = self.parts(kind, p, q, frm)
                    self.send(w, w, r.rs.at[t], (self.ds, z))
                return
            for sem, frm, to, half in ((r.rx, self.dx, self.dy, 0), (r.ry, self.dy, self.dx, 1)):
                self.wait(64, sem.at[t])
                h = self.parts(kind, p, q, frm, half)
                self.send(h, h, r.rd.at[t], (to, z))
                w = self.parts(kind, p, q, frm)
                self.send(w, w, r.rs.at[t], (self.ds, z))
                if kind == "B":
                    n = 0 if to is self.dx else 1

                    @pl.when(self.inner & (i == 2) & (p % 2 == n))
                    def _():
                        self.send(w, w, r.rz.at[self.index("B", p, 3)], (self.d, 3 * (z - 1)))

        self.unit(t, go)

    def d_stage(self, t):
        def go(kind, p, i):
            if kind in "AB":
                self.wait(64, self.r.rd.at[t])
                w = self.parts(kind, p, self.quarter(i), self.dd)
                self.send(w, w, self.r.rs.at[t], (self.ds, self.z))

        self.unit(t, go)

    def s_stage(self, t):
        self.wait(256, self.r.rs.at[t])

    def finish_sends(self):
        kinds = 6
        always = 7 * self.n - 4 + 2 * kinds + 4

        @pl.loop(0, jnp.where(self.inner, always + 2 * kinds, always))
        def _(i):
            self.wait(64, self.r.sends)


    def to_planes(self, view, target, send_sem, recv_sem):
        for k in range(1, 4):
            j = (self.z + k) % 4
            pltpu.make_async_remote_copy(
                src_ref=view(j), dst_ref=target, send_sem=send_sem, recv_sem=recv_sem, device_id=(self.d, j), device_id_type=MESH
            ).start()

    def to_group(self, view, target, send_sem, recv_sem):
        for k in range(1, GROUP):
            m = (self.m + k) % GROUP
            pltpu.make_async_remote_copy(
                src_ref=view(m), dst_ref=target, send_sem=send_sem, recv_sem=recv_sem, device_id=(self.base + m, self.z), device_id_type=MESH
            ).start()

    def share(self, src, dst, sems):
        place = dst(self.m)
        for to in (self.dx, self.dy, self.dd):
            pltpu.make_async_remote_copy(
                src_ref=src, dst_ref=place, send_sem=sems[0], recv_sem=sems[1], device_id=(to, self.z), device_id_type=MESH
            ).start()
        pltpu.make_async_remote_copy(
            src_ref=src, dst_ref=place, send_sem=sems[2], recv_sem=sems[3], device_id=(self.ds, self.z), device_id_type=MESH
        ).start()

    def pass_on(self, three, dst, sems):
        self.done(three, sems[1])
        for frm in (self.dx, self.dy, self.dd):
            place = dst(frm - self.base)
            pltpu.make_async_remote_copy(
                src_ref=place, dst_ref=place, send_sem=sems[2], recv_sem=sems[3], device_id=(self.ds, self.z), device_id_type=MESH
            ).start()

    def done(self, ref, *sems):
        for s in sems:
            pltpu.make_async_copy(ref, ref, s).wait()


class Sems:
    def __init__(self, ref, first):
        self.ref, self.first = ref, first

    def __getitem__(self, k):
        if isinstance(k, slice):
            return [self[i] for i in range(k.start, k.stop)]
        return self.ref.at[self.first + k]


def one_hot(r, p, transposed):
    R, T, n = r.R, r.T, r.n_img
    shape = (T, n * R) if transposed else (n * R, T)
    a = lax.broadcasted_iota(jnp.int32, shape, 1 if transposed else 0)
    b = lax.broadcasted_iota(jnp.int32, shape, 0 if transposed else 1)
    owner = jnp.zeros(shape, jnp.int32)
    for i in range(n):
        owner = jnp.where(a // R == i, r.ids[i, p], owner)
    hit = (b // R == owner) & (a % R == b % R)
    return jnp.where(hit, 1.0, 0.0).astype(BF)


def choose(r, p, flat):
    shape = (r.R, r.T)
    a = lax.broadcasted_iota(jnp.int32, shape, 0)
    b = lax.broadcasted_iota(jnp.int32, shape, 1)
    hit = (b // r.R == r.my_ids[p]) & (a == b % r.R)
    return dot(jnp.where(hit, 1.0, 0.0).astype(BF), flat).astype(BF)


def kernel(names, sizes, *refs):
    r = Bag()
    for n, f in zip(names, refs):
        setattr(r, n, f)
    for n, v in sizes.items():
        setattr(r, n, v)
    c = Stream(r)
    z, d = c.z, c.d
    S, W, FQ, R, n = r.S, r.W, r.FQ, r.R, r.n_img
    r.before, r.gh = r.st.at[:, pl.ds(0, STEP)], r.st.at[:, pl.ds(STEP, STEP)]
    r.hidden, r.gb = r.ds.at[:, pl.ds(0, STEP)], r.ds.at[:, pl.ds(STEP, STEP)]
    r.ga = r.branch
    r.outq, r.gin = r.dzq, r.first
    for k, name in enumerate(("aqd", "aou", "a1d", "a2u")):
        setattr(r, name, r.dense.at[:, pl.ds(k * r.D, r.D)])
    r.length = r.len[z]
    r.my_ids = [r.ids[z, p] for p in range(4)]
    c.greet()
    load = []

    def fetch(ends):
        slot = len(load)
        copy = lambda: pltpu.make_async_copy(*ends(), r.loc.at[slot])
        copy().start()
        load.append(copy)
        return copy

    l_x = fetch(lambda: (r.tokens.at[z], r.x))
    l_ad = {k: fetch(lambda k=k: (getattr(r, "h_" + k), getattr(r, k))) for k in ("aqd", "aqu", "aod", "a1u", "a2d", "aou", "a1d", "a2u")}
    l_q = [fetch(lambda i=i: (r.hq.at[i], r.wq.at[z, :, pl.ds(i * W, W)])) for i in range(3)]
    l_q.append(fetch(lambda: (r.ho, r.wo.at[z])))
    l_f = [fetch(lambda: (r.h1, r.w1.at[z])), fetch(lambda: (r.h2, r.w2.at[z]))]
    l_c = fetch(lambda: (r.cot.at[z], r.dzq.at[z]))
    c.met()

    def wait_all(copies):
        for copy in copies:
            copy().wait()

    def pick_attn():
        wait_all([l_ad["aqu"], l_ad["aod"]])
        hot = one_hot(r, 0, False)
        for i in range(3):
            r.out_qu[:, :, i * W : (i + 1) * W] = dot(hot, r.aqu[:, i].reshape(r.T, W)).astype(BF).reshape(n, R, W)
        r.out_od[...] = dot(one_hot(r, 1, False), r.aod[...]).astype(BF).reshape(n, R, W)
        c.to_planes(lambda j: r.out_qu.at[j], r.sel_qu.at[:, block_of(z, 3 * W)], r.misc.at[0], r.misc.at[1])
        c.to_planes(lambda j: r.out_od.at[j], r.sel_od.at[:, block_of(z, W)], r.misc.at[70], r.misc.at[71])
        r.sel_qu[:, block_of(z, 3 * W)] = r.out_qu[z]
        r.sel_od[:, block_of(z, W)] = r.out_od[z]

    def have_attn():
        c.done(r.sel_qu.at[:, pl.ds(0, 9 * W)], r.misc.at[0], r.misc.at[1])
        c.done(r.sel_od.at[:, pl.ds(0, 3 * W)], r.misc.at[70], r.misc.at[71])

    def pick_ffn():
        wait_all([l_ad["a1u"], l_ad["a2d"]])
        r.out_f1[...] = dot(one_hot(r, 2, False), r.a1u[...]).astype(BF).reshape(n, R, FQ)
        r.out_f2[...] = dot(one_hot(r, 3, False), r.a2d[...]).astype(BF).reshape(n, R, FQ)
        r.sel_f1[:, block_of(z, FQ)] = r.out_f1[z]
        r.sel_f2[:, block_of(z, FQ)] = r.out_f2[z]

    def send_f1():
        c.to_planes(lambda j: r.out_f1.at[j], r.sel_f1.at[:, block_of(z, FQ)], r.misc.at[72], r.misc.at[73])

    def send_f2():
        c.to_planes(lambda j: r.out_f2.at[j], r.sel_f2.at[:, block_of(z, FQ)], r.misc.at[74], r.misc.at[75])

    def have_ffn():
        c.done(r.sel_f1.at[:, pl.ds(0, 3 * FQ)], r.misc.at[72], r.misc.at[73])
        c.done(r.sel_f2.at[:, pl.ds(0, 3 * FQ)], r.misc.at[74], r.misc.at[75])

    def pick_first():
        l_ad["aqd"]().wait()
        r.dn_qkv[...] = choose(r, 0, r.aqd[...])
        r.lift_qkv[...] = dot_nt(r.first[...], r.dn_qkv[...]).astype(BF)

    def pick_rest():
        wait_all([l_ad["aou"], l_ad["a1d"], l_ad["a2u"]])
        r.up_out[...] = choose(r, 1, r.aou[...])
        r.dn_fc1[...] = choose(r, 2, r.a1d[...])
        r.up_fc2[...] = choose(r, 3, r.a2u[...])

    CUTS = 5

    def send_cot(k):
        rows = pl.ds(k * (S // CUTS), S // CUTS)
        c.to_planes(lambda j: r.cot.at[j, rows, :], r.dzq.at[z, rows, :], r.misc.at[2], r.misc.at[3])

    def have_cot():
        c.done(r.dzq.at[pl.ds(0, 3)], r.misc.at[2], r.misc.at[3])
        l_c().wait()
        prep_dz(r)

    def ffn(n):
        i, u = n // 2, n % 2
        q = c.quarter(i)
        ffn_unit(r, q, u)

        @pl.when(i > 0)
        def _():
            wide = pl.ds(pl.multiple_of(q * FQ + u * STEP, STEP), STEP)
            for ref, base in ((r.g_f1, 0), (r.g_f2, FQ)):
                pltpu.make_async_remote_copy(
                    src_ref=ref.at[:, wide], dst_ref=r.sp.at[z, :, pl.ds(pl.multiple_of(base + u * STEP, STEP), STEP)],
                    send_sem=r.misc.at[8], recv_sem=r.misc.at[9], device_id=(d, q), device_id_type=MESH,
                ).start()

    N = c.n
    LZ, LX, LD = 1, 1, 1
    lag = LZ + LX + LD
    c.inner_sends("A", 0)
    c.inner_sends("A", 1)
    l_x().wait()
    prep(r)
    r.branch[...] = jnp.zeros_like(r.branch)
    c.z_stage(0)

    @pl.loop(0, N + lag)
    def _(t):
        pl.when(t < N)(lambda: c.xy_sends(t))
        pl.when((t >= LZ) & (t < LZ + N))(lambda: c.xy_stage(t - LZ))
        pl.when((t >= LZ + LX) & (t < LZ + LX + N))(lambda: c.d_stage(t - LZ - LX))
        pl.when(t >= lag)(lambda: c.s_stage(t - lag))
        pl.when(t + 1 < N)(lambda: c.z_stage(t + 1))
        pl.when((t >= 1) & (t < 5))(lambda: c.inner_sends("B", t - 1))

        @pl.when((t == 0) | (t == 3))
        def _():
            for p in range(2):
                pl.when(t == 0)(lambda: c.outer_sends("A", p, 2))
                pl.when(t == 3)(lambda: c.outer_sends("A", p, 3))

        pl.when((t >= 5) & (t < 9))(lambda: c.outer_sends("B", t - 5, 2))
        pl.when((t >= 10) & (t < 14))(lambda: c.outer_sends("B", t - 10, 3))
        pl.when((t >= 1) & (t < 11) & ((t - 1) % 2 == 0))(lambda: send_cot((t - 1) // 2))
        pl.when(t == 0)(pick_first)
        pl.when(t == 1)(pick_attn)
        pl.when(t == 2)(lambda: wait_all(l_q))
        pl.when(t == 3)(pick_rest)
        pl.when(t == 4)(pick_ffn)
        pl.when(t == 9)(send_f1)
        pl.when(t == 11)(send_f2)
        pl.when(t == 1 + lag)(have_attn)
        pl.when((t == 2) | (t == 1 + lag) | (t == 3 + lag) | (t == 5 + lag))(lambda: attn_fwd(r, c.quarter((t - 1) // 2)))

        @pl.when(t == 5 + lag)
        def _():
            after_attn(r)
            wait_all(l_f)

        pl.when(t == 12)(have_cot)
        pl.when(t == 14)(have_ffn)
        pl.when((t >= 12) & (t != 19))(lambda: ffn(jnp.minimum(t - 12, 7)))

    mine = block_of(z, W)

    def group(lo, own_end, hi, s, fs, fr, out=None):
        cols, own, reps, zc = pl.ds(lo, hi - lo), pl.ds(lo, own_end - lo), pl.ds(own_end, hi - own_end), pl.ds(fr, hi - own_end)
        sem = Sems(r.misc, s)
        fin = pl.ds(fs, own_end - lo)
        fin_s = r.fin_s if out is None else out

        def send_whole(ref, col):
            c.to_planes(lambda j: ref, r.sp.at[z, :, cols], sem[0], sem[1])
            r.sp[z, :, cols] = ref[...]

        def send(sources):
            for ref, width, col in sources:
                c.to_planes(lambda j: ref.at[:, block_of(j, width)], r.sp.at[z, :, pl.ds(col, width)], sem[0], sem[1])
                r.sp[z, :, col : col + width] = ref[:, block_of(z, width)]

        def expand():
            c.done(r.sp.at[pl.ds(0, 3), :, cols], sem[0], sem[1])
            for a, b, p in r.blocks:
                if lo <= a < hi:
                    r.dense[:, a:b] = dot(one_hot(r, p, True), r.sp[:, :, a:b].reshape(n * R, b - a)).astype(BF)
            c.to_group(lambda m: r.dense.at[block_of(m, R), cols], r.rsb.at[c.m, :, cols], sem[2], sem[3])
            r.rsb[c.m, :, cols] = r.dense[block_of(c.m, R), cols]

        def reduce():
            c.done(r.rsb.at[pl.ds(0, GROUP - 1), :, cols], sem[2], sem[3])
            sums = r.rsb[0, :, cols].astype(F32)
            for k in range(1, GROUP):
                sums = sums + r.rsb[k, :, cols].astype(F32)
            r.red[:, cols] = sums.astype(BF)
            if hi > own_end:
                c.to_planes(lambda j: r.red.at[:, reps], r.zb.at[z, :, zc], sem[4], sem[5])
                r.zb[z, :, zc] = r.red[:, reps]
            if own_end > lo:
                c.share(r.red.at[:, own], lambda m: fin_s.at[m, :, fin], sem[6:10])
                fetch(lambda: (r.red.at[:, own], fin_s.at[c.m, :, fin]))

        def share():
            c.done(r.zb.at[pl.ds(0, 3), :, zc], sem[4], sem[5])
            c.share(r.zb.at[:, :, zc], lambda m: r.fin_r.at[m, :, :, zc], sem[10:14])
            fetch(lambda: (r.zb.at[:, :, zc], r.fin_r.at[c.m, :, :, zc]))

        def relay():
            if own_end > lo:
                c.pass_on(fin_s.at[pl.ds(0, 3), :, fin], lambda m: fin_s.at[m, :, fin], sem[6:10])

        def relay_rep():
            c.pass_on(r.fin_r.at[pl.ds(0, 3), :, :, zc], lambda m: r.fin_r.at[m, :, :, zc], sem[10:14])

        def close():
            if own_end > lo:
                c.done(fin_s.at[pl.ds(0, 3), :, fin], sem[6])
                c.done(fin_s.at[pl.ds(0, 4), :, fin], sem[8], sem[9])
            if hi > own_end:
                c.done(r.fin_r.at[pl.ds(0, 3), :, :, zc], sem[10])
                c.done(r.fin_r.at[pl.ds(0, 4), :, :, zc], sem[12], sem[13])

        return send if out is None else send_whole, expand, reduce, share, relay, relay_rep, close

    m0, l0, end = r.starts
    _, e_expand, e_reduce, _, e_relay, _, e_close = group(0, m0, m0, 8, 0, 0)
    m_send, m_expand, m_reduce, m_share, _, m_relay, m_close = group(m0, m0, l0, 22, 0, 0)
    p0 = l0 + 4 * W
    l_send, l_expand, l_reduce, _, l_relay, _, l_close = group(l0, p0, p0, 36, 2 * FQ, 0)
    p_send, p_expand, p_reduce, _, p_relay, _, p_close = group(p0, end, end, 56, 0, 0, r.fin_p)

    def back(q):
        attn_back(r, q)
        for ref, width, col in ((r.g_qu, 3 * W, l0), (r.g_od, W, l0 + 3 * W)):
            src, dst = ref.at[:, block_of(q, width)], r.sp.at[z, :, pl.ds(col, width)]

            @pl.when(z != q)
            def _():
                pltpu.make_async_remote_copy(
                    src_ref=src, dst_ref=dst, send_sem=r.misc.at[36], recv_sem=r.misc.at[37], device_id=(d, q), device_id_type=MESH
                ).start()

    def send_out(k):
        rows = pl.ds(k * (S // 2), S // 2)
        c.to_planes(lambda j: r.outq.at[j, rows, :], r.outr.at[z, rows, :], r.misc.at[4], r.misc.at[5])
        fetch(lambda: (r.outq.at[z, rows, :], r.outr.at[z, rows, :]))

    r.lift_fc2[...] = r.lift_fc2_acc[...].astype(BF)
    after_ffn_out(r)
    send_out(0)
    after_ffn_back(r)
    m_send([(r.g_f1d, W, m0), (r.g_f2u, W, m0 + W), (r.g_ou, W, m0 + 2 * W)])
    send_out(1)
    for ref, base in ((r.g_f1, 0), (r.g_f2, FQ)):
        r.sp[z, :, base : base + FQ] = ref[:, block_of(z, FQ)]
    back_attended(r)
    e_expand()

    @pl.loop(0, 4)
    def _(q):
        back(q)

    e_reduce()
    m_expand()
    finish_grads(r)
    p_send(r.g_qd, p0)
    for ref, width, col in ((r.g_qu, 3 * W, l0), (r.g_od, W, l0 + 3 * W)):
        r.sp[z, :, col : col + width] = ref[:, block_of(z, width)]
    m_reduce()
    back_first(r)
    half = S // 2

    def send_gin(k):
        rows = pl.ds(k * half, half)
        c.to_planes(lambda j: r.gin.at[rows, block_of(j, W)], r.ginr.at[z, rows, :], r.misc.at[6], r.misc.at[7])
        fetch(lambda: (r.gin.at[rows, mine], r.ginr.at[z, rows, :]))

    finish_rows(r, 0)
    send_gin(0)
    p_expand()
    l_expand()
    finish_rows(r, 1)
    send_gin(1)
    e_relay()
    m_share()
    p_reduce()
    l_reduce()
    m_relay()
    l_relay()
    p_relay()
    e_close()
    m_close()
    c.done(r.outr.at[pl.ds(0, 3)], r.misc.at[4], r.misc.at[5])
    c.finish_sends()
    l_close()
    p_close()
    c.done(r.ginr.at[pl.ds(0, 3)], r.misc.at[6], r.misc.at[7])
    wait_all(load[1 + len(l_ad) + 7 :])


def spread(names, *refs):
    r = Bag()
    for n, f in zip(names, refs):
        setattr(r, n, f)
    W = r.b_out.shape[2]
    FQ = r.v_f1u.shape[2]
    loads = []
    for k, (src, dst) in enumerate(((r.outr, r.b_out), (r.ginr, r.b_gin), (r.fin_s, r.b_s), (r.fin_r, r.b_r), (r.fin_p, r.b_p))):
        loads.append(pltpu.make_async_copy(src, dst, r.sem_in.at[k]))
        loads[-1].start()
    stores = []

    def store(key):
        stores.append(pltpu.make_async_copy(getattr(r, "v_" + key), getattr(r, "o_" + key), r.sem_out.at[len(stores)]))
        stores[-1].start()

    def widen(ref, src):
        @pl.loop(0, ref.shape[0])
        def _(i):
            ref[i] = src(i).astype(F32)

    loads[0].wait()
    widen(r.v_out, lambda i: r.b_out[i])
    store("out")
    loads[1].wait()
    widen(r.v_gin, lambda i: r.b_gin[i])
    store("gin")
    loads[2].wait()
    widen(r.v_f1u, lambda i: r.b_s[i, :, :FQ])
    store("f1u")
    widen(r.v_f2d, lambda i: r.b_s[i, :, FQ : 2 * FQ])
    store("f2d")

    @pl.loop(0, r.v_qu.shape[0])
    def _(i):
        for k in range(3):
            r.v_qu[i, k] = r.b_s[i, :, 2 * FQ + k * W : 2 * FQ + (k + 1) * W].astype(F32)

    store("qu")
    widen(r.v_od, lambda i: r.b_s[i, :, 2 * FQ + 3 * W :])
    store("od")
    loads[3].wait()
    for k, key in enumerate(("f1d", "f2u", "ou")):
        ref = getattr(r, "v_" + key)

        @pl.loop(0, ref.shape[0])
        def _(i):
            for j in range(4):
                ref[i, :, W * j : W * (j + 1)] = r.b_r[i, j, :, W * k : W * (k + 1)].astype(F32)

        store(key)
    loads[4].wait()
    widen(r.v_qd, lambda i: r.b_p[i])
    store("qd")
    for cp in stores:
        cp.wait()


def make_shards(groups):
    def shards(
        tokens, lengths, adapter_ids, qkv_weight, qkv_down, qkv_up, out_weight, out_down, out_up,
        fc1_weight, fc1_down, fc1_up, fc2_weight, fc2_down, fc2_up, cotangent,
    ):
        n, S, D = tokens.shape
        A, _, R = qkv_down.shape
        T = A * R
        W = out_weight.shape[0]
        FQ = fc1_weight.shape[1]
        m0 = 2 * FQ
        l0 = m0 + 3 * W
        total = l0 + 4 * W + D
        blocks = (
            (0, FQ, 2), (FQ, m0, 3), (m0, m0 + W, 2), (m0 + W, m0 + 2 * W, 3), (m0 + 2 * W, l0, 1),
            (l0, l0 + 3 * W, 0), (l0 + 3 * W, l0 + 4 * W, 1), (l0 + 4 * W, total, 0),
        )
        sizes = dict(n_img=n, S=S, D=D, R=R, T=T, W=W, FQ=FQ, starts=(m0, l0, total), blocks=blocks)

        def turned(a):
            return jnp.transpose(a, (0, 2, 1)).reshape(T, a.shape[1])

        args = dict(
            len=lengths, ids=adapter_ids, tokens=tokens, cot=cotangent,
            hq=jnp.transpose(qkv_weight, (1, 0, 2)), ho=out_weight, h1=fc1_weight, h2=fc2_weight,
            h_aqd=turned(qkv_down), h_aqu=jnp.transpose(qkv_up, (0, 2, 1, 3)), h_aod=turned(out_down),
            h_a1u=fc1_up.reshape(T, FQ), h_a2d=turned(fc2_down), h_aou=out_up.reshape(T, D),
            h_a1d=turned(fc1_down), h_a2u=fc2_up.reshape(T, D),
        )
        outs = dict(outr=(n, S, W), ginr=(n, S, W), fin_s=(GROUP, R, 2 * FQ + 4 * W), fin_r=(GROUP, 4, R, 3 * W), fin_p=(GROUP, R, D))
        heads = W // HD
        vm = dict(
            wq=((4, D, 3 * W), BF), wo=((4, W, D), BF), w1=((4, D, FQ), BF), w2=((4, FQ, D), BF),
            aqu=((A, 3, R, W), BF), aod=((T, W), BF), a1u=((T, FQ), BF), a2d=((T, FQ), BF),
            out_qu=((n, R, 3 * W), BF), out_od=((n, R, W), BF), out_f1=((n, R, FQ), BF), out_f2=((n, R, FQ), BF),
            sel_qu=((R, 12 * W), BF), sel_od=((R, 4 * W), BF), sel_f1=((R, 4 * FQ), BF), sel_f2=((R, 4 * FQ), BF),
            dn_qkv=((R, D), BF), up_out=((R, D), BF), dn_fc1=((R, D), BF), up_fc2=((R, D), BF),
            x=((S, D), BF), dzq=((4, S, W), BF), dz=((S, D), BF),
            first=((S, D), BF), lift_qkv=((S, R), BF), g_fc2=((S, R), BF), proj=((4, S, 3 * W), BF), qm=((4, heads * S, W), BF),
            st=((S, heads * S), F32), ds=((S, heads * S), BF), soft=((4, S, heads * S), F32), att=((S, 4 * W), BF),
            branch=((S, D), F32), lift_out=((S, R), BF), mixed=((S, D), F32), second=((S, D), BF), lift_fc1=((S, R), BF),
            outacc=((S, D), F32), gsec=((S, D), F32), lift_fc2_acc=((S, R), F32), glf1_acc=((S, R), F32),
            lift_fc2=((S, R), BF), gbr=((S, D), BF), g_out=((S, R), BF), gm=((heads * S, W), BF), gp=((S, 12 * W), BF),
            g_qkv=((S, R), BF),
            g_f1=((R, 4 * FQ), BF), g_f2=((R, 4 * FQ), BF), g_f1d=((R, D), BF), g_f2u=((R, D), BF), g_ou=((R, D), BF),
            g_qu=((R, 12 * W), BF), g_od=((R, 4 * W), BF), g_qd=((R, D), BF),
            sp=((n, R, total), BF), dense=((T, total), BF), rsb=((GROUP, R, total), BF), red=((R, total), BF),
            zb=((4, R, 3 * W), BF),
        )
        units = 18
        sems = dict(rz=units, rx=units, ry=units, rd=units, rs=units, sends=None, loc=28, misc=76)
        names = list(args) + list(outs) + list(vm) + list(sems)
        anywhere = pl.BlockSpec(memory_space=pl.ANY)
        got = pl.pallas_call(
            lambda *refs: kernel(names, sizes, *refs),
            out_shape=tuple(jax.ShapeDtypeStruct(s, BF) for s in outs.values()),
            in_specs=[pl.BlockSpec(memory_space=pltpu.SMEM)] * 2 + [anywhere] * (len(args) - 2),
            out_specs=tuple([anywhere] * len(outs)),
            scratch_shapes=[pltpu.VMEM(s, t) for s, t in vm.values()]
            + [pltpu.SemaphoreType.DMA if k is None else pltpu.SemaphoreType.DMA((k,)) for k in sems.values()],
            compiler_params=pltpu.CompilerParams(collective_id=0, has_side_effects=True, vmem_limit_bytes=60 * 2**20),
        )(*args.values())
        outr, ginr, fin_s, fin_r, fin_p = got
        if groups > 1:
            across = [[m + GROUP * g for g in range(groups)] for m in range(GROUP)]
            fin_s, fin_r, fin_p = lax.psum(tuple(v.astype(F32) for v in (fin_s, fin_r, fin_p)), "dp", axis_index_groups=across)
        full = (A, R, D)
        wide = dict(
            out=(n, S, W), gin=(n, S, W), qd=full, qu=(A, 3, R, W), od=(A, R, W), ou=full, f1d=full, f1u=(A, R, FQ), f2d=(A, R, FQ), f2u=full
        )
        held = dict(b_out=outr, b_gin=ginr, b_s=fin_s, b_r=fin_r, b_p=fin_p)
        names = ["outr", "ginr", "fin_s", "fin_r", "fin_p"] + ["o_" + k for k in wide] + list(held) + ["v_" + k for k in wide] + ["sem_in", "sem_out"]
        output, input_grad, qd, qu, od, ou, f1d, f1u, f2d, f2u = pl.pallas_call(
            lambda *refs: spread(names, *refs),
            out_shape=tuple(jax.ShapeDtypeStruct(v, F32) for v in wide.values()),
            in_specs=[anywhere] * 5,
            out_specs=tuple([anywhere] * len(wide)),
            scratch_shapes=[pltpu.VMEM(v.shape, v.dtype) for v in held.values()]
            + [pltpu.VMEM(v, F32) for v in wide.values()]
            + [pltpu.SemaphoreType.DMA((5,)), pltpu.SemaphoreType.DMA((len(wide),))],
            compiler_params=pltpu.CompilerParams(vmem_limit_bytes=60 * 2**20),
        )(outr, ginr, fin_s, fin_r, fin_p)
        back = lambda a: jnp.transpose(a, (0, 2, 1))
        return (output, input_grad, back(qd), jnp.transpose(qu, (0, 2, 1, 3)), back(od), ou, back(f1d), f1u, back(f2d), f2u)

    return shards


def solution(mesh):
    in_specs = (
        P("dp", None, None), P("dp"), P("dp", None), P(None, None, "tensor"), P(), P(None, None, None, "tensor"),
        P("tensor", None), P(None, "tensor", None), P(), P(None, "tensor"), P(), P(None, None, "tensor"),
        P("tensor", None), P(None, "tensor", None), P(), P("dp", None, "tensor"),
    )
    out_specs = (
        P("dp", None, "tensor"), P("dp", None, "tensor"), P(), P(None, None, None, "tensor"), P(None, "tensor", None),
        P(), P(), P(None, None, "tensor"), P(None, "tensor", None), P(),
    )
    shards = make_shards(mesh.shape["dp"] // GROUP)
    return jax.shard_map(shards, mesh=mesh, in_specs=in_specs, out_specs=out_specs, check_vma=False)
```

```python
import jax
import jax.numpy as jnp
from jax import lax
from jax.experimental import pallas as pl
from jax.experimental.pallas import tpu as pltpu
from jax.sharding import PartitionSpec as P


BF = jnp.bfloat16
F32 = jnp.float32
MESH = pl.DeviceIdType.MESH
EPSILON = 1e-6
NEG_FILL = -1e30
HD = 64
GROUP = 8
BLOCK = 160
SMALL = 32
STEP = 512


def dot(a, b):
    return lax.dot_general(a, b, (((1,), (0,)), ((), ())), preferred_element_type=F32)


def dot_nt(a, b):
    return lax.dot_general(a, b, (((1,), (1,)), ((), ())), preferred_element_type=F32)


def dot_tn(a, b):
    return lax.dot_general(a, b, (((0,), (0,)), ((), ())), preferred_element_type=F32)


def rows_loop(count, body, block=BLOCK):
    @pl.loop(0, count // block)
    def _(i):
        body(pl.ds(pl.multiple_of(i * block, block), block))


def moments(values):
    centred = values - jnp.mean(values, axis=-1, keepdims=True)
    inverse = lax.rsqrt(jnp.mean(centred * centred, axis=-1, keepdims=True) + EPSILON)
    return centred, inverse


def norm_back(values, grad):
    centred, inverse = moments(values)
    hat = centred * inverse
    return inverse * (
        grad - jnp.mean(grad, axis=-1, keepdims=True) - hat * jnp.mean(grad * hat, axis=-1, keepdims=True)
    )


class Bag:
    pass


def prep(r):
    def body(rows):
        centred, inverse = moments(r.x[rows, :].astype(F32))
        r.first[rows, :] = (centred * inverse).astype(BF)

    rows_loop(r.S, body)


def prep_dz(r):
    def body(rows):
        keep = (lax.broadcasted_iota(jnp.int32, (BLOCK, 1), 0) + rows.start) < r.length
        for j in range(4):
            v = r.dzq[j, rows, :]
            r.dz[rows, r.W * j : r.W * (j + 1)] = jnp.where(keep, v, jnp.zeros_like(v))

    rows_loop(r.S, body)
    r.g_fc2[...] = dot_nt(r.dz[...], r.up_fc2[...]).astype(BF)


def by_head(r, v, ref):
    head = lax.broadcasted_iota(jnp.int32, (r.S, r.W), 1) // HD
    for h in range(r.W // HD):
        ref[h * r.S : (h + 1) * r.S, :] = jnp.where(head == h, v, jnp.zeros_like(v))


def own_lanes(r, t):
    head = lax.broadcasted_iota(jnp.int32, (r.S, r.W), 1) // HD
    out = t[: r.S]
    for h in range(1, r.W // HD):
        out = jnp.where(head == h, t[h * r.S : (h + 1) * r.S], out)
    return out


def block_of(q, width):
    return pl.ds(pl.multiple_of(q * width, width), width)


def attn_fwd(r, q):
    S, W = r.S, r.W
    p = dot(r.first[...], r.wq[q]) + dot(r.lift_qkv[...], r.sel_qu[:, block_of(q, 3 * W)])
    r.proj[q] = p.astype(BF)
    by_head(r, r.proj[q, :, 0:W], r.qm.at[q])
    r.st[...] = dot_nt(r.proj[q, :, W : 2 * W], r.qm[q])
    valid = lax.broadcasted_iota(jnp.int32, (S, 128), 0) < r.length

    for k in range(r.st.shape[1] // 128):
        c = slice(k * 128, (k + 1) * 128)
        v = jnp.where(valid, r.st[:, c] * (HD**-0.5), NEG_FILL)
        e = jnp.exp(v - jnp.max(v, axis=0, keepdims=True))
        soft = e * (1.0 / jnp.sum(e, axis=0, keepdims=True))
        r.soft[q, :, c] = soft
        r.ds[:, c] = soft.astype(BF)

    att = own_lanes(r, dot_tn(r.ds[...], r.proj[q, :, 2 * W : 3 * W])).astype(BF)
    r.att[:, block_of(q, W)] = att
    r.branch[...] += dot(att, r.wo[q])


def after_attn(r):
    r.lift_out[...] = dot_nt(r.att[...], r.sel_od[...]).astype(BF)
    r.branch[...] += dot(r.lift_out[...], r.up_out[...])

    def body(rows):
        mixed = r.x[rows, :].astype(F32) + r.branch[rows, :]
        r.mixed[rows, :] = mixed
        centred, inverse = moments(mixed)
        r.second[rows, :] = (centred * inverse).astype(BF)

    rows_loop(r.S, body)
    r.lift_fc1[...] = dot_nt(r.second[...], r.dn_fc1[...]).astype(BF)
    r.outacc[...] = jnp.zeros_like(r.outacc)
    r.gsec[...] = jnp.zeros_like(r.gsec)
    r.lift_fc2_acc[...] = jnp.zeros_like(r.lift_fc2_acc)
    r.glf1_acc[...] = jnp.zeros_like(r.glf1_acc)


def ffn_unit(r, q, u):
    FQ = r.FQ
    cols = block_of(u, STEP)
    wide = pl.ds(pl.multiple_of(q * FQ + u * STEP, STEP), STEP)
    up1 = r.sel_f1[:, wide]
    dn2 = r.sel_f2[:, wide]
    r.before[...] = dot(r.second[...], r.w1[q, :, cols]) + dot(r.lift_fc1[...], up1)
    r.gh[...] = dot_nt(r.dz[...], r.w2[q, cols, :]) + dot(r.g_fc2[...], dn2)

    def body(rows):
        b = r.before[rows, :]
        cdf = 0.5 * (1.0 + lax.erf(b * (0.5**0.5)))
        r.hidden[rows, :] = (b * cdf).astype(BF)
        slope = cdf + b * jnp.exp(-0.5 * b * b) * 0.3989422804014327
        r.gb[rows, :] = (slope * r.gh[rows, :]).astype(BF)

    for k in range(r.S // SMALL):
        body(pl.ds(k * SMALL, SMALL))
    h = r.hidden[...]
    g = r.gb[...]
    r.outacc[...] += dot(h, r.w2[q, cols, :])
    r.gsec[...] += dot_nt(g, r.w1[q, :, cols])
    r.lift_fc2_acc[...] += dot_nt(h, dn2)
    r.glf1_acc[...] += dot_nt(g, up1)
    r.g_f1[:, wide] = dot_tn(r.lift_fc1[...], g).astype(BF)
    r.g_f2[:, wide] = dot_tn(r.g_fc2[...], h).astype(BF)


def after_ffn_out(r):
    r.outacc[...] += dot(r.lift_fc2[...], r.up_fc2[...])

    def body(rows):
        keep = (lax.broadcasted_iota(jnp.int32, (BLOCK, 1), 0) + rows.start) < r.length
        v = jnp.where(keep, r.mixed[rows, :] + r.outacc[rows, :], 0.0).astype(BF)
        for j in range(4):
            r.outq[j, rows, :] = v[:, r.W * j : r.W * (j + 1)]

    rows_loop(r.S, body)


def after_ffn_back(r):
    g1 = r.glf1_acc[...].astype(BF)
    r.g_f2u[...] = dot_tn(r.lift_fc2[...], r.dz[...]).astype(BF)
    r.g_f1d[...] = dot_tn(g1, r.second[...]).astype(BF)
    r.gsec[...] += dot(g1, r.dn_fc1[...])

    def body(rows):
        g = r.dz[rows, :].astype(F32) + norm_back(r.mixed[rows, :], r.gsec[rows, :])
        r.gsec[rows, :] = g
        r.gbr[rows, :] = g.astype(BF)

    rows_loop(r.S, body)
    gbr = r.gbr[...]
    r.g_ou[...] = dot_tn(r.lift_out[...], gbr).astype(BF)
    r.g_out[...] = dot_nt(gbr, r.up_out[...]).astype(BF)


def back_attended(r):
    W = r.W
    r.ga[...] = dot(r.g_out[...], r.sel_od[...])
    for q in range(4):
        c = slice(q * W, (q + 1) * W)
        r.ga[:, c] += dot_nt(r.gbr[...], r.wo[q])
    r.g_od[...] = dot_tn(r.g_out[...], r.att[...]).astype(BF)


def attn_back(r, q):
    W = r.W
    sc = HD**-0.5
    by_head(r, r.ga[:, block_of(q, W)].astype(BF), r.gm)
    k = r.proj[q, :, W : 2 * W]
    r.st[...] = dot_nt(r.proj[q, :, 2 * W : 3 * W], r.gm[...])
    gv = dot(r.soft[q].astype(BF), r.gm[...])

    for i in range(r.st.shape[1] // 128):
        c = slice(i * 128, (i + 1) * 128)
        soft, gs = r.soft[q, :, c], r.st[:, c]
        r.ds[:, c] = (soft * (gs - jnp.sum(soft * gs, axis=0, keepdims=True))).astype(BF)

    ds = r.ds[...]
    base = pl.multiple_of(3 * W * q, 128)
    r.gp[:, pl.ds(base, W)] = (own_lanes(r, dot_tn(ds, k)) * sc).astype(BF)
    r.gp[:, pl.ds(base + W, W)] = (dot(ds, r.qm[q]) * sc).astype(BF)
    r.gp[:, pl.ds(base + 2 * W, W)] = gv.astype(BF)
    wide = block_of(q, 3 * W)
    r.g_qu[:, wide] = dot_tn(r.lift_qkv[...], r.gp[:, wide]).astype(BF)


def finish_grads(r):
    gq = dot_nt(r.gp[...], r.sel_qu[...]).astype(BF)
    r.g_qd[...] = dot_tn(gq, r.first[...]).astype(BF)
    r.g_qkv[...] = gq


def back_first(r):
    W = r.W
    r.mixed[...] = dot(r.g_qkv[...], r.dn_qkv[...])
    for q in range(4):
        r.mixed[...] += dot_nt(r.gp[:, 3 * W * q : 3 * W * (q + 1)], r.wq[q])


def finish_rows(r, k):
    rows = slice(k * (r.S // 2), (k + 1) * (r.S // 2))
    r.gin[rows, :] = (r.gsec[rows, :] + norm_back(r.x[rows, :].astype(F32), r.mixed[rows, :])).astype(BF)


class Stream:
    def __init__(self, r):
        self.r = r
        d = self.d = lax.axis_index("dp")
        self.z = lax.axis_index("tensor")
        m = self.m = d % GROUP
        self.base = d - m
        self.dx = d + 2 - 4 * ((m // 2) % 2)
        self.dy = d + 4 - 8 * (m // 4)
        self.ds = d + 1 - 2 * (m % 2)
        self.dd = self.dx + self.dy - d
        self.inner = (self.z + 1) // 2 == 1
        self.n_a, self.n = 6, 18

    def quarter(self, i):
        return (self.z + jnp.where(self.z < 2, i, 4 - i)) % 4

    def unit(self, t, f):
        pl.when(t < self.n_a)(lambda: f("A", t % 2, t // 2 + 1))
        pl.when((t >= self.n_a) & (t < self.n - 2))(lambda: f("B", (t - self.n_a) % 4, (t - self.n_a) // 4 + 1))
        last = t - (self.n - 2)
        pl.when((last >= 0) & (last % 2 == 0))(lambda: f("X", last + 2, 3))
        pl.when((last >= 0) & (last % 2 == 1))(lambda: f("Y", last + 2, 3))

    def pair(self, kind):
        return (self.dy, self.dx) if kind == "X" else (self.dx, self.dy)

    def greet(self):
        bar = pltpu.get_barrier_semaphore()
        for k in range(1, GROUP):
            peer = self.base + (self.m + k) % GROUP
            pl.semaphore_signal(bar, inc=1, device_id=(peer, self.z), device_id_type=MESH)
        for k in range(1, 4):
            pl.semaphore_signal(bar, inc=1, device_id=(self.d, (self.z + k) % 4), device_id_type=MESH)

    def met(self):
        pl.semaphore_wait(pltpu.get_barrier_semaphore(), GROUP + 2)

    def parts(self, kind, p, q, d, half=None):
        r, m = self.r, d - self.base
        first, c = (0, pl.ds(0, r.D)) if half is None else (half, pl.ds(r.D // 2 * half, r.D // 2))
        if kind == "A":
            n = r.D // GROUP // 2
            k = r.W // GROUP // 2
            part = n if half is None else n // 2
            a = pl.ds(pl.multiple_of((2 * m + p) * n + first * part, part), part)
            b = pl.ds(pl.multiple_of((2 * m + p) * k, k), k)
            return ((r.wq.at[q, a, :]), (r.wo.at[q, b, c]))
        n = r.D // GROUP
        width = r.FQ // 4
        k = width // GROUP
        part = n if half is None else n // 2
        a = pl.ds(pl.multiple_of(m * n + first * part, part), part)
        b = pl.ds(pl.multiple_of(p * width + m * k, k), k)
        return (r.w1.at[q, a, block_of(p, width)], r.w2.at[q, b, c])

    def own(self, kind, p, d=None):
        r, z = self.r, self.z
        d = self.d if d is None else d
        m = d - self.base
        first, second = self.parts(kind, p, z, d)
        if kind == "A":
            n = r.D // GROUP // 2
            k = r.W // GROUP // 2
            a = pl.ds(pl.multiple_of((2 * m + p) * n, n), n)
            pairs = [(r.hq.at[i, a, :], r.wq.at[z, a, pl.ds(i * r.W, r.W)]) for i in range(3)]
            return pairs + [(r.ho.at[pl.ds(pl.multiple_of((2 * m + p) * k, k), k), :], second)]
        n = r.D // GROUP
        k = r.FQ // 4 // GROUP
        a = pl.ds(pl.multiple_of(m * n, n), n)
        b = pl.ds(pl.multiple_of(p * (r.FQ // 4) + m * k, k), k)
        return [(r.h1.at[a, block_of(p, r.FQ // 4)], first), (r.h2.at[b, :], second)]

    def send(self, srcs, dsts, sem, dev):
        for s, t in zip(srcs, dsts):
            pltpu.make_async_remote_copy(
                src_ref=s, dst_ref=t, send_sem=self.r.sends, recv_sem=sem, device_id=dev, device_id_type=MESH
            ).start()

    def wait(self, rows, sem):
        v = self.r.w2.at[0, pl.ds(0, rows), :]
        pltpu.make_async_copy(v, v, sem).wait()

    def index(self, kind, p, i):
        return (i - 1) * 2 + p if kind == "A" else 6 + (i - 1) * 4 + p

    def inner_sends(self, kind, p):
        z, d = self.z, self.d

        @pl.when(self.inner)
        def _():
            src, dst = zip(*self.own(kind, p))
            for to in (3 * (z - 1), 3 - z):
                self.send(src, dst, self.r.rz.at[self.index(kind, p, 1)], (d, to))

    def outer_sends(self, kind, p, i):
        z, d = self.z, self.d

        @pl.when(z % 3 == 0)
        def _():
            src, dst = zip(*self.own(kind, p))
            to = 2 - z // 3 if i == 2 else 1 + z // 3
            sem = self.r.rz.at[self.index(kind, p, i)]
            self.send(src, dst, sem, (d, to))
            if kind == "B" and i == 3:
                for n, wide in ((0, "X"), (1, "Y")):

                    @pl.when(p == n + 2)
                    def _():
                        src, dst = zip(*self.own("B", p, self.pair(wide)[0]))
                        self.send(src, dst, sem, (d, to))

    def z_stage(self, t):
        def forward(kind, p, i):
            self.wait(128 if kind in "XY" else 64, self.r.rz.at[t])
            if kind in "AB":

                @pl.when(self.inner & (i < 3))
                def _():
                    piece = self.parts(kind, p, self.quarter(i), self.d)
                    self.send(piece, piece, self.r.rz.at[self.index(kind, p, i + 1)], (self.d, 3 * (self.z - 1)))

        self.unit(t, forward)

    def xy_sends(self, t):
        def go(kind, p, i):
            z, r, q = self.z, self.r, self.quarter(i)
            if kind in "AB":
                carried, targets = (self.d,), ((r.rx, self.dx), (r.ry, self.dy))
            else:
                beside, across = self.pair(kind)
                carried, targets = (self.d, beside), (((r.rx if kind == "X" else r.ry), across),)
            for frm in carried:
                piece = self.parts(kind, p, q, frm)
                for sem, to in targets + ((r.rs, self.ds),):
                    self.send(piece, piece, sem.at[t], (to, z))

        self.unit(t, go)

    def xy_stage(self, t):
        def go(kind, p, i):
            z, q, r = self.z, self.quarter(i), self.r
            if kind in "XY":
                self.wait(128, (r.rx if kind == "X" else r.ry).at[t])
                for frm in (self.pair(kind)[1], self.dd):
                    w = self.parts(kind, p, q, frm)
                    self.send(w, w, r.rs.at[t], (self.ds, z))
                return
            for sem, frm, to, half in ((r.rx, self.dx, self.dy, 0), (r.ry, self.dy, self.dx, 1)):
                self.wait(64, sem.at[t])
                h = self.parts(kind, p, q, frm, half)
                self.send(h, h, r.rd.at[t], (to, z))
                w = self.parts(kind, p, q, frm)
                self.send(w, w, r.rs.at[t], (self.ds, z))
                if kind == "B":
                    n = 0 if to is self.dx else 1

                    @pl.when(self.inner & (i == 2) & (p == n + 2))
                    def _():
                        self.send(w, w, r.rz.at[self.index("B", p, 3)], (self.d, 3 * (z - 1)))

        self.unit(t, go)

    def d_stage(self, t):
        def go(kind, p, i):
            if kind in "AB":
                self.wait(64, self.r.rd.at[t])
                w = self.parts(kind, p, self.quarter(i), self.dd)
                self.send(w, w, self.r.rs.at[t], (self.ds, self.z))

        self.unit(t, go)

    def s_stage(self, t):
        self.wait(256, self.r.rs.at[t])

    def finish_sends(self):
        kinds = 6
        always = 7 * self.n - 2 + 2 * kinds + 2

        @pl.loop(0, jnp.where(self.inner, always + 2 * kinds, always))
        def _(i):
            self.wait(64, self.r.sends)


    def to_planes(self, view, target, send_sem, recv_sem):
        for k in range(1, 4):
            j = (self.z + k) % 4
            pltpu.make_async_remote_copy(
                src_ref=view(j), dst_ref=target, send_sem=send_sem, recv_sem=recv_sem, device_id=(self.d, j), device_id_type=MESH
            ).start()

    def to_group(self, view, target, send_sem, recv_sem):
        for k in range(1, GROUP):
            m = (self.m + k) % GROUP
            pltpu.make_async_remote_copy(
                src_ref=view(m), dst_ref=target, send_sem=send_sem, recv_sem=recv_sem, device_id=(self.base + m, self.z), device_id_type=MESH
            ).start()

    def share(self, src, dst, sems):
        place = dst(self.m)
        for to in (self.dx, self.dy, self.dd):
            pltpu.make_async_remote_copy(
                src_ref=src, dst_ref=place, send_sem=sems[0], recv_sem=sems[1], device_id=(to, self.z), device_id_type=MESH
            ).start()
        pltpu.make_async_remote_copy(
            src_ref=src, dst_ref=place, send_sem=sems[2], recv_sem=sems[3], device_id=(self.ds, self.z), device_id_type=MESH
        ).start()

    def pass_on(self, three, dst, sems):
        self.done(three, sems[1])
        for frm in (self.dx, self.dy, self.dd):
            place = dst(frm - self.base)
            pltpu.make_async_remote_copy(
                src_ref=place, dst_ref=place, send_sem=sems[2], recv_sem=sems[3], device_id=(self.ds, self.z), device_id_type=MESH
            ).start()

    def done(self, ref, *sems):
        for s in sems:
            pltpu.make_async_copy(ref, ref, s).wait()


class Sems:
    def __init__(self, ref, first):
        self.ref, self.first = ref, first

    def __getitem__(self, k):
        if isinstance(k, slice):
            return [self[i] for i in range(k.start, k.stop)]
        return self.ref.at[self.first + k]


def one_hot(r, p, transposed):
    R, T, n = r.R, r.T, r.n_img
    shape = (T, n * R) if transposed else (n * R, T)
    a = lax.broadcasted_iota(jnp.int32, shape, 1 if transposed else 0)
    b = lax.broadcasted_iota(jnp.int32, shape, 0 if transposed else 1)
    owner = jnp.zeros(shape, jnp.int32)
    for i in range(n):
        owner = jnp.where(a // R == i, r.ids[i, p], owner)
    hit = (b // R == owner) & (a % R == b % R)
    return jnp.where(hit, 1.0, 0.0).astype(BF)


def choose(r, p, flat):
    shape = (r.R, r.T)
    a = lax.broadcasted_iota(jnp.int32, shape, 0)
    b = lax.broadcasted_iota(jnp.int32, shape, 1)
    hit = (b // r.R == r.my_ids[p]) & (a == b % r.R)
    return dot(jnp.where(hit, 1.0, 0.0).astype(BF), flat).astype(BF)


def kernel(names, sizes, *refs):
    r = Bag()
    for n, f in zip(names, refs):
        setattr(r, n, f)
    for n, v in sizes.items():
        setattr(r, n, v)
    c = Stream(r)
    z, d = c.z, c.d
    S, W, FQ, R, n = r.S, r.W, r.FQ, r.R, r.n_img
    r.before, r.gh = r.st.at[:, pl.ds(0, STEP)], r.st.at[:, pl.ds(STEP, STEP)]
    r.hidden, r.gb = r.ds.at[:, pl.ds(0, STEP)], r.ds.at[:, pl.ds(STEP, STEP)]
    r.ga = r.branch
    r.outq, r.gin = r.dzq, r.first
    for k, name in enumerate(("aqd", "aou", "a1d", "a2u")):
        setattr(r, name, r.dense.at[:, pl.ds(k * r.D, r.D)])
    r.length = r.len[z]
    r.my_ids = [r.ids[z, p] for p in range(4)]
    c.greet()
    load = []

    def fetch(ends):
        slot = len(load)
        copy = lambda: pltpu.make_async_copy(*ends(), r.loc.at[slot])
        copy().start()
        load.append(copy)
        return copy

    l_x = fetch(lambda: (r.tokens.at[z], r.x))
    l_ad = {k: fetch(lambda k=k: (getattr(r, "h_" + k), getattr(r, k))) for k in ("aqd", "aqu", "aod", "a1u", "a2d", "aou", "a1d", "a2u")}
    l_q = [fetch(lambda i=i: (r.hq.at[i], r.wq.at[z, :, pl.ds(i * W, W)])) for i in range(3)]
    l_q.append(fetch(lambda: (r.ho, r.wo.at[z])))
    l_f = [fetch(lambda: (r.h1, r.w1.at[z])), fetch(lambda: (r.h2, r.w2.at[z]))]
    l_c = fetch(lambda: (r.cot.at[z], r.dzq.at[z]))
    c.met()

    def wait_all(copies):
        for copy in copies:
            copy().wait()

    def pick_attn():
        wait_all([l_ad["aqu"], l_ad["aod"]])
        hot = one_hot(r, 0, False)
        for i in range(3):
            r.out_qu[:, :, i * W : (i + 1) * W] = dot(hot, r.aqu[:, i].reshape(r.T, W)).astype(BF).reshape(n, R, W)
        r.out_od[...] = dot(one_hot(r, 1, False), r.aod[...]).astype(BF).reshape(n, R, W)
        c.to_planes(lambda j: r.out_qu.at[j], r.sel_qu.at[:, block_of(z, 3 * W)], r.misc.at[0], r.misc.at[1])
        c.to_planes(lambda j: r.out_od.at[j], r.sel_od.at[:, block_of(z, W)], r.misc.at[70], r.misc.at[71])
        r.sel_qu[:, block_of(z, 3 * W)] = r.out_qu[z]
        r.sel_od[:, block_of(z, W)] = r.out_od[z]

    def have_attn():
        c.done(r.sel_qu.at[:, pl.ds(0, 9 * W)], r.misc.at[0], r.misc.at[1])
        c.done(r.sel_od.at[:, pl.ds(0, 3 * W)], r.misc.at[70], r.misc.at[71])

    def pick_ffn():
        wait_all([l_ad["a1u"], l_ad["a2d"]])
        r.out_f1[...] = dot(one_hot(r, 2, False), r.a1u[...]).astype(BF).reshape(n, R, FQ)
        r.out_f2[...] = dot(one_hot(r, 3, False), r.a2d[...]).astype(BF).reshape(n, R, FQ)
        r.sel_f1[:, block_of(z, FQ)] = r.out_f1[z]
        r.sel_f2[:, block_of(z, FQ)] = r.out_f2[z]

    def send_f1():
        c.to_planes(lambda j: r.out_f1.at[j], r.sel_f1.at[:, block_of(z, FQ)], r.misc.at[72], r.misc.at[73])

    def send_f2():
        c.to_planes(lambda j: r.out_f2.at[j], r.sel_f2.at[:, block_of(z, FQ)], r.misc.at[74], r.misc.at[75])

    def have_ffn():
        c.done(r.sel_f1.at[:, pl.ds(0, 3 * FQ)], r.misc.at[72], r.misc.at[73])
        c.done(r.sel_f2.at[:, pl.ds(0, 3 * FQ)], r.misc.at[74], r.misc.at[75])

    def pick_first():
        l_ad["aqd"]().wait()
        r.dn_qkv[...] = choose(r, 0, r.aqd[...])
        r.lift_qkv[...] = dot_nt(r.first[...], r.dn_qkv[...]).astype(BF)

    def pick_rest():
        wait_all([l_ad["aou"], l_ad["a1d"], l_ad["a2u"]])
        r.up_out[...] = choose(r, 1, r.aou[...])
        r.dn_fc1[...] = choose(r, 2, r.a1d[...])
        r.up_fc2[...] = choose(r, 3, r.a2u[...])

    CUTS = 5

    def send_cot(k):
        rows = pl.ds(k * (S // CUTS), S // CUTS)
        c.to_planes(lambda j: r.cot.at[j, rows, :], r.dzq.at[z, rows, :], r.misc.at[2], r.misc.at[3])

    def have_cot():
        c.done(r.dzq.at[pl.ds(0, 3)], r.misc.at[2], r.misc.at[3])
        l_c().wait()
        prep_dz(r)

    def ffn(n):
        i, u = n // 2, n % 2
        q = c.quarter(i)
        ffn_unit(r, q, u)

        @pl.when(i > 0)
        def _():
            wide = pl.ds(pl.multiple_of(q * FQ + u * STEP, STEP), STEP)
            for ref, base in ((r.g_f1, 0), (r.g_f2, FQ)):
                pltpu.make_async_remote_copy(
                    src_ref=ref.at[:, wide], dst_ref=r.sp.at[z, :, pl.ds(pl.multiple_of(base + u * STEP, STEP), STEP)],
                    send_sem=r.misc.at[8], recv_sem=r.misc.at[9], device_id=(d, q), device_id_type=MESH,
                ).start()

    N = c.n
    LZ, LX, LD = 1, 1, 1
    lag = LZ + LX + LD
    c.inner_sends("A", 0)
    c.inner_sends("A", 1)
    l_x().wait()
    prep(r)
    r.branch[...] = jnp.zeros_like(r.branch)
    c.z_stage(0)

    @pl.loop(0, N + lag)
    def _(t):
        pl.when(t < N)(lambda: c.xy_sends(t))
        pl.when((t >= LZ) & (t < LZ + N))(lambda: c.xy_stage(t - LZ))
        pl.when((t >= LZ + LX) & (t < LZ + LX + N))(lambda: c.d_stage(t - LZ - LX))
        pl.when(t >= lag)(lambda: c.s_stage(t - lag))
        pl.when(t + 1 < N)(lambda: c.z_stage(t + 1))
        pl.when((t >= 1) & (t < 5))(lambda: c.inner_sends("B", t - 1))

        @pl.when((t == 0) | (t == 3))
        def _():
            for p in range(2):
                pl.when(t == 0)(lambda: c.outer_sends("A", p, 2))
                pl.when(t == 3)(lambda: c.outer_sends("A", p, 3))

        pl.when((t >= 5) & (t < 9))(lambda: c.outer_sends("B", t - 5, 2))
        pl.when((t >= 10) & (t < 14))(lambda: c.outer_sends("B", t - 10, 3))
        pl.when((t >= 1) & (t < 11) & ((t - 1) % 2 == 0))(lambda: send_cot((t - 1) // 2))
        pl.when(t == 0)(pick_first)
        pl.when(t == 1)(pick_attn)
        pl.when(t == 2)(lambda: wait_all(l_q))
        pl.when(t == 3)(pick_rest)
        pl.when(t == 4)(pick_ffn)
        pl.when(t == 9)(send_f1)
        pl.when(t == 11)(send_f2)
        pl.when(t == 1 + lag)(have_attn)
        pl.when((t == 2) | (t == 1 + lag) | (t == 3 + lag) | (t == 5 + lag))(lambda: attn_fwd(r, c.quarter((t - 1) // 2)))

        @pl.when(t == 5 + lag)
        def _():
            after_attn(r)
            wait_all(l_f)

        pl.when(t == 12)(have_cot)
        pl.when(t == 14)(have_ffn)
        pl.when((t >= 12) & (t != 19))(lambda: ffn(jnp.minimum(t - 12, 7)))

    mine = block_of(z, W)

    def group(lo, own_end, hi, s, fs, fr, out=None):
        cols, own, reps, zc = pl.ds(lo, hi - lo), pl.ds(lo, own_end - lo), pl.ds(own_end, hi - own_end), pl.ds(fr, hi - own_end)
        sem = Sems(r.misc, s)
        fin = pl.ds(fs, own_end - lo)
        fin_s = r.fin_s if out is None else out

        def send_whole(ref, col):
            c.to_planes(lambda j: ref, r.sp.at[z, :, cols], sem[0], sem[1])
            r.sp[z, :, cols] = ref[...]

        def send(sources):
            for ref, width, col in sources:
                c.to_planes(lambda j: ref.at[:, block_of(j, width)], r.sp.at[z, :, pl.ds(col, width)], sem[0], sem[1])
                r.sp[z, :, col : col + width] = ref[:, block_of(z, width)]

        def expand():
            c.done(r.sp.at[pl.ds(0, 3), :, cols], sem[0], sem[1])
            for a, b, p in r.blocks:
                if lo <= a < hi:
                    r.dense[:, a:b] = dot(one_hot(r, p, True), r.sp[:, :, a:b].reshape(n * R, b - a)).astype(BF)
            c.to_group(lambda m: r.dense.at[block_of(m, R), cols], r.rsb.at[c.m, :, cols], sem[2], sem[3])
            r.rsb[c.m, :, cols] = r.dense[block_of(c.m, R), cols]

        def reduce():
            c.done(r.rsb.at[pl.ds(0, GROUP - 1), :, cols], sem[2], sem[3])
            sums = r.rsb[0, :, cols].astype(F32)
            for k in range(1, GROUP):
                sums = sums + r.rsb[k, :, cols].astype(F32)
            r.red[:, cols] = sums.astype(BF)
            if hi > own_end:
                c.to_planes(lambda j: r.red.at[:, reps], r.zb.at[z, :, zc], sem[4], sem[5])
                r.zb[z, :, zc] = r.red[:, reps]
            if own_end > lo:
                c.share(r.red.at[:, own], lambda m: fin_s.at[m, :, fin], sem[6:10])
                fetch(lambda: (r.red.at[:, own], fin_s.at[c.m, :, fin]))

        def share():
            c.done(r.zb.at[pl.ds(0, 3), :, zc], sem[4], sem[5])
            c.share(r.zb.at[:, :, zc], lambda m: r.fin_r.at[m, :, :, zc], sem[10:14])
            fetch(lambda: (r.zb.at[:, :, zc], r.fin_r.at[c.m, :, :, zc]))

        def relay():
            if own_end > lo:
                c.pass_on(fin_s.at[pl.ds(0, 3), :, fin], lambda m: fin_s.at[m, :, fin], sem[6:10])

        def relay_rep():
            c.pass_on(r.fin_r.at[pl.ds(0, 3), :, :, zc], lambda m: r.fin_r.at[m, :, :, zc], sem[10:14])

        def close():
            if own_end > lo:
                c.done(fin_s.at[pl.ds(0, 3), :, fin], sem[6])
                c.done(fin_s.at[pl.ds(0, 4), :, fin], sem[8], sem[9])
            if hi > own_end:
                c.done(r.fin_r.at[pl.ds(0, 3), :, :, zc], sem[10])
                c.done(r.fin_r.at[pl.ds(0, 4), :, :, zc], sem[12], sem[13])

        return send if out is None else send_whole, expand, reduce, share, relay, relay_rep, close

    m0, l0, end = r.starts
    _, e_expand, e_reduce, _, e_relay, _, e_close = group(0, m0, m0, 8, 0, 0)
    m_send, m_expand, m_reduce, m_share, _, m_relay, m_close = group(m0, m0, l0, 22, 0, 0)
    p0 = l0 + 4 * W
    l_send, l_expand, l_reduce, _, l_relay, _, l_close = group(l0, p0, p0, 36, 2 * FQ, 0)
    p_send, p_expand, p_reduce, _, p_relay, _, p_close = group(p0, end, end, 56, 0, 0, r.fin_p)

    def back(q):
        attn_back(r, q)
        for ref, width, col in ((r.g_qu, 3 * W, l0), (r.g_od, W, l0 + 3 * W)):
            src, dst = ref.at[:, block_of(q, width)], r.sp.at[z, :, pl.ds(col, width)]

            @pl.when(z != q)
            def _():
                pltpu.make_async_remote_copy(
                    src_ref=src, dst_ref=dst, send_sem=r.misc.at[36], recv_sem=r.misc.at[37], device_id=(d, q), device_id_type=MESH
                ).start()

    def send_out(k):
        rows = pl.ds(k * (S // 2), S // 2)
        c.to_planes(lambda j: r.outq.at[j, rows, :], r.outr.at[z, rows, :], r.misc.at[4], r.misc.at[5])
        fetch(lambda: (r.outq.at[z, rows, :], r.outr.at[z, rows, :]))

    r.lift_fc2[...] = r.lift_fc2_acc[...].astype(BF)
    after_ffn_out(r)
    send_out(0)
    after_ffn_back(r)
    m_send([(r.g_f1d, W, m0), (r.g_f2u, W, m0 + W), (r.g_ou, W, m0 + 2 * W)])
    send_out(1)
    for ref, base in ((r.g_f1, 0), (r.g_f2, FQ)):
        r.sp[z, :, base : base + FQ] = ref[:, block_of(z, FQ)]
    back_attended(r)
    e_expand()

    @pl.loop(0, 4)
    def _(q):
        back(q)

    e_reduce()
    m_expand()
    finish_grads(r)
    p_send(r.g_qd, p0)
    for ref, width, col in ((r.g_qu, 3 * W, l0), (r.g_od, W, l0 + 3 * W)):
        r.sp[z, :, col : col + width] = ref[:, block_of(z, width)]
    m_reduce()
    back_first(r)
    half = S // 2

    def send_gin(k):
        rows = pl.ds(k * half, half)
        c.to_planes(lambda j: r.gin.at[rows, block_of(j, W)], r.ginr.at[z, rows, :], r.misc.at[6], r.misc.at[7])
        fetch(lambda: (r.gin.at[rows, mine], r.ginr.at[z, rows, :]))

    finish_rows(r, 0)
    send_gin(0)
    p_expand()
    l_expand()
    finish_rows(r, 1)
    send_gin(1)
    e_relay()
    m_share()
    p_reduce()
    l_reduce()
    m_relay()
    l_relay()
    p_relay()
    e_close()
    m_close()
    c.done(r.outr.at[pl.ds(0, 3)], r.misc.at[4], r.misc.at[5])
    c.finish_sends()
    l_close()
    p_close()
    c.done(r.ginr.at[pl.ds(0, 3)], r.misc.at[6], r.misc.at[7])
    wait_all(load[1 + len(l_ad) + 7 :])


def spread(names, *refs):
    r = Bag()
    for n, f in zip(names, refs):
        setattr(r, n, f)
    W = r.b_out.shape[2]
    FQ = r.v_f1u.shape[2]
    loads = []
    pieces = [(ref.at[i], buf.at[i]) for ref, buf in ((r.outr, r.b_out), (r.ginr, r.b_gin)) for i in range(r.b_out.shape[0])]
    for k, (src, dst) in enumerate(pieces + [(r.fin_s, r.b_s), (r.fin_r, r.b_r), (r.fin_p, r.b_p)]):
        loads.append(pltpu.make_async_copy(src, dst, r.sem_in.at[k]))
        loads[-1].start()
    images = r.b_out.shape[0]
    stores = []

    def store(key):
        stores.append(pltpu.make_async_copy(getattr(r, "v_" + key), getattr(r, "o_" + key), r.sem_out.at[len(stores)]))
        stores[-1].start()

    def widen(ref, src):
        @pl.loop(0, ref.shape[0])
        def _(i):
            ref[i] = src(i).astype(F32)

    for j, key in enumerate(("out", "gin")):
        for i in range(images):
            loads[j * images + i].wait()
            wide = getattr(r, "v_" + key)
            wide[i] = getattr(r, "b_" + key)[i].astype(F32)
            stores.append(pltpu.make_async_copy(wide.at[i], getattr(r, "o_" + key).at[i], r.sem_out.at[len(stores)]))
            stores[-1].start()
    loads = loads[2 * images - 2 :]
    loads[2].wait()
    widen(r.v_f1u, lambda i: r.b_s[i, :, :FQ])
    store("f1u")
    widen(r.v_f2d, lambda i: r.b_s[i, :, FQ : 2 * FQ])
    store("f2d")

    @pl.loop(0, r.v_qu.shape[0])
    def _(i):
        for k in range(3):
            r.v_qu[i, k] = r.b_s[i, :, 2 * FQ + k * W : 2 * FQ + (k + 1) * W].astype(F32)

    store("qu")
    widen(r.v_od, lambda i: r.b_s[i, :, 2 * FQ + 3 * W :])
    store("od")
    loads[3].wait()
    for k, key in enumerate(("f1d", "f2u", "ou")):
        ref = getattr(r, "v_" + key)

        @pl.loop(0, ref.shape[0])
        def _(i):
            for j in range(4):
                ref[i, :, W * j : W * (j + 1)] = r.b_r[i, j, :, W * k : W * (k + 1)].astype(F32)

        store(key)
    loads[4].wait()
    widen(r.v_qd, lambda i: r.b_p[i])
    store("qd")
    for cp in stores:
        cp.wait()


def make_shards(groups):
    def shards(
        tokens, lengths, adapter_ids, qkv_weight, qkv_down, qkv_up, out_weight, out_down, out_up,
        fc1_weight, fc1_down, fc1_up, fc2_weight, fc2_down, fc2_up, cotangent,
    ):
        n, S, D = tokens.shape
        A, _, R = qkv_down.shape
        T = A * R
        W = out_weight.shape[0]
        FQ = fc1_weight.shape[1]
        m0 = 2 * FQ
        l0 = m0 + 3 * W
        total = l0 + 4 * W + D
        blocks = (
            (0, FQ, 2), (FQ, m0, 3), (m0, m0 + W, 2), (m0 + W, m0 + 2 * W, 3), (m0 + 2 * W, l0, 1),
            (l0, l0 + 3 * W, 0), (l0 + 3 * W, l0 + 4 * W, 1), (l0 + 4 * W, total, 0),
        )
        sizes = dict(n_img=n, S=S, D=D, R=R, T=T, W=W, FQ=FQ, starts=(m0, l0, total), blocks=blocks)

        def turned(a):
            return jnp.transpose(a, (0, 2, 1)).reshape(T, a.shape[1])

        args = dict(
            len=lengths, ids=adapter_ids, tokens=tokens, cot=cotangent,
            hq=jnp.transpose(qkv_weight, (1, 0, 2)), ho=out_weight, h1=fc1_weight, h2=fc2_weight,
            h_aqd=turned(qkv_down), h_aqu=jnp.transpose(qkv_up, (0, 2, 1, 3)), h_aod=turned(out_down),
            h_a1u=fc1_up.reshape(T, FQ), h_a2d=turned(fc2_down), h_aou=out_up.reshape(T, D),
            h_a1d=turned(fc1_down), h_a2u=fc2_up.reshape(T, D),
        )
        outs = dict(outr=(n, S, W), ginr=(n, S, W), fin_s=(GROUP, R, 2 * FQ + 4 * W), fin_r=(GROUP, 4, R, 3 * W), fin_p=(GROUP, R, D))
        heads = W // HD
        vm = dict(
            wq=((4, D, 3 * W), BF), wo=((4, W, D), BF), w1=((4, D, FQ), BF), w2=((4, FQ, D), BF),
            aqu=((A, 3, R, W), BF), aod=((T, W), BF), a1u=((T, FQ), BF), a2d=((T, FQ), BF),
            out_qu=((n, R, 3 * W), BF), out_od=((n, R, W), BF), out_f1=((n, R, FQ), BF), out_f2=((n, R, FQ), BF),
            sel_qu=((R, 12 * W), BF), sel_od=((R, 4 * W), BF), sel_f1=((R, 4 * FQ), BF), sel_f2=((R, 4 * FQ), BF),
            dn_qkv=((R, D), BF), up_out=((R, D), BF), dn_fc1=((R, D), BF), up_fc2=((R, D), BF),
            x=((S, D), BF), dzq=((4, S, W), BF), dz=((S, D), BF),
            first=((S, D), BF), lift_qkv=((S, R), BF), g_fc2=((S, R), BF), proj=((4, S, 3 * W), BF), qm=((4, heads * S, W), BF),
            st=((S, heads * S), F32), ds=((S, heads * S), BF), soft=((4, S, heads * S), F32), att=((S, 4 * W), BF),
            branch=((S, D), F32), lift_out=((S, R), BF), mixed=((S, D), F32), second=((S, D), BF), lift_fc1=((S, R), BF),
            outacc=((S, D), F32), gsec=((S, D), F32), lift_fc2_acc=((S, R), F32), glf1_acc=((S, R), F32),
            lift_fc2=((S, R), BF), gbr=((S, D), BF), g_out=((S, R), BF), gm=((heads * S, W), BF), gp=((S, 12 * W), BF),
            g_qkv=((S, R), BF),
            g_f1=((R, 4 * FQ), BF), g_f2=((R, 4 * FQ), BF), g_f1d=((R, D), BF), g_f2u=((R, D), BF), g_ou=((R, D), BF),
            g_qu=((R, 12 * W), BF), g_od=((R, 4 * W), BF), g_qd=((R, D), BF),
            sp=((n, R, total), BF), dense=((T, total), BF), rsb=((GROUP, R, total), BF), red=((R, total), BF),
            zb=((4, R, 3 * W), BF),
        )
        units = 18
        sems = dict(rz=units, rx=units, ry=units, rd=units, rs=units, sends=None, loc=28, misc=76)
        names = list(args) + list(outs) + list(vm) + list(sems)
        anywhere = pl.BlockSpec(memory_space=pl.ANY)
        got = pl.pallas_call(
            lambda *refs: kernel(names, sizes, *refs),
            out_shape=tuple(jax.ShapeDtypeStruct(s, BF) for s in outs.values()),
            in_specs=[pl.BlockSpec(memory_space=pltpu.SMEM)] * 2 + [anywhere] * (len(args) - 2),
            out_specs=tuple([anywhere] * len(outs)),
            scratch_shapes=[pltpu.VMEM(s, t) for s, t in vm.values()]
            + [pltpu.SemaphoreType.DMA if k is None else pltpu.SemaphoreType.DMA((k,)) for k in sems.values()],
            compiler_params=pltpu.CompilerParams(collective_id=0, has_side_effects=True, vmem_limit_bytes=60 * 2**20),
        )(*args.values())
        outr, ginr, fin_s, fin_r, fin_p = got
        if groups > 1:
            across = [[m + GROUP * g for g in range(groups)] for m in range(GROUP)]
            fin_s, fin_r, fin_p = lax.psum(tuple(v.astype(F32) for v in (fin_s, fin_r, fin_p)), "dp", axis_index_groups=across)
        full = (A, R, D)
        wide = dict(
            out=(n, S, W), gin=(n, S, W), qd=full, qu=(A, 3, R, W), od=(A, R, W), ou=full, f1d=full, f1u=(A, R, FQ), f2d=(A, R, FQ), f2u=full
        )
        held = dict(b_out=outr, b_gin=ginr, b_s=fin_s, b_r=fin_r, b_p=fin_p)
        names = ["outr", "ginr", "fin_s", "fin_r", "fin_p"] + ["o_" + k for k in wide] + list(held) + ["v_" + k for k in wide] + ["sem_in", "sem_out"]
        output, input_grad, qd, qu, od, ou, f1d, f1u, f2d, f2u = pl.pallas_call(
            lambda *refs: spread(names, *refs),
            out_shape=tuple(jax.ShapeDtypeStruct(v, F32) for v in wide.values()),
            in_specs=[anywhere] * 5,
            out_specs=tuple([anywhere] * len(wide)),
            scratch_shapes=[pltpu.VMEM(v.shape, v.dtype) for v in held.values()]
            + [pltpu.VMEM(v, F32) for v in wide.values()]
            + [pltpu.SemaphoreType.DMA((2 * n + 3,)), pltpu.SemaphoreType.DMA((2 * n + 8,))],
            compiler_params=pltpu.CompilerParams(vmem_limit_bytes=60 * 2**20),
        )(outr, ginr, fin_s, fin_r, fin_p)
        back = lambda a: jnp.transpose(a, (0, 2, 1))
        return (output, input_grad, back(qd), jnp.transpose(qu, (0, 2, 1, 3)), back(od), ou, back(f1d), f1u, back(f2d), f2u)

    return shards


def solution(mesh):
    in_specs = (
        P("dp", None, None), P("dp"), P("dp", None), P(None, None, "tensor"), P(), P(None, None, None, "tensor"),
        P("tensor", None), P(None, "tensor", None), P(), P(None, "tensor"), P(), P(None, None, "tensor"),
        P("tensor", None), P(None, "tensor", None), P(), P("dp", None, "tensor"),
    )
    out_specs = (
        P("dp", None, "tensor"), P("dp", None, "tensor"), P(), P(None, None, None, "tensor"), P(None, "tensor", None),
        P(), P(), P(None, None, "tensor"), P(None, "tensor", None), P(),
    )
    shards = make_shards(mesh.shape["dp"] // GROUP)
    return jax.shard_map(shards, mesh=mesh, in_specs=in_specs, out_specs=out_specs, check_vma=False)
```

```python
import jax
import jax.numpy as jnp
from jax import lax
from jax.experimental import pallas as pl
from jax.experimental.pallas import tpu as pltpu
from jax.sharding import PartitionSpec as P


BF = jnp.bfloat16
F32 = jnp.float32
MESH = pl.DeviceIdType.MESH
EPSILON = 1e-6
NEG_FILL = -1e30
HD = 64
GROUP = 8
BLOCK = 160
SMALL = 32
STEP = 512


def dot(a, b):
    return lax.dot_general(a, b, (((1,), (0,)), ((), ())), preferred_element_type=F32)


def dot_nt(a, b):
    return lax.dot_general(a, b, (((1,), (1,)), ((), ())), preferred_element_type=F32)


def dot_tn(a, b):
    return lax.dot_general(a, b, (((0,), (0,)), ((), ())), preferred_element_type=F32)


def rows_loop(count, body, block=BLOCK):
    @pl.loop(0, count // block)
    def _(i):
        body(pl.ds(pl.multiple_of(i * block, block), block))


def moments(values):
    centred = values - jnp.mean(values, axis=-1, keepdims=True)
    inverse = lax.rsqrt(jnp.mean(centred * centred, axis=-1, keepdims=True) + EPSILON)
    return centred, inverse


def norm_back(values, grad):
    centred, inverse = moments(values)
    hat = centred * inverse
    return inverse * (
        grad - jnp.mean(grad, axis=-1, keepdims=True) - hat * jnp.mean(grad * hat, axis=-1, keepdims=True)
    )


class Bag:
    pass


def prep(r):
    def body(rows):
        centred, inverse = moments(r.x[rows, :].astype(F32))
        r.first[rows, :] = (centred * inverse).astype(BF)

    rows_loop(r.S, body)


def prep_dz(r):
    def body(rows):
        keep = (lax.broadcasted_iota(jnp.int32, (BLOCK, 1), 0) + rows.start) < r.length
        for j in range(4):
            v = r.dzq[j, rows, :]
            r.dz[rows, r.W * j : r.W * (j + 1)] = jnp.where(keep, v, jnp.zeros_like(v))

    rows_loop(r.S, body)
    r.g_fc2[...] = dot_nt(r.dz[...], r.up_fc2[...]).astype(BF)


def by_head(r, v, ref):
    head = lax.broadcasted_iota(jnp.int32, (r.S, r.W), 1) // HD
    for h in range(r.W // HD):
        ref[h * r.S : (h + 1) * r.S, :] = jnp.where(head == h, v, jnp.zeros_like(v))


def own_lanes(r, t):
    head = lax.broadcasted_iota(jnp.int32, (r.S, r.W), 1) // HD
    out = t[: r.S]
    for h in range(1, r.W // HD):
        out = jnp.where(head == h, t[h * r.S : (h + 1) * r.S], out)
    return out


def block_of(q, width):
    return pl.ds(pl.multiple_of(q * width, width), width)


def attn_fwd(r, q):
    S, W = r.S, r.W
    p = dot(r.first[...], r.wq[q]) + dot(r.lift_qkv[...], r.sel_qu[:, block_of(q, 3 * W)])
    r.proj[q] = p.astype(BF)
    by_head(r, r.proj[q, :, 0:W], r.qm.at[q])
    r.st[...] = dot_nt(r.proj[q, :, W : 2 * W], r.qm[q])
    valid = lax.broadcasted_iota(jnp.int32, (S, 128), 0) < r.length

    for k in range(r.st.shape[1] // 128):
        c = slice(k * 128, (k + 1) * 128)
        v = jnp.where(valid, r.st[:, c] * (HD**-0.5), NEG_FILL)
        e = jnp.exp(v - jnp.max(v, axis=0, keepdims=True))
        soft = e * (1.0 / jnp.sum(e, axis=0, keepdims=True))
        r.soft[q, :, c] = soft
        r.ds[:, c] = soft.astype(BF)

    att = own_lanes(r, dot_tn(r.ds[...], r.proj[q, :, 2 * W : 3 * W])).astype(BF)
    r.att[:, block_of(q, W)] = att
    r.branch[...] += dot(att, r.wo[q])


def after_attn(r):
    r.lift_out[...] = dot_nt(r.att[...], r.sel_od[...]).astype(BF)
    r.branch[...] += dot(r.lift_out[...], r.up_out[...])

    def body(rows):
        mixed = r.x[rows, :].astype(F32) + r.branch[rows, :]
        r.mixed[rows, :] = mixed
        centred, inverse = moments(mixed)
        r.second[rows, :] = (centred * inverse).astype(BF)

    rows_loop(r.S, body)
    r.lift_fc1[...] = dot_nt(r.second[...], r.dn_fc1[...]).astype(BF)
    r.outacc[...] = jnp.zeros_like(r.outacc)
    r.gsec[...] = jnp.zeros_like(r.gsec)
    r.lift_fc2_acc[...] = jnp.zeros_like(r.lift_fc2_acc)
    r.glf1_acc[...] = jnp.zeros_like(r.glf1_acc)


def ffn_unit(r, q, u):
    FQ = r.FQ
    cols = block_of(u, STEP)
    wide = pl.ds(pl.multiple_of(q * FQ + u * STEP, STEP), STEP)
    up1 = r.sel_f1[:, wide]
    dn2 = r.sel_f2[:, wide]
    r.before[...] = dot(r.second[...], r.w1[q, :, cols]) + dot(r.lift_fc1[...], up1)
    r.gh[...] = dot_nt(r.dz[...], r.w2[q, cols, :]) + dot(r.g_fc2[...], dn2)

    def body(rows):
        b = r.before[rows, :]
        cdf = 0.5 * (1.0 + lax.erf(b * (0.5**0.5)))
        r.hidden[rows, :] = (b * cdf).astype(BF)
        slope = cdf + b * jnp.exp(-0.5 * b * b) * 0.3989422804014327
        r.gb[rows, :] = (slope * r.gh[rows, :]).astype(BF)

    for k in range(r.S // SMALL):
        body(pl.ds(k * SMALL, SMALL))
    h = r.hidden[...]
    g = r.gb[...]
    r.outacc[...] += dot(h, r.w2[q, cols, :])
    r.gsec[...] += dot_nt(g, r.w1[q, :, cols])
    r.lift_fc2_acc[...] += dot_nt(h, dn2)
    r.glf1_acc[...] += dot_nt(g, up1)
    r.g_f1[:, wide] = dot_tn(r.lift_fc1[...], g).astype(BF)
    r.g_f2[:, wide] = dot_tn(r.g_fc2[...], h).astype(BF)


def after_ffn_out(r):
    r.outacc[...] += dot(r.lift_fc2[...], r.up_fc2[...])

    def body(rows):
        keep = (lax.broadcasted_iota(jnp.int32, (BLOCK, 1), 0) + rows.start) < r.length
        v = jnp.where(keep, r.mixed[rows, :] + r.outacc[rows, :], 0.0).astype(BF)
        for j in range(4):
            r.outq[j, rows, :] = v[:, r.W * j : r.W * (j + 1)]

    rows_loop(r.S, body)


def after_ffn_back(r):
    g1 = r.glf1_acc[...].astype(BF)
    r.g_f2u[...] = dot_tn(r.lift_fc2[...], r.dz[...]).astype(BF)
    r.g_f1d[...] = dot_tn(g1, r.second[...]).astype(BF)
    r.gsec[...] += dot(g1, r.dn_fc1[...])

    def body(rows):
        g = r.dz[rows, :].astype(F32) + norm_back(r.mixed[rows, :], r.gsec[rows, :])
        r.gsec[rows, :] = g
        r.gbr[rows, :] = g.astype(BF)

    rows_loop(r.S, body)
    gbr = r.gbr[...]
    r.g_ou[...] = dot_tn(r.lift_out[...], gbr).astype(BF)
    r.g_out[...] = dot_nt(gbr, r.up_out[...]).astype(BF)


def back_attended(r):
    W = r.W
    r.ga[...] = dot(r.g_out[...], r.sel_od[...])

    @pl.loop(0, 4)
    def _(q):
        r.ga[:, block_of(q, W)] += dot_nt(r.gbr[...], r.wo[q])

    r.g_od[...] = dot_tn(r.g_out[...], r.att[...]).astype(BF)


def attn_back(r, q):
    W = r.W
    sc = HD**-0.5
    by_head(r, r.ga[:, block_of(q, W)].astype(BF), r.gm)
    k = r.proj[q, :, W : 2 * W]
    r.st[...] = dot_nt(r.proj[q, :, 2 * W : 3 * W], r.gm[...])
    gv = dot(r.soft[q].astype(BF), r.gm[...])

    for i in range(r.st.shape[1] // 128):
        c = slice(i * 128, (i + 1) * 128)
        soft, gs = r.soft[q, :, c], r.st[:, c]
        r.ds[:, c] = (soft * (gs - jnp.sum(soft * gs, axis=0, keepdims=True))).astype(BF)

    ds = r.ds[...]
    base = pl.multiple_of(3 * W * q, 128)
    r.gp[:, pl.ds(base, W)] = (own_lanes(r, dot_tn(ds, k)) * sc).astype(BF)
    r.gp[:, pl.ds(base + W, W)] = (dot(ds, r.qm[q]) * sc).astype(BF)
    r.gp[:, pl.ds(base + 2 * W, W)] = gv.astype(BF)
    wide = block_of(q, 3 * W)
    r.g_qu[:, wide] = dot_tn(r.lift_qkv[...], r.gp[:, wide]).astype(BF)


def finish_grads(r):
    gq = dot_nt(r.gp[...], r.sel_qu[...]).astype(BF)
    r.g_qd[...] = dot_tn(gq, r.first[...]).astype(BF)
    r.g_qkv[...] = gq


def back_first(r):
    W = r.W
    r.mixed[...] = dot(r.g_qkv[...], r.dn_qkv[...])

    @pl.loop(0, 4)
    def _(q):
        r.mixed[...] += dot_nt(r.gp[:, block_of(q, 3 * W)], r.wq[q])


def finish_rows(r, k):
    rows = slice(k * (r.S // 2), (k + 1) * (r.S // 2))
    r.gin[rows, :] = (r.gsec[rows, :] + norm_back(r.x[rows, :].astype(F32), r.mixed[rows, :])).astype(BF)


class Stream:
    def __init__(self, r):
        self.r = r
        d = self.d = lax.axis_index("dp")
        self.z = lax.axis_index("tensor")
        m = self.m = d % GROUP
        self.base = d - m
        self.dx = d + 2 - 4 * ((m // 2) % 2)
        self.dy = d + 4 - 8 * (m // 4)
        self.ds = d + 1 - 2 * (m % 2)
        self.dd = self.dx + self.dy - d
        self.inner = (self.z + 1) // 2 == 1
        self.n_a, self.n = 6, 18

    def quarter(self, i):
        return (self.z + jnp.where(self.z < 2, i, 4 - i)) % 4

    def unit(self, t, f):
        pl.when(t < self.n_a)(lambda: f("A", t % 2, t // 2 + 1))
        pl.when((t >= self.n_a) & (t < self.n - 2))(lambda: f("B", (t - self.n_a) % 4, (t - self.n_a) // 4 + 1))
        last = t - (self.n - 2)
        pl.when((last >= 0) & (last % 2 == 0))(lambda: f("X", last + 2, 3))
        pl.when((last >= 0) & (last % 2 == 1))(lambda: f("Y", last + 2, 3))

    def pair(self, kind):
        return (self.dy, self.dx) if kind == "X" else (self.dx, self.dy)

    def greet(self):
        bar = pltpu.get_barrier_semaphore()
        for k in range(1, GROUP):
            peer = self.base + (self.m + k) % GROUP
            pl.semaphore_signal(bar, inc=1, device_id=(peer, self.z), device_id_type=MESH)
        for k in range(1, 4):
            pl.semaphore_signal(bar, inc=1, device_id=(self.d, (self.z + k) % 4), device_id_type=MESH)

    def met(self):
        pl.semaphore_wait(pltpu.get_barrier_semaphore(), GROUP + 2)

    def parts(self, kind, p, q, d, half=None):
        r, m = self.r, d - self.base
        first, c = (0, pl.ds(0, r.D)) if half is None else (half, pl.ds(r.D // 2 * half, r.D // 2))
        if kind == "A":
            n = r.D // GROUP // 2
            k = r.W // GROUP // 2
            part = n if half is None else n // 2
            a = pl.ds(pl.multiple_of((2 * m + p) * n + first * part, part), part)
            b = pl.ds(pl.multiple_of((2 * m + p) * k, k), k)
            return ((r.wq.at[q, a, :]), (r.wo.at[q, b, c]))
        n = r.D // GROUP
        width = r.FQ // 4
        k = width // GROUP
        part = n if half is None else n // 2
        a = pl.ds(pl.multiple_of(m * n + first * part, part), part)
        b = pl.ds(pl.multiple_of(p * width + m * k, k), k)
        return (r.w1.at[q, a, block_of(p, width)], r.w2.at[q, b, c])

    def own(self, kind, p, d=None):
        r, z = self.r, self.z
        d = self.d if d is None else d
        m = d - self.base
        first, second = self.parts(kind, p, z, d)
        if kind == "A":
            n = r.D // GROUP // 2
            k = r.W // GROUP // 2
            a = pl.ds(pl.multiple_of((2 * m + p) * n, n), n)
            pairs = [(r.hq.at[i, a, :], r.wq.at[z, a, pl.ds(i * r.W, r.W)]) for i in range(3)]
            return pairs + [(r.ho.at[pl.ds(pl.multiple_of((2 * m + p) * k, k), k), :], second)]
        n = r.D // GROUP
        k = r.FQ // 4 // GROUP
        a = pl.ds(pl.multiple_of(m * n, n), n)
        b = pl.ds(pl.multiple_of(p * (r.FQ // 4) + m * k, k), k)
        return [(r.h1.at[a, block_of(p, r.FQ // 4)], first), (r.h2.at[b, :], second)]

    def send(self, srcs, dsts, sem, dev):
        for s, t in zip(srcs, dsts):
            pltpu.make_async_remote_copy(
                src_ref=s, dst_ref=t, send_sem=self.r.sends, recv_sem=sem, device_id=dev, device_id_type=MESH
            ).start()

    def wait(self, rows, sem):
        v = self.r.w2.at[0, pl.ds(0, rows), :]
        pltpu.make_async_copy(v, v, sem).wait()

    def index(self, kind, p, i):
        return (i - 1) * 2 + p if kind == "A" else 6 + (i - 1) * 4 + p

    def inner_sends(self, kind, p):
        z, d = self.z, self.d

        @pl.when(self.inner)
        def _():
            src, dst = zip(*self.own(kind, p))
            for to in (3 * (z - 1), 3 - z):
                self.send(src, dst, self.r.rz.at[self.index(kind, p, 1)], (d, to))

    def outer_sends(self, kind, p, i):
        z, d = self.z, self.d

        @pl.when(z % 3 == 0)
        def _():
            src, dst = zip(*self.own(kind, p))
            to = 2 - z // 3 if i == 2 else 1 + z // 3
            sem = self.r.rz.at[self.index(kind, p, i)]
            self.send(src, dst, sem, (d, to))
            if kind == "B" and i == 3:
                for n, wide in ((0, "X"), (1, "Y")):

                    @pl.when(p == n + 2)
                    def _():
                        src, dst = zip(*self.own("B", p, self.pair(wide)[0]))
                        self.send(src, dst, sem, (d, to))

    def z_stage(self, t):
        def forward(kind, p, i):
            self.wait(128 if kind in "XY" else 64, self.r.rz.at[t])
            if kind in "AB":

                @pl.when(self.inner & (i < 3))
                def _():
                    piece = self.parts(kind, p, self.quarter(i), self.d)
                    self.send(piece, piece, self.r.rz.at[self.index(kind, p, i + 1)], (self.d, 3 * (self.z - 1)))

        self.unit(t, forward)

    def xy_sends(self, t):
        def go(kind, p, i):
            z, r, q = self.z, self.r, self.quarter(i)
            if kind in "AB":
                carried, targets = (self.d,), ((r.rx, self.dx), (r.ry, self.dy))
            else:
                beside, across = self.pair(kind)
                carried, targets = (self.d, beside), (((r.rx if kind == "X" else r.ry), across),)
            for frm in carried:
                piece = self.parts(kind, p, q, frm)
                for sem, to in targets + ((r.rs, self.ds),):
                    self.send(piece, piece, sem.at[t], (to, z))

        self.unit(t, go)

    def xy_stage(self, t):
        def go(kind, p, i):
            z, q, r = self.z, self.quarter(i), self.r
            if kind in "XY":
                self.wait(128, (r.rx if kind == "X" else r.ry).at[t])
                for frm in (self.pair(kind)[1], self.dd):
                    w = self.parts(kind, p, q, frm)
                    self.send(w, w, r.rs.at[t], (self.ds, z))
                return
            for sem, frm, to, half in ((r.rx, self.dx, self.dy, 0), (r.ry, self.dy, self.dx, 1)):
                self.wait(64, sem.at[t])
                h = self.parts(kind, p, q, frm, half)
                self.send(h, h, r.rd.at[t], (to, z))
                w = self.parts(kind, p, q, frm)
                self.send(w, w, r.rs.at[t], (self.ds, z))
                if kind == "B":
                    n = 0 if to is self.dx else 1

                    @pl.when(self.inner & (i == 2) & (p == n + 2))
                    def _():
                        self.send(w, w, r.rz.at[self.index("B", p, 3)], (self.d, 3 * (z - 1)))

        self.unit(t, go)

    def d_stage(self, t):
        def go(kind, p, i):
            if kind in "AB":
                self.wait(64, self.r.rd.at[t])
                w = self.parts(kind, p, self.quarter(i), self.dd)
                self.send(w, w, self.r.rs.at[t], (self.ds, self.z))

        self.unit(t, go)

    def s_stage(self, t):
        self.wait(256, self.r.rs.at[t])

    def finish_sends(self):
        kinds = 6
        always = 7 * self.n - 2 + 2 * kinds + 2

        @pl.loop(0, jnp.where(self.inner, always + 2 * kinds, always))
        def _(i):
            self.wait(64, self.r.sends)


    def to_planes(self, view, target, send_sem, recv_sem):
        for k in range(1, 4):
            j = (self.z + k) % 4
            pltpu.make_async_remote_copy(
                src_ref=view(j), dst_ref=target, send_sem=send_sem, recv_sem=recv_sem, device_id=(self.d, j), device_id_type=MESH
            ).start()

    def to_group(self, view, target, send_sem, recv_sem):
        for k in range(1, GROUP):
            m = (self.m + k) % GROUP
            pltpu.make_async_remote_copy(
                src_ref=view(m), dst_ref=target, send_sem=send_sem, recv_sem=recv_sem, device_id=(self.base + m, self.z), device_id_type=MESH
            ).start()

    def share(self, src, dst, sems):
        place = dst(self.m)
        for to in (self.dx, self.dy, self.dd):
            pltpu.make_async_remote_copy(
                src_ref=src, dst_ref=place, send_sem=sems[0], recv_sem=sems[1], device_id=(to, self.z), device_id_type=MESH
            ).start()
        pltpu.make_async_remote_copy(
            src_ref=src, dst_ref=place, send_sem=sems[2], recv_sem=sems[3], device_id=(self.ds, self.z), device_id_type=MESH
        ).start()

    def pass_on(self, three, dst, sems):
        self.done(three, sems[1])
        for frm in (self.dx, self.dy, self.dd):
            place = dst(frm - self.base)
            pltpu.make_async_remote_copy(
                src_ref=place, dst_ref=place, send_sem=sems[2], recv_sem=sems[3], device_id=(self.ds, self.z), device_id_type=MESH
            ).start()

    def done(self, ref, *sems):
        for s in sems:
            pltpu.make_async_copy(ref, ref, s).wait()


class Sems:
    def __init__(self, ref, first):
        self.ref, self.first = ref, first

    def __getitem__(self, k):
        if isinstance(k, slice):
            return [self[i] for i in range(k.start, k.stop)]
        return self.ref.at[self.first + k]


def one_hot(r, p, transposed):
    R, T, n = r.R, r.T, r.n_img
    shape = (T, n * R) if transposed else (n * R, T)
    a = lax.broadcasted_iota(jnp.int32, shape, 1 if transposed else 0)
    b = lax.broadcasted_iota(jnp.int32, shape, 0 if transposed else 1)
    owner = jnp.zeros(shape, jnp.int32)
    for i in range(n):
        owner = jnp.where(a // R == i, r.ids[i, p], owner)
    hit = (b // R == owner) & (a % R == b % R)
    return jnp.where(hit, 1.0, 0.0).astype(BF)


def choose(r, p, flat):
    shape = (r.R, r.T)
    a = lax.broadcasted_iota(jnp.int32, shape, 0)
    b = lax.broadcasted_iota(jnp.int32, shape, 1)
    hit = (b // r.R == r.my_ids[p]) & (a == b % r.R)
    return dot(jnp.where(hit, 1.0, 0.0).astype(BF), flat).astype(BF)


def kernel(names, sizes, *refs):
    r = Bag()
    for n, f in zip(names, refs):
        setattr(r, n, f)
    for n, v in sizes.items():
        setattr(r, n, v)
    c = Stream(r)
    z, d = c.z, c.d
    S, W, FQ, R, n = r.S, r.W, r.FQ, r.R, r.n_img
    r.before, r.gh = r.st.at[:, pl.ds(0, STEP)], r.st.at[:, pl.ds(STEP, STEP)]
    r.hidden, r.gb = r.ds.at[:, pl.ds(0, STEP)], r.ds.at[:, pl.ds(STEP, STEP)]
    r.ga = r.branch
    r.outq, r.gin = r.dzq, r.first
    for k, name in enumerate(("aqd", "aou", "a1d", "a2u")):
        setattr(r, name, r.dense.at[:, pl.ds(k * r.D, r.D)])
    r.length = r.len[z]
    r.my_ids = [r.ids[z, p] for p in range(4)]
    c.greet()
    load = []

    def fetch(ends):
        slot = len(load)
        copy = lambda: pltpu.make_async_copy(*ends(), r.loc.at[slot])
        copy().start()
        load.append(copy)
        return copy

    l_x = fetch(lambda: (r.tokens.at[z], r.x))
    l_ad = {k: fetch(lambda k=k: (getattr(r, "h_" + k), getattr(r, k))) for k in ("aqd", "aqu", "aod", "a1u", "a2d", "aou", "a1d", "a2u")}
    l_q = [fetch(lambda i=i: (r.hq.at[i], r.wq.at[z, :, pl.ds(i * W, W)])) for i in range(3)]
    l_q.append(fetch(lambda: (r.ho, r.wo.at[z])))
    l_f = [fetch(lambda: (r.h1, r.w1.at[z])), fetch(lambda: (r.h2, r.w2.at[z]))]
    l_c = fetch(lambda: (r.cot.at[z], r.dzq.at[z]))
    c.met()

    def wait_all(copies):
        for copy in copies:
            copy().wait()

    def pick_attn():
        wait_all([l_ad["aqu"], l_ad["aod"]])
        hot = one_hot(r, 0, False)
        for i in range(3):
            r.out_qu[:, :, i * W : (i + 1) * W] = dot(hot, r.aqu[:, i].reshape(r.T, W)).astype(BF).reshape(n, R, W)
        r.out_od[...] = dot(one_hot(r, 1, False), r.aod[...]).astype(BF).reshape(n, R, W)
        c.to_planes(lambda j: r.out_qu.at[j], r.sel_qu.at[:, block_of(z, 3 * W)], r.misc.at[0], r.misc.at[1])
        c.to_planes(lambda j: r.out_od.at[j], r.sel_od.at[:, block_of(z, W)], r.misc.at[70], r.misc.at[71])
        r.sel_qu[:, block_of(z, 3 * W)] = r.out_qu[z]
        r.sel_od[:, block_of(z, W)] = r.out_od[z]

    def have_attn():
        c.done(r.sel_qu.at[:, pl.ds(0, 9 * W)], r.misc.at[0], r.misc.at[1])
        c.done(r.sel_od.at[:, pl.ds(0, 3 * W)], r.misc.at[70], r.misc.at[71])

    def pick_ffn():
        wait_all([l_ad["a1u"], l_ad["a2d"]])
        r.out_f1[...] = dot(one_hot(r, 2, False), r.a1u[...]).astype(BF).reshape(n, R, FQ)
        r.out_f2[...] = dot(one_hot(r, 3, False), r.a2d[...]).astype(BF).reshape(n, R, FQ)
        r.sel_f1[:, block_of(z, FQ)] = r.out_f1[z]
        r.sel_f2[:, block_of(z, FQ)] = r.out_f2[z]

    def send_f1():
        c.to_planes(lambda j: r.out_f1.at[j], r.sel_f1.at[:, block_of(z, FQ)], r.misc.at[72], r.misc.at[73])

    def send_f2():
        c.to_planes(lambda j: r.out_f2.at[j], r.sel_f2.at[:, block_of(z, FQ)], r.misc.at[74], r.misc.at[75])

    def have_ffn():
        c.done(r.sel_f1.at[:, pl.ds(0, 3 * FQ)], r.misc.at[72], r.misc.at[73])
        c.done(r.sel_f2.at[:, pl.ds(0, 3 * FQ)], r.misc.at[74], r.misc.at[75])

    def pick_first():
        l_ad["aqd"]().wait()
        r.dn_qkv[...] = choose(r, 0, r.aqd[...])
        r.lift_qkv[...] = dot_nt(r.first[...], r.dn_qkv[...]).astype(BF)

    def pick_rest():
        wait_all([l_ad["aou"], l_ad["a1d"], l_ad["a2u"]])
        r.up_out[...] = choose(r, 1, r.aou[...])
        r.dn_fc1[...] = choose(r, 2, r.a1d[...])
        r.up_fc2[...] = choose(r, 3, r.a2u[...])

    CUTS = 5

    def send_cot(k):
        rows = pl.ds(k * (S // CUTS), S // CUTS)
        c.to_planes(lambda j: r.cot.at[j, rows, :], r.dzq.at[z, rows, :], r.misc.at[2], r.misc.at[3])

    def have_cot():
        c.done(r.dzq.at[pl.ds(0, 3)], r.misc.at[2], r.misc.at[3])
        l_c().wait()
        prep_dz(r)

    def ffn(n):
        i, u = n // 2, n % 2
        q = c.quarter(i)
        ffn_unit(r, q, u)

        @pl.when(i > 0)
        def _():
            wide = pl.ds(pl.multiple_of(q * FQ + u * STEP, STEP), STEP)
            for ref, base in ((r.g_f1, 0), (r.g_f2, FQ)):
                pltpu.make_async_remote_copy(
                    src_ref=ref.at[:, wide], dst_ref=r.sp.at[z, :, pl.ds(pl.multiple_of(base + u * STEP, STEP), STEP)],
                    send_sem=r.misc.at[8], recv_sem=r.misc.at[9], device_id=(d, q), device_id_type=MESH,
                ).start()

    N = c.n
    LZ, LX, LD = 1, 1, 1
    lag = LZ + LX + LD
    c.inner_sends("A", 0)
    c.inner_sends("A", 1)
    l_x().wait()
    prep(r)
    r.branch[...] = jnp.zeros_like(r.branch)
    c.z_stage(0)

    @pl.loop(0, N + lag)
    def _(t):
        pl.when(t < N)(lambda: c.xy_sends(t))
        pl.when((t >= LZ) & (t < LZ + N))(lambda: c.xy_stage(t - LZ))
        pl.when((t >= LZ + LX) & (t < LZ + LX + N))(lambda: c.d_stage(t - LZ - LX))
        pl.when(t >= lag)(lambda: c.s_stage(t - lag))
        pl.when(t + 1 < N)(lambda: c.z_stage(t + 1))
        pl.when((t >= 1) & (t < 5))(lambda: c.inner_sends("B", t - 1))

        @pl.when((t == 0) | (t == 3))
        def _():
            for p in range(2):
                pl.when(t == 0)(lambda: c.outer_sends("A", p, 2))
                pl.when(t == 3)(lambda: c.outer_sends("A", p, 3))

        pl.when((t >= 5) & (t < 9))(lambda: c.outer_sends("B", t - 5, 2))
        pl.when((t >= 10) & (t < 14))(lambda: c.outer_sends("B", t - 10, 3))
        pl.when((t >= 1) & (t < 11) & ((t - 1) % 2 == 0))(lambda: send_cot((t - 1) // 2))
        pl.when(t == 0)(pick_first)
        pl.when(t == 1)(pick_attn)
        pl.when(t == 2)(lambda: wait_all(l_q))
        pl.when(t == 3)(pick_rest)
        pl.when(t == 4)(pick_ffn)
        pl.when(t == 9)(send_f1)
        pl.when(t == 11)(send_f2)
        pl.when(t == 1 + lag)(have_attn)
        pl.when((t == 2) | (t == 1 + lag) | (t == 3 + lag) | (t == 5 + lag))(lambda: attn_fwd(r, c.quarter((t - 1) // 2)))

        @pl.when(t == 5 + lag)
        def _():
            after_attn(r)
            wait_all(l_f)

        pl.when(t == 12)(have_cot)
        pl.when(t == 14)(have_ffn)
        pl.when((t >= 12) & (t != 19))(lambda: ffn(jnp.minimum(t - 12, 7)))

    mine = block_of(z, W)

    def group(lo, own_end, hi, s, fs, fr, out=None):
        cols, own, reps, zc = pl.ds(lo, hi - lo), pl.ds(lo, own_end - lo), pl.ds(own_end, hi - own_end), pl.ds(fr, hi - own_end)
        sem = Sems(r.misc, s)
        fin = pl.ds(fs, own_end - lo)
        fin_s = r.fin_s if out is None else out

        def send_whole(ref, col):
            c.to_planes(lambda j: ref, r.sp.at[z, :, cols], sem[0], sem[1])
            r.sp[z, :, cols] = ref[...]

        def send(sources):
            for ref, width, col in sources:
                c.to_planes(lambda j: ref.at[:, block_of(j, width)], r.sp.at[z, :, pl.ds(col, width)], sem[0], sem[1])
                r.sp[z, :, col : col + width] = ref[:, block_of(z, width)]

        def expand():
            c.done(r.sp.at[pl.ds(0, 3), :, cols], sem[0], sem[1])
            for a, b, p in r.blocks:
                if lo <= a < hi:
                    r.dense[:, a:b] = dot(one_hot(r, p, True), r.sp[:, :, a:b].reshape(n * R, b - a)).astype(BF)
            c.to_group(lambda m: r.dense.at[block_of(m, R), cols], r.rsb.at[c.m, :, cols], sem[2], sem[3])
            r.rsb[c.m, :, cols] = r.dense[block_of(c.m, R), cols]

        def reduce():
            c.done(r.rsb.at[pl.ds(0, GROUP - 1), :, cols], sem[2], sem[3])
            sums = r.rsb[0, :, cols].astype(F32)
            for k in range(1, GROUP):
                sums = sums + r.rsb[k, :, cols].astype(F32)
            r.red[:, cols] = sums.astype(BF)
            if hi > own_end:
                c.to_planes(lambda j: r.red.at[:, reps], r.zb.at[z, :, zc], sem[4], sem[5])
                r.zb[z, :, zc] = r.red[:, reps]
            if own_end > lo:
                c.share(r.red.at[:, own], lambda m: fin_s.at[m, :, fin], sem[6:10])
                fetch(lambda: (r.red.at[:, own], fin_s.at[c.m, :, fin]))

        def share():
            c.done(r.zb.at[pl.ds(0, 3), :, zc], sem[4], sem[5])
            c.share(r.zb.at[:, :, zc], lambda m: r.fin_r.at[m, :, :, zc], sem[10:14])
            fetch(lambda: (r.zb.at[:, :, zc], r.fin_r.at[c.m, :, :, zc]))

        def relay():
            if own_end > lo:
                c.pass_on(fin_s.at[pl.ds(0, 3), :, fin], lambda m: fin_s.at[m, :, fin], sem[6:10])

        def relay_rep():
            c.pass_on(r.fin_r.at[pl.ds(0, 3), :, :, zc], lambda m: r.fin_r.at[m, :, :, zc], sem[10:14])

        def close():
            if own_end > lo:
                c.done(fin_s.at[pl.ds(0, 3), :, fin], sem[6])
                c.done(fin_s.at[pl.ds(0, 4), :, fin], sem[8], sem[9])
            if hi > own_end:
                c.done(r.fin_r.at[pl.ds(0, 3), :, :, zc], sem[10])
                c.done(r.fin_r.at[pl.ds(0, 4), :, :, zc], sem[12], sem[13])

        return send if out is None else send_whole, expand, reduce, share, relay, relay_rep, close

    m0, l0, end = r.starts
    _, e_expand, e_reduce, _, e_relay, _, e_close = group(0, m0, m0, 8, 0, 0)
    m_send, m_expand, m_reduce, m_share, _, m_relay, m_close = group(m0, m0, l0, 22, 0, 0)
    p0 = l0 + 4 * W
    l_send, l_expand, l_reduce, _, l_relay, _, l_close = group(l0, p0, p0, 36, 2 * FQ, 0)
    p_send, p_expand, p_reduce, _, p_relay, _, p_close = group(p0, end, end, 56, 0, 0, r.fin_p)

    def back(q):
        attn_back(r, q)
        for ref, width, col in ((r.g_qu, 3 * W, l0), (r.g_od, W, l0 + 3 * W)):
            src, dst = ref.at[:, block_of(q, width)], r.sp.at[z, :, pl.ds(col, width)]

            @pl.when(z != q)
            def _():
                pltpu.make_async_remote_copy(
                    src_ref=src, dst_ref=dst, send_sem=r.misc.at[36], recv_sem=r.misc.at[37], device_id=(d, q), device_id_type=MESH
                ).start()

    def send_out(k):
        rows = pl.ds(k * (S // 2), S // 2)
        c.to_planes(lambda j: r.outq.at[j, rows, :], r.outr.at[z, rows, :], r.misc.at[4], r.misc.at[5])
        fetch(lambda: (r.outq.at[z, rows, :], r.outr.at[z, rows, :]))

    r.lift_fc2[...] = r.lift_fc2_acc[...].astype(BF)
    after_ffn_out(r)
    send_out(0)
    after_ffn_back(r)
    m_send([(r.g_f1d, W, m0), (r.g_f2u, W, m0 + W), (r.g_ou, W, m0 + 2 * W)])
    send_out(1)
    for ref, base in ((r.g_f1, 0), (r.g_f2, FQ)):
        r.sp[z, :, base : base + FQ] = ref[:, block_of(z, FQ)]
    back_attended(r)
    e_expand()

    @pl.loop(0, 4)
    def _(q):
        back(q)

    e_reduce()
    m_expand()
    finish_grads(r)
    p_send(r.g_qd, p0)
    for ref, width, col in ((r.g_qu, 3 * W, l0), (r.g_od, W, l0 + 3 * W)):
        r.sp[z, :, col : col + width] = ref[:, block_of(z, width)]
    m_reduce()
    back_first(r)
    half = S // 2

    def send_gin(k):
        rows = pl.ds(k * half, half)
        c.to_planes(lambda j: r.gin.at[rows, block_of(j, W)], r.ginr.at[z, rows, :], r.misc.at[6], r.misc.at[7])
        fetch(lambda: (r.gin.at[rows, mine], r.ginr.at[z, rows, :]))

    finish_rows(r, 0)
    send_gin(0)
    p_expand()
    l_expand()
    finish_rows(r, 1)
    send_gin(1)
    e_relay()
    m_share()
    p_reduce()
    l_reduce()
    m_relay()
    l_relay()
    p_relay()
    e_close()
    m_close()
    c.done(r.outr.at[pl.ds(0, 3)], r.misc.at[4], r.misc.at[5])
    c.finish_sends()
    l_close()
    p_close()
    c.done(r.ginr.at[pl.ds(0, 3)], r.misc.at[6], r.misc.at[7])
    wait_all(load[1 + len(l_ad) + 7 :])


def spread(names, *refs):
    r = Bag()
    for n, f in zip(names, refs):
        setattr(r, n, f)
    W = r.b_out.shape[2]
    FQ = r.v_f1u.shape[2]
    loads = []
    pieces = [(ref.at[i], buf.at[i]) for ref, buf in ((r.outr, r.b_out), (r.ginr, r.b_gin)) for i in range(r.b_out.shape[0])]
    for k, (src, dst) in enumerate(pieces + [(r.fin_s, r.b_s), (r.fin_r, r.b_r), (r.fin_p, r.b_p)]):
        loads.append(pltpu.make_async_copy(src, dst, r.sem_in.at[k]))
        loads[-1].start()
    images = r.b_out.shape[0]
    stores = []

    def store(key):
        stores.append(pltpu.make_async_copy(getattr(r, "v_" + key), getattr(r, "o_" + key), r.sem_out.at[len(stores)]))
        stores[-1].start()

    def widen(ref, src):
        @pl.loop(0, ref.shape[0])
        def _(i):
            ref[i] = src(i).astype(F32)

    for j, key in enumerate(("out", "gin")):
        for i in range(images):
            loads[j * images + i].wait()
            wide = getattr(r, "v_" + key)
            wide[i] = getattr(r, "b_" + key)[i].astype(F32)
            stores.append(pltpu.make_async_copy(wide.at[i], getattr(r, "o_" + key).at[i], r.sem_out.at[len(stores)]))
            stores[-1].start()
    loads = loads[2 * images - 2 :]
    loads[2].wait()
    widen(r.v_f1u, lambda i: r.b_s[i, :, :FQ])
    store("f1u")
    widen(r.v_f2d, lambda i: r.b_s[i, :, FQ : 2 * FQ])
    store("f2d")

    @pl.loop(0, r.v_qu.shape[0])
    def _(i):
        for k in range(3):
            r.v_qu[i, k] = r.b_s[i, :, 2 * FQ + k * W : 2 * FQ + (k + 1) * W].astype(F32)

    store("qu")
    widen(r.v_od, lambda i: r.b_s[i, :, 2 * FQ + 3 * W :])
    store("od")
    loads[3].wait()
    for k, key in enumerate(("f1d", "f2u", "ou")):
        ref = getattr(r, "v_" + key)

        @pl.loop(0, ref.shape[0])
        def _(i):
            for j in range(4):
                ref[i, :, W * j : W * (j + 1)] = r.b_r[i, j, :, W * k : W * (k + 1)].astype(F32)

        store(key)
    loads[4].wait()
    widen(r.v_qd, lambda i: r.b_p[i])
    store("qd")
    for cp in stores:
        cp.wait()


def make_shards(groups):
    def shards(
        tokens, lengths, adapter_ids, qkv_weight, qkv_down, qkv_up, out_weight, out_down, out_up,
        fc1_weight, fc1_down, fc1_up, fc2_weight, fc2_down, fc2_up, cotangent,
    ):
        n, S, D = tokens.shape
        A, _, R = qkv_down.shape
        T = A * R
        W = out_weight.shape[0]
        FQ = fc1_weight.shape[1]
        m0 = 2 * FQ
        l0 = m0 + 3 * W
        total = l0 + 4 * W + D
        blocks = (
            (0, FQ, 2), (FQ, m0, 3), (m0, m0 + W, 2), (m0 + W, m0 + 2 * W, 3), (m0 + 2 * W, l0, 1),
            (l0, l0 + 3 * W, 0), (l0 + 3 * W, l0 + 4 * W, 1), (l0 + 4 * W, total, 0),
        )
        sizes = dict(n_img=n, S=S, D=D, R=R, T=T, W=W, FQ=FQ, starts=(m0, l0, total), blocks=blocks)

        def turned(a):
            return jnp.transpose(a, (0, 2, 1)).reshape(T, a.shape[1])

        args = dict(
            len=lengths, ids=adapter_ids, tokens=tokens, cot=cotangent,
            hq=jnp.transpose(qkv_weight, (1, 0, 2)), ho=out_weight, h1=fc1_weight, h2=fc2_weight,
            h_aqd=turned(qkv_down), h_aqu=jnp.transpose(qkv_up, (0, 2, 1, 3)), h_aod=turned(out_down),
            h_a1u=fc1_up.reshape(T, FQ), h_a2d=turned(fc2_down), h_aou=out_up.reshape(T, D),
            h_a1d=turned(fc1_down), h_a2u=fc2_up.reshape(T, D),
        )
        outs = dict(outr=(n, S, W), ginr=(n, S, W), fin_s=(GROUP, R, 2 * FQ + 4 * W), fin_r=(GROUP, 4, R, 3 * W), fin_p=(GROUP, R, D))
        heads = W // HD
        vm = dict(
            wq=((4, D, 3 * W), BF), wo=((4, W, D), BF), w1=((4, D, FQ), BF), w2=((4, FQ, D), BF),
            aqu=((A, 3, R, W), BF), aod=((T, W), BF), a1u=((T, FQ), BF), a2d=((T, FQ), BF),
            out_qu=((n, R, 3 * W), BF), out_od=((n, R, W), BF), out_f1=((n, R, FQ), BF), out_f2=((n, R, FQ), BF),
            sel_qu=((R, 12 * W), BF), sel_od=((R, 4 * W), BF), sel_f1=((R, 4 * FQ), BF), sel_f2=((R, 4 * FQ), BF),
            dn_qkv=((R, D), BF), up_out=((R, D), BF), dn_fc1=((R, D), BF), up_fc2=((R, D), BF),
            x=((S, D), BF), dzq=((4, S, W), BF), dz=((S, D), BF),
            first=((S, D), BF), lift_qkv=((S, R), BF), g_fc2=((S, R), BF), proj=((4, S, 3 * W), BF), qm=((4, heads * S, W), BF),
            st=((S, heads * S), F32), ds=((S, heads * S), BF), soft=((4, S, heads * S), F32), att=((S, 4 * W), BF),
            branch=((S, D), F32), lift_out=((S, R), BF), mixed=((S, D), F32), second=((S, D), BF), lift_fc1=((S, R), BF),
            outacc=((S, D), F32), gsec=((S, D), F32), lift_fc2_acc=((S, R), F32), glf1_acc=((S, R), F32),
            lift_fc2=((S, R), BF), gbr=((S, D), BF), g_out=((S, R), BF), gm=((heads * S, W), BF), gp=((S, 12 * W), BF),
            g_qkv=((S, R), BF),
            g_f1=((R, 4 * FQ), BF), g_f2=((R, 4 * FQ), BF), g_f1d=((R, D), BF), g_f2u=((R, D), BF), g_ou=((R, D), BF),
            g_qu=((R, 12 * W), BF), g_od=((R, 4 * W), BF), g_qd=((R, D), BF),
            sp=((n, R, total), BF), dense=((T, total), BF), rsb=((GROUP, R, total), BF), red=((R, total), BF),
            zb=((4, R, 3 * W), BF),
        )
        units = 18
        sems = dict(rz=units, rx=units, ry=units, rd=units, rs=units, sends=None, loc=28, misc=76)
        names = list(args) + list(outs) + list(vm) + list(sems)
        anywhere = pl.BlockSpec(memory_space=pl.ANY)
        got = pl.pallas_call(
            lambda *refs: kernel(names, sizes, *refs),
            out_shape=tuple(jax.ShapeDtypeStruct(s, BF) for s in outs.values()),
            in_specs=[pl.BlockSpec(memory_space=pltpu.SMEM)] * 2 + [anywhere] * (len(args) - 2),
            out_specs=tuple([anywhere] * len(outs)),
            scratch_shapes=[pltpu.VMEM(s, t) for s, t in vm.values()]
            + [pltpu.SemaphoreType.DMA if k is None else pltpu.SemaphoreType.DMA((k,)) for k in sems.values()],
            compiler_params=pltpu.CompilerParams(collective_id=0, has_side_effects=True, vmem_limit_bytes=60 * 2**20),
        )(*args.values())
        outr, ginr, fin_s, fin_r, fin_p = got
        if groups > 1:
            across = [[m + GROUP * g for g in range(groups)] for m in range(GROUP)]
            fin_s, fin_r, fin_p = lax.psum(tuple(v.astype(F32) for v in (fin_s, fin_r, fin_p)), "dp", axis_index_groups=across)
        full = (A, R, D)
        wide = dict(
            out=(n, S, W), gin=(n, S, W), qd=full, qu=(A, 3, R, W), od=(A, R, W), ou=full, f1d=full, f1u=(A, R, FQ), f2d=(A, R, FQ), f2u=full
        )
        held = dict(b_out=outr, b_gin=ginr, b_s=fin_s, b_r=fin_r, b_p=fin_p)
        names = ["outr", "ginr", "fin_s", "fin_r", "fin_p"] + ["o_" + k for k in wide] + list(held) + ["v_" + k for k in wide] + ["sem_in", "sem_out"]
        output, input_grad, qd, qu, od, ou, f1d, f1u, f2d, f2u = pl.pallas_call(
            lambda *refs: spread(names, *refs),
            out_shape=tuple(jax.ShapeDtypeStruct(v, F32) for v in wide.values()),
            in_specs=[anywhere] * 5,
            out_specs=tuple([anywhere] * len(wide)),
            scratch_shapes=[pltpu.VMEM(v.shape, v.dtype) for v in held.values()]
            + [pltpu.VMEM(v, F32) for v in wide.values()]
            + [pltpu.SemaphoreType.DMA((2 * n + 3,)), pltpu.SemaphoreType.DMA((2 * n + 8,))],
            compiler_params=pltpu.CompilerParams(vmem_limit_bytes=60 * 2**20),
        )(outr, ginr, fin_s, fin_r, fin_p)
        back = lambda a: jnp.transpose(a, (0, 2, 1))
        return (output, input_grad, back(qd), jnp.transpose(qu, (0, 2, 1, 3)), back(od), ou, back(f1d), f1u, back(f2d), f2u)

    return shards


def solution(mesh):
    in_specs = (
        P("dp", None, None), P("dp"), P("dp", None), P(None, None, "tensor"), P(), P(None, None, None, "tensor"),
        P("tensor", None), P(None, "tensor", None), P(), P(None, "tensor"), P(), P(None, None, "tensor"),
        P("tensor", None), P(None, "tensor", None), P(), P("dp", None, "tensor"),
    )
    out_specs = (
        P("dp", None, "tensor"), P("dp", None, "tensor"), P(), P(None, None, None, "tensor"), P(None, "tensor", None),
        P(), P(), P(None, None, "tensor"), P(None, "tensor", None), P(),
    )
    shards = make_shards(mesh.shape["dp"] // GROUP)
    return jax.shard_map(shards, mesh=mesh, in_specs=in_specs, out_specs=out_specs, check_vma=False)
```
